32 devices in a mesh: rows: 4 (over x, core), seq: 8 (over z, y).
Axes of the slice: x: 2, y: 2, z: 4, core: 2. Of those that a mesh axis runs over, the one named last changes fastest.
Arguments:
- hidden_in: bfloat16 [16, 512, 1024], P('rows', 'seq'), may hold values from -6 to 6
- segment_ids: int32 [16, 512], P('rows', 'seq'), may hold values from 0 to 6, as said below
- positions: int32 [16, 512], P('rows', 'seq'), may hold values from 0 to 385, as said below
- expert_ids: int32 [16, 512, 8], P('rows', 'seq'), may hold values from 0 to 31, all different within a row; in each aligned block of 64 rows (0 to 63, 64 to 127, ..., all dimensions but the last counted through in order) at most 32 rows name the same one
- first_gain: float32 [1024], replicated, may hold values from 0.25 to 1.75
- query_weight: bfloat16 [1024, 1024], replicated, may hold values from -0.1875 to 0.1875
- key_weight: bfloat16 [1024, 512], replicated, may hold values from -0.1875 to 0.1875
- value_weight: bfloat16 [1024, 512], replicated, may hold values from -0.1875 to 0.1875
- output_weight: bfloat16 [1024, 1024], replicated, may hold values from -0.75 to 0.75
- second_gain: float32 [1024], replicated, may hold values from 0.25 to 1.75
- router_weight: bfloat16 [1024, 32], replicated, may hold values from -0.09375 to 0.09375
- gate_weight: bfloat16 [32, 1024, 512], P('seq'), may hold values from -0.1875 to 0.1875
- up_weight: bfloat16 [32, 1024, 512], P('seq'), may hold values from -0.1875 to 0.1875
- down_weight: bfloat16 [32, 512, 1024], P('seq'), may hold values from -1 to 1
- out_grad: bfloat16 [16, 512, 1024], P('rows', 'seq'), may hold values from -6 to 6
Outputs:
- hidden_out: bfloat16 [16, 512, 1024], P('rows', 'seq')
- grad_hidden: float32 [16, 512, 1024], P('rows', 'seq')
- grad_first: float32 [1024], replicated
- grad_query: float32 [1024, 1024], replicated
- grad_key: float32 [1024, 512], replicated
- grad_value: float32 [1024, 512], replicated
- grad_output: float32 [1024, 1024], replicated
- grad_second: float32 [1024], replicated
- grad_router: float32 [1024, 32], replicated
- grad_gate: float32 [32, 1024, 512], P('seq')
- grad_up: float32 [32, 1024, 512], P('seq')
- grad_down: float32 [32, 512, 1024], P('seq')
The draws below stay inside these ranges and needn't reach their ends.
Inputs may be any that keep to these rules, and one draw needn't show every extreme that they name: `segment_ids`: along each row the ids start at 0, never fall and rise by one at each of 6 boundaries; a document is a run of equal ids. In each group of 4 rows on one index of rows, one row holds a document that begins within the row's first 64 tokens and ends within its last 64. `positions`: each token's offset from the first token of its document. `expert_ids`: each token names 8 different experts. Among the 64 tokens of one row on one device no expert is named by more than 32 tokens, and in some such block one expert is named by exactly 32.
All inputs are finite; a program needn't handle non-finite values.
Results may differ from the reference program's by a relative error of at most 0.023.
Values may be sent and summed in bfloat16 or wider, within the bound.
No kernel may reach another device: no remote copies, remote signals or barrier semaphores. Data moves between devices by JAX's collectives and lax.ppermute only.
A program may use at most 256 MiB of HBM per device.

```python
import math
import jax
import jax.numpy as jnp
import numpy as np
from jax import lax

D = 1024
HEADS = 16
KV_HEADS = 8
HEAD_DIM = 64
FF = 512
EXPERTS = 32
TOPK = 8
BLK = 64
ROWS_DEV = 4
CUTS = 6
MOST = 32
SEQ_LEN = 512
ROWS = 16
N_SEQ = 8


def picked_rows(key, count, total):
    row_keys = jax.random.split(key, ROWS)
    shuffled = jax.vmap(lambda one_key: jax.random.permutation(one_key, total))(row_keys)
    return shuffled[:, :count].astype(jnp.int32)


def document_marks(key):
    split_keys = jax.random.split(key, 4)
    early_count = (CUTS + 1) // 2
    late_count = CUTS - early_count
    spread_pick = picked_rows(split_keys[0], CUTS - 2, SEQ_LEN - 3) + 1
    spread_pick = spread_pick + (spread_pick >= BLK).astype(jnp.int32)
    spread_pick = spread_pick + (spread_pick >= SEQ_LEN - BLK).astype(jnp.int32)
    spread_fixed = jnp.broadcast_to(jnp.array([BLK, SEQ_LEN - BLK], jnp.int32)[None, :], (ROWS, 2))
    spread_cuts = jnp.concatenate([spread_fixed, spread_pick], axis=1)
    early_pick = picked_rows(split_keys[1], early_count - 1, BLK - 2) + 1
    late_pick = picked_rows(split_keys[2], late_count - 1, BLK - 2) + (SEQ_LEN - BLK + 2)
    bound_fixed = jnp.broadcast_to(jnp.array([BLK - 1, SEQ_LEN - BLK + 1], jnp.int32)[None, :], (ROWS, 2))
    bounded = jnp.concatenate([bound_fixed, early_pick, late_pick], axis=1)
    chosen = jax.random.randint(split_keys[3], (ROWS // ROWS_DEV, 1), 0, ROWS_DEV)
    longest = (jnp.arange(ROWS_DEV, dtype=jnp.int32)[None, :] == chosen).reshape(ROWS)
    cut_points = jnp.where(longest[:, None], bounded, spread_cuts)
    places = jnp.arange(SEQ_LEN, dtype=jnp.int32)
    marks = jnp.any(places[None, :, None] == cut_points[:, None, :], axis=-1)
    return (marks, places)


def draw_segment_ids(key, part):
    marks, places = document_marks(key)
    return jnp.cumsum(marks.astype(jnp.int32), axis=1, dtype=jnp.int32)


def draw_positions(key, part):
    marks, places = document_marks(key)
    starts = lax.cummax(jnp.where(marks, places[None, :], 0), axis=1)
    return places[None, :] - starts


def levels(own_key, extent, cuts, smallest, high):
    level = 1.0
    for dim, parts in cuts:
        draws = jax.random.uniform(jax.random.fold_in(jax.random.fold_in(own_key, 6), dim), (parts,), jnp.float32, smallest / len(cuts), high / len(cuts))
        level = level * jnp.repeat(jnp.exp(draws), extent[dim] // parts).reshape((-1,) + (1,) * (len(extent) - 1 - dim))
    return level


def shared_out(stream_key, own, number, rows, count, top, reach, lean):
    order = jax.random.permutation(stream_key, count)
    packed, ordinary = portions_of(count, rows * top, reach, lean, True), portions_of(count, rows * top, reach, lean, False)
    places = jnp.arange(count)

    def named(sizes, offset_by):
        used = int((sizes > 0).sum())
        fixed = max(1, used // 4)
        passed = fixed + (places - fixed + offset_by * (used - fixed)) % max(1, count - fixed)
        return jnp.zeros((count,), jnp.int32).at[order[jnp.where(places < fixed, places, passed)]].set(jnp.asarray(sizes, jnp.int32))

    sizes = jnp.where(number % 4 == 0, named(packed, number // 4), named(ordinary, number - number // 4 - 1))
    mixed = jax.random.permutation(jax.random.fold_in(own, 3), count)
    donor, sink = mixed[0:count // 2 * 2:2], mixed[1:count // 2 * 2:2]
    margin = jnp.minimum(sizes[donor] - 1, reach - sizes[sink]) // 2
    margin = jnp.where((donor == order[0]) | (sink == order[0]) | (sizes[sink] == 0), 0, jnp.maximum(margin, 0))
    passed = jax.random.randint(jax.random.fold_in(own, 4), (count // 2,), 0, 1 << 20) % (margin + 1)
    sizes = sizes.at[donor].add(-passed).at[sink].add(passed)
    items = jnp.searchsorted(jnp.cumsum(sizes), jnp.arange(rows * top), side="right").astype(jnp.int32)
    listing = items.reshape(top, rows).T
    listing = listing[jax.random.permutation(jax.random.fold_in(own, 1), rows)]
    offset_by = jax.random.randint(jax.random.fold_in(own, 2), (rows, 1), 0, top)
    return jnp.take_along_axis(listing, (jnp.arange(top)[None, :] + offset_by) % top, axis=1)


def portions_of(number_of, total, bound, lean, full):
    weights = [(1 << 20) // math.isqrt(rank ** lean) + 1 for rank in range(1, number_of + 1)]
    largest = bound if full else min(bound, max(-(-total // number_of), total * weights[0] // sum(weights)))
    least = 1 if total - largest >= number_of - 1 else 0
    given, spare = [largest] + [least] * (number_of - 1), total - largest - least * (number_of - 1)
    while spare > 0:
        free = [i for i in range(1, number_of) if given[i] < largest] or [i for i in range(1, number_of) if given[i] < bound]
        whole, left = sum([weights[i] for i in free]), spare
        for i in free:
            more = min(bound - given[i], max(1, left * weights[i] // whole), spare)
            given[i] = given[i] + more
            spare = spare - more
    return np.array(given)


def bell_draw(rng, shape, spread, limit, cuts=(), kind=jnp.bfloat16):
    values = jax.random.normal(rng, shape, jnp.float32) * spread
    if len(cuts) > 0:
        values = levels(rng, shape, cuts, -0.22, 0.18) * values
    return jnp.clip(values, min=-limit, max=limit).astype(kind)


def setup_inputs(seed: int = 0) -> dict:
    streams_of = jax.random.split(jax.random.key(seed), 16)
    hidden_in = bell_draw(streams_of[0], (ROWS, SEQ_LEN, D), 1.0, 6.0, ((0, 4), (1, 8)))
    segment_ids = draw_segment_ids(jax.random.fold_in(streams_of[15], 71), 0)
    positions = draw_positions(jax.random.fold_in(streams_of[15], 71), 0)
    expert_ids_keys = jax.random.split(jax.random.fold_in(streams_of[3], 1), ROWS * SEQ_LEN // BLK)
    expert_ids_turns = jax.random.permutation(jax.random.fold_in(streams_of[3], 3), ROWS * SEQ_LEN // BLK)
    expert_ids = jax.vmap(lambda own, number: shared_out(jax.random.fold_in(streams_of[3], 2), own, number, BLK, EXPERTS, TOPK, MOST, 1))(expert_ids_keys, expert_ids_turns).reshape((ROWS, SEQ_LEN, TOPK))
    first_gain = jnp.clip(1.0 + 0.15 * jax.random.normal(streams_of[4], (D,), jnp.float32), 0.25, 1.75)
    query_weight = bell_draw(streams_of[5], (D, HEADS * HEAD_DIM), D ** -0.5, 0.1875)
    key_weight = bell_draw(streams_of[6], (D, KV_HEADS * HEAD_DIM), D ** -0.5, 0.1875)
    value_weight = bell_draw(streams_of[7], (D, KV_HEADS * HEAD_DIM), D ** -0.5, 0.1875)
    output_weight = bell_draw(streams_of[8], (HEADS * HEAD_DIM, D), HEAD_DIM ** -0.5, 0.75)
    second_gain = jnp.clip(1.0 + 0.15 * jax.random.normal(streams_of[9], (D,), jnp.float32), 0.25, 1.75)
    router_weight = bell_draw(streams_of[10], (D, EXPERTS), (4 * D) ** -0.5, 0.09375)
    gate_weight = bell_draw(streams_of[11], (EXPERTS, D, FF), D ** -0.5, 0.1875, ((0, 8),))
    up_weight = bell_draw(streams_of[12], (EXPERTS, D, FF), D ** -0.5, 0.1875, ((0, 8),))
    down_weight = bell_draw(streams_of[13], (EXPERTS, FF, D), (FF // 16) ** -0.5, 1.0, ((0, 8),))
    out_grad = bell_draw(streams_of[14], (ROWS, SEQ_LEN, D), 1.0, 6.0, ((0, 4), (1, 8)))
    return {"hidden_in": hidden_in, "segment_ids": segment_ids, "positions": positions, "expert_ids": expert_ids, "first_gain": first_gain, "query_weight": query_weight, "key_weight": key_weight, "value_weight": value_weight, "output_weight": output_weight, "second_gain": second_gain, "router_weight": router_weight, "gate_weight": gate_weight, "up_weight": up_weight, "down_weight": down_weight, "out_grad": out_grad}


EPS = 1e-06
THETA = 10000.0
NEG = -1e+30

@jax.custom_vjp
def low(v):
    return lax.optimization_barrier(v.astype(jnp.bfloat16)).astype(jnp.float32)

@jax.custom_vjp
def low_back(v):
    return v

def low_keep(v):
    return (low(v), None)

def low_pass(kept, grad):
    return (grad,)

def back_keep(v):
    return (v, None)

def back_low(kept, grad):
    return (low(grad),)
low.defvjp(low_keep, low_pass)
low_back.defvjp(back_keep, back_low)

def rms_scale(values, gain):
    return values * lax.rsqrt(lax.optimization_barrier(jnp.mean(values * values, axis=-1, keepdims=True)) + EPS) * gain

def project(left, right):
    return jnp.einsum('...d,de->...e', left, right, precision=lax.Precision.HIGHEST)

def rotate(values, places):
    middle = values.shape[-1] // 2
    frequency = jnp.exp(jnp.arange(middle, dtype=jnp.float32) * (-2.0 * math.log(THETA) / values.shape[-1]))
    angles = places.astype(jnp.float32)[..., None, None] * frequency
    cosine = jnp.cos(angles)
    sine_part = jnp.sin(angles)
    first = values[..., :middle]
    second = values[..., middle:]
    return jnp.concatenate([first * cosine - second * sine_part, second * cosine + first * sine_part], axis=-1)

def attention(queries, key_rows, value_rows, segments):
    length = queries.shape[1]
    block_rows = math.gcd(length, 512)
    block_count = length // block_rows
    scale = queries.shape[-1] ** (-0.5)
    key_places = jnp.arange(length, dtype=jnp.int32)

    def one_row(operands):
        query_row, key_row, value_row, segment_row = operands

        def one_block(pieces):
            query_block, segment_block, start = pieces
            raw_scores = low_back(jnp.einsum('qgjd,kgd->qgjk', query_block, key_row, precision=lax.Precision.HIGHEST))
            query_places = start + jnp.arange(block_rows, dtype=jnp.int32)
            allowed = (key_places[None, :] <= query_places[:, None]) & (segment_row[None, :] == segment_block[:, None])
            scores = jnp.where(allowed[:, None, None, :], raw_scores * scale, NEG)
            probs = jax.nn.softmax(scores, axis=-1)
            return jnp.einsum('qgjk,kgd->qgjd', low(probs), value_row, precision=lax.Precision.HIGHEST)
        blocks = (query_row.reshape((block_count, block_rows) + query_row.shape[1:]), segment_row.reshape(block_count, block_rows), jnp.arange(block_count, dtype=jnp.int32) * block_rows)
        outcome = lax.map(jax.checkpoint(one_block), blocks)
        return outcome.reshape(length, -1)
    return lax.map(jax.checkpoint(one_row), (queries, key_rows, value_rows, segments))

def mixture(expert_input, gates, expert_ids, w_gate, w_up, w_down):
    blocks = ROWS * N_SEQ
    flat_input = expert_input.reshape(blocks * BLK, D)
    routes = expert_ids.reshape(blocks, BLK, TOPK)
    gate_blocks = gates.reshape(blocks, BLK, TOPK)
    one_hot = (routes[..., None] == jnp.arange(EXPERTS, dtype=jnp.int32)).astype(jnp.int32)
    one_hot = one_hot.reshape(blocks, BLK * TOPK, EXPERTS)
    ranks = jnp.cumsum(one_hot, axis=1, dtype=jnp.int32) - 1
    slots = lax.optimization_barrier(jnp.sum(ranks * one_hot, axis=-1, dtype=jnp.int32)).reshape(blocks, BLK, TOPK)
    block_index = jnp.broadcast_to(jnp.arange(blocks, dtype=jnp.int32)[:, None, None], routes.shape)
    token_index = jnp.broadcast_to(jnp.arange(blocks * BLK, dtype=jnp.int32).reshape(blocks, BLK)[:, :, None], routes.shape)
    slot_token = jnp.full((EXPERTS, blocks, MOST), blocks * BLK, jnp.int32).at[routes, block_index, slots].set(token_index)
    padded = jnp.concatenate([flat_input, jnp.zeros((1, D), jnp.float32)], axis=0)

    def one_expert(operands):
        weight_gate, weight_up, weight_down, rows_index = operands
        entering = low_back(padded[rows_index.reshape(-1)])
        gate_pre = low_back(project(entering, weight_gate))
        up_pre = low_back(project(entering, weight_up))
        hidden_act = low(jax.nn.silu(gate_pre) * up_pre)
        return low(low_back(project(hidden_act, weight_down)))
    produced = lax.map(jax.checkpoint(one_expert), (w_gate, w_up, w_down, slot_token))
    produced = produced.reshape(EXPERTS, blocks, MOST, D)
    picked = produced[routes, block_index, slots]
    return lax.optimization_barrier(jnp.sum(gate_blocks[..., None] * picked, axis=2)).reshape(ROWS, SEQ_LEN, D)

def reference(hidden_in, segment_ids, positions, expert_ids, first_gain, query_weight, key_weight, value_weight, output_weight, second_gain, router_weight, gate_weight, up_weight, down_weight, out_grad):

    def forward(inputs, gain_one, w_query, w_key, w_value, w_output, gain_two, w_router, w_gate, w_up, w_down):
        mixer_input = low(rms_scale(inputs, gain_one))
        query_pre = low_back(project(mixer_input, w_query)).reshape(ROWS, SEQ_LEN, HEADS, HEAD_DIM)
        key_pre = low_back(project(mixer_input, w_key)).reshape(ROWS, SEQ_LEN, KV_HEADS, HEAD_DIM)
        value_rows = low(low_back(project(mixer_input, w_value))).reshape(ROWS, SEQ_LEN, KV_HEADS, HEAD_DIM)
        queries = low(rotate(query_pre, positions)).reshape(ROWS, SEQ_LEN, KV_HEADS, HEADS // KV_HEADS, HEAD_DIM)
        key_rows = low(rotate(key_pre, positions))
        attended = low(low_back(attention(queries, key_rows, value_rows, segment_ids)))
        residual = inputs + low_back(project(attended, w_output))
        expert_input = low(rms_scale(residual, gain_two))
        logits = project(expert_input, w_router)
        gates = jax.nn.softmax(jnp.take_along_axis(logits, expert_ids, axis=-1), axis=-1)
        return residual + mixture(expert_input, gates, expert_ids, w_gate, w_up, w_down)
    operands = (hidden_in.astype(jnp.float32), first_gain.astype(jnp.float32), query_weight.astype(jnp.float32), key_weight.astype(jnp.float32), value_weight.astype(jnp.float32), output_weight.astype(jnp.float32), second_gain.astype(jnp.float32), router_weight.astype(jnp.float32), gate_weight.astype(jnp.float32), up_weight.astype(jnp.float32), down_weight.astype(jnp.float32))
    result, pullback = jax.vjp(forward, *operands)
    grads = pullback(out_grad.astype(jnp.float32))
    return (result.astype(jnp.bfloat16), grads[0], grads[1], grads[2], grads[3], grads[4], grads[5], grads[6], grads[7], grads[8], grads[9], grads[10])
```

```python
import functools
import math

import jax
import jax.numpy as jnp
from jax import lax
from jax.experimental import pallas as pl
from jax.experimental.pallas import tpu as pltpu
from jax.sharding import PartitionSpec as P

HEADS = 16
KV_HEADS = 8
HEAD_DIM = 64
TOPK = 8
MOST = 32
BLOCK = 64
LANES = 128
TILES = KV_HEADS * HEAD_DIM // LANES
PAIR = 2
PAD = 16

EPS = 1e-06
THETA = 10000.0
NEG = -1e30
F32 = jnp.float32
BF16 = jnp.bfloat16
EXACT = lax.Precision.HIGHEST
NN = (((1,), (0,)), ((), ()))
NT = (((1,), (1,)), ((), ()))
TN = (((0,), (0,)), ((), ()))


def mul(left, right, dims=NN, precision=None):
    return lax.dot_general(left, right, dims, precision=precision, preferred_element_type=F32)


def params(megabytes):
    return pltpu.CompilerParams(vmem_limit_bytes=megabytes << 20)


def whole():
    return pl.BlockSpec(memory_space=pltpu.VMEM)


def scalars():
    return pl.BlockSpec(memory_space=pltpu.SMEM)


def struct(shape, dtype):
    return jax.ShapeDtypeStruct(shape, dtype)


def cost(flops, moved):
    return pl.CostEstimate(flops=int(flops), bytes_accessed=int(moved), transcendentals=0)


def low_half(shape):
    return lax.broadcasted_iota(jnp.int32, shape, 1) < HEAD_DIM


def swap_halves(tile):
    lane = lax.broadcasted_iota(jnp.int32, tile.shape, 1)
    quarter = HEAD_DIM // 2
    forward = pltpu.roll(tile, LANES - quarter, 1)
    backward = pltpu.roll(tile, quarter, 1)
    return jnp.where(lane % HEAD_DIM < quarter, forward, backward)


def rotate(tile, cosine, signed_sine):
    return tile * cosine + swap_halves(tile) * signed_sine


def unrotate(tile, cosine, signed_sine):
    return tile * cosine - swap_halves(tile) * signed_sine


def spread_heads(first, second):
    low = low_half(first.shape)
    return jnp.concatenate(
        [
            jnp.where(low, first, 0.0),
            jnp.where(low, pltpu.roll(first, HEAD_DIM, 1), 0.0),
            jnp.where(low, 0.0, pltpu.roll(second, HEAD_DIM, 1)),
            jnp.where(low, 0.0, second),
        ],
        axis=0,
    )


def gather_heads(stacked):
    low = low_half((BLOCK, LANES))
    one, two, three, four = (stacked[i * BLOCK : (i + 1) * BLOCK] for i in range(4))
    first = jnp.where(low, one, pltpu.roll(two, HEAD_DIM, 1))
    second = jnp.where(low, pltpu.roll(three, HEAD_DIM, 1), four)
    return first, second


def allowed_keys(piece, members, member, pos_ref):
    keys = (piece + 1) * members * BLOCK
    start = (piece * members + member) * BLOCK
    place = start + lax.broadcasted_iota(jnp.int32, (BLOCK, keys), 0)
    key = lax.broadcasted_iota(jnp.int32, (BLOCK, keys), 1)
    opening = place - pos_ref[piece * BLOCK : (piece + 1) * BLOCK, :]
    return (key <= place) & (key >= opening)


def probabilities(stacked, key_tile, allowed):
    keys = key_tile.shape[0]
    scores = mul(stacked, key_tile, NT) * HEAD_DIM**-0.5
    scores = scores.reshape(4, BLOCK, keys)
    scores = jnp.where(allowed[None], scores, NEG)
    weights = jnp.exp(scores - jnp.max(scores, axis=-1, keepdims=True))
    probs = weights * (1.0 / jnp.sum(weights, axis=-1, keepdims=True))
    return probs.reshape(4 * BLOCK, keys)


def two_parts(values):
    high = values.astype(BF16).astype(F32)
    return jnp.concatenate([high, values - high], axis=0).astype(BF16)


def front_kernel(
    members,
    me_ref,
    h_ref,
    cos_ref,
    sin_ref,
    pos_ref,
    ids_ref,
    gain_one_ref,
    wq_ref,
    wk_ref,
    wv_ref,
    wo_ref,
    gain_two_ref,
    router_ref,
    mix_ref,
    own_ref,
    qz_ref,
    k_ref,
    v_ref,
    att_ref,
    res_ref,
    xg_ref,
    gates_ref,
):
    member = me_ref[0]
    length, width = h_ref.shape
    tokens = own_ref.shape[0]
    pieces = tokens // BLOCK
    step = 256

    def keys_step(i, carry):
        rows = pl.ds(pl.multiple_of(i * step, step), step)
        x = h_ref[rows, :].astype(F32)
        scale = lax.rsqrt(jnp.mean(x * x, axis=-1, keepdims=True) + EPS)
        mix = (x * scale * gain_one_ref[...]).astype(BF16)
        mix_ref[rows, :] = mix
        v_ref[rows, :] = mul(mix, wv_ref[...]).astype(BF16)
        pre = mul(mix, wk_ref[...])
        cosine, sine = cos_ref[rows, :], sin_ref[rows, :]
        for tile in range(TILES):
            lanes = slice(tile * LANES, (tile + 1) * LANES)
            k_ref[rows, lanes] = rotate(pre[:, lanes], cosine, sine).astype(BF16)
        return carry

    lax.fori_loop(0, length // step, keys_step, 0)
    own = [pl.ds(pl.multiple_of((p * members + member) * BLOCK, BLOCK), BLOCK) for p in range(pieces)]
    for piece in range(pieces):
        own_ref[piece * BLOCK : (piece + 1) * BLOCK, :] = mix_ref[own[piece], :]

    def query_step(tile, carry):
        pre = mul(own_ref[...], wq_ref[:, pl.ds(pl.multiple_of(tile * 256, 256), 256)])
        for piece in range(pieces):
            rows = slice(piece * BLOCK, (piece + 1) * BLOCK)
            cosine, sine = cos_ref[own[piece], :], sin_ref[own[piece], :]
            first = rotate(pre[rows, :LANES], cosine, sine)
            second = rotate(pre[rows, LANES:], cosine, sine)
            qz_ref[piece, tile] = spread_heads(first, second).astype(BF16)
        return carry

    lax.fori_loop(0, TILES, query_step, 0)
    for piece in range(pieces):
        allowed = allowed_keys(piece, members, member, pos_ref)
        keys = allowed.shape[1]
        rows = slice(piece * BLOCK, (piece + 1) * BLOCK)

        def attend(tile, carry):
            lanes = pl.ds(pl.multiple_of(tile * LANES, LANES), LANES)
            probs = probabilities(qz_ref[piece, tile], k_ref[:keys, lanes], allowed)
            first, second = gather_heads(mul(probs.astype(BF16), v_ref[:keys, lanes]))
            at = pl.multiple_of(tile * 256, 256)
            att_ref[rows, pl.ds(at, LANES)] = first.astype(BF16)
            att_ref[rows, pl.ds(at + LANES, LANES)] = second.astype(BF16)
            return carry

        lax.fori_loop(0, TILES, attend, 0)
    mixed = mul(att_ref[...], wo_ref[...])
    for piece in range(pieces):
        rows = slice(piece * BLOCK, (piece + 1) * BLOCK)
        res_ref[rows, :] = h_ref[own[piece], :].astype(F32) + mixed[rows]
    residual = res_ref[...]
    scale = lax.rsqrt(jnp.mean(residual * residual, axis=-1, keepdims=True) + EPS)
    chosen = (residual * scale * gain_two_ref[...]).astype(BF16)
    xg_ref[:tokens, :] = chosen
    logits = mul(router_ref[...], chosen, NT)
    expert = lax.broadcasted_iota(jnp.int32, logits.shape, 0)
    named = expert == ids_ref[0:1, :]
    for k in range(1, TOPK):
        named = named | (expert == ids_ref[k : k + 1, :])
    logits = jnp.where(named, logits, NEG)
    weights = jnp.where(named, jnp.exp(logits - jnp.max(logits, axis=0, keepdims=True)), 0.0)
    gates = weights / jnp.sum(weights, axis=0, keepdims=True)
    gates_ref[...] = gates
    for part in range(logits.shape[0] // 8):
        lanes = slice(part * tokens, (part + 1) * tokens)
        xg_ref[tokens:, lanes] = two_parts(gates[part * 8 : (part + 1) * 8])


def one_hot(slot_row, rows):
    slot = lax.broadcasted_iota(jnp.int32, (rows, slot_row.shape[1]), 0).astype(F32)
    return slot == slot_row


def upstream_kernel(named_ref, u_ref, wd_ref, slot_ref, ug_ref, v_ref):
    experts = wd_ref.shape[0]
    tokens = named_ref.shape[2]
    width = wd_ref.shape[2]
    rows = tokens * MOST // BLOCK
    earlier = lax.broadcasted_iota(jnp.int32, (tokens, tokens), 0)
    later = lax.broadcasted_iota(jnp.int32, (tokens, tokens), 1)
    before = (earlier < later).astype(F32).astype(BF16)
    for c in range(PAIR):
        named = named_ref[c]
        rank = mul(named.astype(BF16), before)
        slot_ref[c] = jnp.where(named > 0, rank, -1.0)

    def expert_step(e, carry):
        at = pl.ds(pl.multiple_of(e * rows, rows), rows)
        both = []
        for c in range(PAIR):
            pick = one_hot(slot_ref[c, pl.ds(e, 1), :], rows).astype(F32).astype(BF16)
            picked = mul(pick, u_ref[:, c, 0].reshape(tokens, width)).astype(BF16)
            ug_ref[c, at, :] = picked
            both.append(picked)
        product = mul(jnp.concatenate(both, axis=0), wd_ref[e], NT)
        for c in range(PAIR):
            v_ref[c, at, :] = product[c * rows : (c + 1) * rows]
        return carry

    lax.fori_loop(0, experts, expert_step, 0)


def expert_kernel(
    me_ref,
    xg_ref,
    slot_ref,
    v_ref,
    wg_ref,
    wu_ref,
    wd_ref,
    dx_ref,
    y_ref,
    xs_ref,
    hs_ref,
    dg_ref,
    du_ref,
    dxs_ref,
    ys_ref,
    pick_ref,
    gates_ref,
    back_ref,
):
    experts = wd_ref.shape[0]
    tokens = slot_ref.shape[2]
    rows = tokens * MOST // BLOCK
    first = me_ref[1] * experts
    back_ref[...] = jnp.zeros_like(back_ref)

    def expert_step(e, carry):
        at = pl.ds(pl.multiple_of(e * rows, rows), rows)
        number = first + e
        row = lax.rem(number, 8)
        lanes = pl.ds(pl.multiple_of(lax.div(number, 8) * tokens, tokens), tokens)
        entering, gate = [], []
        for c in range(PAIR):
            hot = one_hot(slot_ref[c, pl.ds(e, 1), :], rows)
            pick = hot.astype(F32).astype(BF16)
            pick_ref[c, at, :] = pick
            picked = mul(pick, xg_ref[c, :tokens, :]).astype(BF16)
            xs_ref[c, at, :] = picked
            entering.append(picked)
            sent = xg_ref[c, tokens:, lanes].astype(F32)
            gates_ref[...] = sent[:8] + sent[8:]
            gate.append(jnp.sum(jnp.where(hot, gates_ref[pl.ds(row, 1), :], 0.0), axis=1, keepdims=True))
        entering = jnp.concatenate(entering, axis=0)
        gate = jnp.concatenate(gate, axis=0)
        gate_pre = mul(entering, wg_ref[e])
        up_pre = mul(entering, wu_ref[e])
        share = 1.0 / (1.0 + jnp.exp(-gate_pre))
        silu = gate_pre * share
        hidden = silu * up_pre
        product = jnp.concatenate([v_ref[c, at, :] for c in range(PAIR)], axis=0)
        grad_gate = jnp.sum(hidden * product, axis=1, keepdims=True)
        grad_act = gate * product
        grad_gate_pre = (grad_act * up_pre * share * (1.0 + gate_pre * (1.0 - share))).astype(BF16)
        grad_up_pre = (grad_act * silu).astype(BF16)
        gated = (gate * hidden).astype(BF16)
        grad_rows = (mul(grad_gate_pre, wg_ref[e], NT) + mul(grad_up_pre, wu_ref[e], NT)).astype(BF16)
        out_rows = mul(gated, wd_ref[e]).astype(BF16)
        for c in range(PAIR):
            part = slice(c * rows, (c + 1) * rows)
            hs_ref[c, at, :] = gated[part]
            dg_ref[c, at, :] = grad_gate_pre[part]
            du_ref[c, at, :] = grad_up_pre[part]
            dxs_ref[c, at, :] = grad_rows[part]
            ys_ref[c, at, :] = out_rows[part]
            hot = one_hot(slot_ref[c, pl.ds(e, 1), :], rows)
            returned = jnp.sum(jnp.where(hot, grad_gate[part], 0.0), axis=0, keepdims=True)
            high = returned.astype(BF16).astype(F32)
            back_ref[c, pl.ds(row, 1), lanes] = high
            back_ref[c, pl.ds(row + 8, 1), lanes] = returned - high
        return carry

    lax.fori_loop(0, experts, expert_step, 0)
    for c in range(PAIR):
        dx_ref[c, :tokens, :] = mul(pick_ref[c], dxs_ref[c], TN).astype(BF16)
        dx_ref[c, tokens:, :] = back_ref[c].astype(BF16)
        y_ref[c] = mul(pick_ref[c], ys_ref[c], TN).astype(BF16)


def expert_grads_kernel(
    xs_ref, us_ref, hs_ref, dg_ref, du_ref, gate_ref, up_ref, down_ref, gate_acc, up_acc, down_acc
):
    count = pl.num_programs(1)
    group, rows, width = xs_ref.shape
    inner = hs_ref.shape[2]
    flat = lambda ref: ref[...].reshape(group * rows, ref.shape[2])

    @pl.when(pl.program_id(1) == 0)
    def _():
        gate_acc[...] = jnp.zeros_like(gate_acc)
        up_acc[...] = jnp.zeros_like(up_acc)
        down_acc[...] = jnp.zeros_like(down_acc)

    step = 256
    for at in range(0, width, step):
        entering = xs_ref[:, :, at : at + step].reshape(group * rows, step)
        gate_acc[at : at + step, :] += mul(entering, flat(dg_ref), TN)
        up_acc[at : at + step, :] += mul(entering, flat(du_ref), TN)
    for at in range(0, inner, step):
        gated = hs_ref[:, :, at : at + step].reshape(group * rows, step)
        down_acc[at : at + step, :] += mul(gated, flat(us_ref), TN)

    @pl.when(pl.program_id(1) == count - 1)
    def _():
        gate_ref[0] = gate_acc[...].astype(BF16)
        up_ref[0] = up_acc[...].astype(BF16)
        down_ref[0] = down_acc[...].astype(BF16)


def middle_kernel(
    dx_ref,
    u_ref,
    xg_ref,
    res_ref,
    gates_ref,
    gain_two_ref,
    router_ref,
    wo_ref,
    att_ref,
    output_ref,
    vectors_ref,
    gres_ref,
    gaz_ref,
):
    tokens, width = u_ref.shape
    experts = gates_ref.shape[0]
    pieces = tokens // BLOCK
    parts = []
    for part in range(experts // 8):
        sent = dx_ref[tokens:, part * tokens : (part + 1) * tokens].astype(F32)
        parts.append(sent[:8] + sent[8:])
    grad_gates = jnp.concatenate(parts, axis=0)
    gates = gates_ref[...]
    grad_logits = gates * (grad_gates - jnp.sum(gates * grad_gates, axis=0, keepdims=True))
    grad_normed = dx_ref[:tokens, :].astype(F32) + mul(
        grad_logits, router_ref[...].astype(F32), TN, EXACT
    )
    router = mul(grad_logits, xg_ref[:tokens, :].astype(F32), NN, EXACT)
    residual = res_ref[...]
    scale = lax.rsqrt(jnp.mean(residual * residual, axis=-1, keepdims=True) + EPS)
    normed = residual * scale
    second = jnp.sum(grad_normed * normed, axis=0, keepdims=True)
    vectors_ref[...] = jnp.concatenate(
        [router, second, jnp.zeros((vectors_ref.shape[0] - experts - 1, width), F32)], axis=0
    ).astype(BF16)
    scaled = grad_normed * gain_two_ref[...]
    grad_residual = u_ref[...].astype(F32) + scale * (
        scaled - normed * jnp.mean(scaled * normed, axis=-1, keepdims=True)
    )
    gres_ref[...] = grad_residual
    grad_mixed = grad_residual.astype(BF16)
    output_ref[...] = mul(att_ref[...], grad_mixed, TN).astype(BF16)
    for tile in range(TILES):
        grad_att = mul(grad_mixed, wo_ref[tile * 256 : (tile + 1) * 256, :], NT)
        for piece in range(pieces):
            rows = slice(piece * BLOCK, (piece + 1) * BLOCK)
            gaz_ref[piece, tile] = spread_heads(
                grad_att[rows, :LANES], grad_att[rows, LANES:]
            ).astype(BF16)


def attention_back_kernel(
    members,
    me_ref,
    qz_ref,
    gaz_ref,
    k_ref,
    v_ref,
    pos_ref,
    cos_ref,
    sin_ref,
    mix_ref,
    own_ref,
    dq_ref,
    dkv_ref,
    query_ref,
    keyval_ref,
    dk_acc,
    dv_acc,
    row_ref,
):
    member = me_ref[0]
    tokens = own_ref.shape[0]
    pieces = tokens // BLOCK
    length = k_ref.shape[0]
    inner = k_ref.shape[1]
    dk_acc[...] = jnp.zeros_like(dk_acc)
    dv_acc[...] = jnp.zeros_like(dv_acc)
    for piece in range(pieces):
        allowed = allowed_keys(piece, members, member, pos_ref)
        keys = allowed.shape[1]
        rows = slice(piece * BLOCK, (piece + 1) * BLOCK)
        at = pl.ds(pl.multiple_of((piece * members + member) * BLOCK, BLOCK), BLOCK)

        def step(tile, carry):
            lanes = pl.ds(pl.multiple_of(tile * LANES, LANES), LANES)
            stacked, grads = qz_ref[piece, tile], gaz_ref[piece, tile]
            key_tile = k_ref[:keys, lanes]
            probs = probabilities(stacked, key_tile, allowed)
            grad_probs = mul(grads, v_ref[:keys, lanes], NT)
            delta = jnp.sum(probs * grad_probs, axis=-1, keepdims=True)
            grad_scores = (probs * (grad_probs - delta) * HEAD_DIM**-0.5).astype(BF16)
            dk_acc[:keys, lanes] += mul(grad_scores, stacked, TN)
            dv_acc[:keys, lanes] += mul(probs.astype(BF16), grads, TN)
            first, second = gather_heads(mul(grad_scores, key_tile))
            cosine, sine = cos_ref[at, :], sin_ref[at, :]
            out = pl.multiple_of(tile * 256, 256)
            dq_ref[rows, pl.ds(out, LANES)] = unrotate(first, cosine, sine).astype(BF16)
            dq_ref[rows, pl.ds(out + LANES, LANES)] = unrotate(second, cosine, sine).astype(BF16)
            return carry

        lax.fori_loop(0, TILES, step, 0)
    for block in range(length // BLOCK):
        rows = slice(block * BLOCK, (block + 1) * BLOCK)
        cosine, sine = cos_ref[rows, :], sin_ref[rows, :]
        for tile in range(TILES):
            lanes = slice(tile * LANES, (tile + 1) * LANES)
            row_ref[rows, lanes] = unrotate(dk_acc[rows, lanes], cosine, sine).astype(BF16)
        row_ref[rows, inner:] = dv_acc[rows, :].astype(BF16)
        piece, owner = block // members, block % members
        dkv_ref[owner, piece * BLOCK : (piece + 1) * BLOCK, :] = row_ref[rows, :]
    query_ref[...] = mul(own_ref[...], dq_ref[...], TN).astype(BF16)
    keyval_ref[...] = mul(mix_ref[...], row_ref[...], TN).astype(BF16)


def last_kernel(
    members, me_ref, dq_ref, dkv_ref, wq_ref, wk_ref, wv_ref, h_ref, gres_ref, gain_one_ref, gh_ref, first_ref
):
    member = me_ref[0]
    tokens = dq_ref.shape[0]
    inner = wk_ref.shape[1]
    grad_kv = dkv_ref[0].astype(F32)
    for other in range(1, members):
        grad_kv = grad_kv + dkv_ref[other].astype(F32)
    grad_kv = grad_kv.astype(BF16)
    grad_mixer = (
        mul(dq_ref[...], wq_ref[...], NT)
        + mul(grad_kv[:, :inner], wk_ref[...], NT)
        + mul(grad_kv[:, inner:], wv_ref[...], NT)
    )
    x = jnp.concatenate(
        [
            h_ref[pl.ds(pl.multiple_of((p * members + member) * BLOCK, BLOCK), BLOCK), :]
            for p in range(tokens // BLOCK)
        ],
        axis=0,
    ).astype(F32)
    scale = lax.rsqrt(jnp.mean(x * x, axis=-1, keepdims=True) + EPS)
    normed = x * scale
    first_ref[...] = jnp.broadcast_to(
        jnp.sum(grad_mixer * normed, axis=0, keepdims=True), first_ref.shape
    ).astype(first_ref.dtype)
    scaled = grad_mixer * gain_one_ref[...]
    gh_ref[...] = (
        gres_ref[...]
        + scale * (scaled - normed * jnp.mean(scaled * normed, axis=-1, keepdims=True))
    ).astype(gh_ref.dtype)


def rope_tables(places):
    middle = HEAD_DIM // 2
    frequency = jnp.exp(jnp.arange(middle, dtype=F32) * (-2.0 * math.log(THETA) / HEAD_DIM))
    angles = places.astype(F32)[:, None] * frequency
    cosine, sine = jnp.cos(angles), jnp.sin(angles)
    return (
        jnp.concatenate([cosine] * 4, axis=1),
        jnp.concatenate([-sine, sine, -sine, sine], axis=1),
    )


def local(
    hidden_in,
    segment_ids,
    positions,
    expert_ids,
    first_gain,
    query_weight,
    key_weight,
    value_weight,
    output_weight,
    second_gain,
    router_weight,
    gate_weight,
    up_weight,
    down_weight,
    out_grad,
):
    rows_here, block, width = hidden_in.shape
    tokens = rows_here * block
    shards = lax.axis_size("seq")
    members = shards // rows_here
    length = shards * block
    inner = key_weight.shape[1]
    expert_count = router_weight.shape[1]
    experts, _, hidden = gate_weight.shape
    me = lax.axis_index("seq")
    row, member = me // members, me % members
    me_pair = jnp.stack([member, me]).astype(jnp.int32)
    same_member = [[r * members + m for r in range(rows_here)] for m in range(members)]
    same_row = [[r * members + m for m in range(members)] for r in range(rows_here)]
    slots = tokens * MOST // BLOCK
    groups = shards // PAIR

    meta = jnp.concatenate(
        [positions.reshape(1, tokens), expert_ids.reshape(tokens, TOPK).T], axis=0
    )
    meta = lax.all_to_all(
        jnp.broadcast_to(meta[None], (shards,) + meta.shape), "seq", 0, 0, tiled=True
    )
    row_in = lax.all_to_all(jnp.repeat(hidden_in, members, axis=0), "seq", 0, 0, tiled=True)
    row_in = row_in.reshape(length, width)
    upstream = lax.all_gather(out_grad, "seq", axis=0, tiled=False)

    meta = meta.reshape(rows_here, members, TOPK + 1, rows_here, block)
    row_meta = lax.dynamic_index_in_dim(meta, row, 3, keepdims=False)
    own_meta = lax.dynamic_index_in_dim(row_meta, member, 1, keepdims=False)
    cosine, sine = rope_tables(row_meta[:, :, 0].reshape(length))
    own_pos = own_meta[:, 0].reshape(tokens, 1)
    own_ids = own_meta[:, 1:].transpose(1, 0, 2).reshape(TOPK, tokens)
    lane = jnp.arange(8, dtype=jnp.int32)
    wanted = jnp.where(lane < experts, me * experts + lane, -1)
    named = jnp.any(
        meta[:, :, 1:, None] == wanted[None, None, None, :, None, None], axis=2
    )
    named = named.transpose(3, 1, 2, 0, 4).reshape(shards, 8, tokens).astype(F32)

    gain_one, gain_two = first_gain.reshape(1, width), second_gain.reshape(1, width)
    router = router_weight.T
    mix, own_mix, qz, k_row, v_row, att, residual, xg, gates = pl.pallas_call(
        functools.partial(front_kernel, members),
        out_shape=[
            struct((length, width), BF16),
            struct((tokens, width), BF16),
            struct((rows_here, TILES, 4 * BLOCK, LANES), BF16),
            struct((length, inner), BF16),
            struct((length, inner), BF16),
            struct((tokens, width), BF16),
            struct((tokens, width), F32),
            struct((tokens + PAD, width), BF16),
            struct((expert_count, tokens), F32),
        ],
        in_specs=[scalars()] + [whole()] * 12,
        out_specs=[whole()] * 9,
        compiler_params=params(56),
        cost_estimate=cost(5e9, 12e6),
        name="front",
    )(
        me_pair,
        row_in,
        cosine,
        sine,
        own_pos,
        own_ids,
        gain_one,
        query_weight,
        key_weight,
        value_weight,
        output_weight,
        gain_two,
        router,
    )

    constant = lambda shape: pl.BlockSpec(
        shape, lambda i: (0,) * len(shape), pipeline_mode=pl.Buffered(1)
    )
    grouped = lambda *shape: pl.BlockSpec((PAIR,) + shape, lambda i: (i,) + (0,) * len(shape))
    per_row = members // PAIR
    upstream = upstream.reshape(rows_here, members, rows_here, block, width)
    slot, us, product = pl.pallas_call(
        upstream_kernel,
        grid=(groups,),
        out_shape=[
            struct((shards, 8, tokens), F32),
            struct((shards, experts * slots, width), BF16),
            struct((shards, experts * slots, hidden), F32),
        ],
        in_specs=[
            grouped(8, tokens),
            pl.BlockSpec(
                (rows_here, PAIR, 1, block, width),
                lambda i: (0, i % per_row, i // per_row, 0, 0),
            ),
            constant((experts, hidden, width)),
        ],
        out_specs=[
            grouped(8, tokens),
            grouped(experts * slots, width),
            grouped(experts * slots, hidden),
        ],
        compiler_params=params(48),
        cost_estimate=cost(6e9, 20e6),
        name="upstream",
    )(named, upstream, down_weight)

    gathered = lax.all_gather(xg, "seq", axis=0, tiled=False)
    dx, y, xs, hs, dgs, dus = pl.pallas_call(
        expert_kernel,
        grid=(groups,),
        out_shape=[
            struct((shards, tokens + PAD, width), BF16),
            struct((shards, tokens, width), BF16),
            struct((shards, experts * slots, width), BF16),
            struct((shards, experts * slots, hidden), BF16),
            struct((shards, experts * slots, hidden), BF16),
            struct((shards, experts * slots, hidden), BF16),
        ],
        in_specs=[
            scalars(),
            grouped(tokens + PAD, width),
            grouped(8, tokens),
            grouped(experts * slots, hidden),
            constant((experts, width, hidden)),
            constant((experts, width, hidden)),
            constant((experts, hidden, width)),
        ],
        out_specs=[
            grouped(tokens + PAD, width),
            grouped(tokens, width),
            grouped(experts * slots, width),
            grouped(experts * slots, hidden),
            grouped(experts * slots, hidden),
            grouped(experts * slots, hidden),
        ],
        scratch_shapes=[
            pltpu.VMEM((PAIR, experts * slots, width), BF16),
            pltpu.VMEM((PAIR, experts * slots, width), BF16),
            pltpu.VMEM((PAIR, experts * slots, tokens), BF16),
            pltpu.VMEM((8, tokens), F32),
            pltpu.VMEM((PAIR, PAD, width), F32),
        ],
        compiler_params=params(58),
        cost_estimate=cost(30e9, 50e6),
        name="experts",
    )(me_pair, gathered, slot, product, gate_weight, up_weight, down_weight)
    dx_sum = lax.psum_scatter(dx, "seq", scatter_dimension=0, tiled=False)

    step = 8
    one_expert = lambda w: pl.BlockSpec((step, slots, w), lambda e, i: (i, e, 0))
    grad_spec = lambda a, b: pl.BlockSpec((1, a, b), lambda e, i: (e, 0, 0))
    gate_part, up_part, down_part = pl.pallas_call(
        expert_grads_kernel,
        grid=(experts, shards // step),
        out_shape=[
            struct((experts, width, hidden), BF16),
            struct((experts, width, hidden), BF16),
            struct((experts, hidden, width), BF16),
        ],
        in_specs=[
            one_expert(width),
            one_expert(width),
            one_expert(hidden),
            one_expert(hidden),
            one_expert(hidden),
        ],
        out_specs=[grad_spec(width, hidden), grad_spec(width, hidden), grad_spec(hidden, width)],
        scratch_shapes=[
            pltpu.VMEM((width, hidden), F32),
            pltpu.VMEM((width, hidden), F32),
            pltpu.VMEM((hidden, width), F32),
        ],
        compiler_params=params(48),
        cost_estimate=cost(13e9, 45e6),
        name="expert_grads",
    )(xs, us, hs, dgs, dus)
    gate_sum, up_sum, down_sum = lax.psum((gate_part, up_part, down_part), "rows")
    y_sum = lax.psum_scatter(y, "seq", scatter_dimension=0, tiled=False)

    own_upstream = lax.dynamic_index_in_dim(upstream, row, 2, keepdims=False)
    own_upstream = lax.dynamic_index_in_dim(own_upstream, member, 1, keepdims=False)
    own_upstream = own_upstream.reshape(tokens, width)
    output_part, vectors, grad_residual, gaz = pl.pallas_call(
        middle_kernel,
        out_shape=[
            struct((width, width), BF16),
            struct((expert_count + PAD, width), BF16),
            struct((tokens, width), F32),
            struct((rows_here, TILES, 4 * BLOCK, LANES), BF16),
        ],
        in_specs=[whole()] * 9,
        out_specs=[whole()] * 4,
        compiler_params=params(48),
        cost_estimate=cost(2e9, 10e6),
        name="middle",
    )(dx_sum, own_upstream, xg, residual, gates, gain_two, router, output_weight, att)

    dq, dkv, query_part, keyval_part = pl.pallas_call(
        functools.partial(attention_back_kernel, members),
        out_shape=[
            struct((tokens, width), BF16),
            struct((members, tokens, width), BF16),
            struct((width, width), BF16),
            struct((width, width), BF16),
        ],
        in_specs=[scalars()] + [whole()] * 9,
        out_specs=[whole()] * 4,
        scratch_shapes=[
            pltpu.VMEM((length, inner), F32),
            pltpu.VMEM((length, inner), F32),
            pltpu.VMEM((length, width), BF16),
        ],
        compiler_params=params(58),
        cost_estimate=cost(5e9, 12e6),
        name="attention_back",
    )(me_pair, qz, gaz, k_row, v_row, own_pos, cosine, sine, mix, own_mix)
    dkv = lax.all_to_all(dkv, "seq", 0, 0, tiled=True, axis_index_groups=same_row)
    grad_in, first_part = pl.pallas_call(
        functools.partial(last_kernel, members),
        out_shape=[struct((tokens, width), BF16), struct((PAD, width), BF16)],
        in_specs=[scalars()] + [whole()] * 8,
        out_specs=[whole()] * 2,
        compiler_params=params(48),
        cost_estimate=cost(1e9, 8e6),
        name="last",
    )(me_pair, dq, dkv, query_weight, key_weight, value_weight, row_in, grad_residual, gain_one)

    shared = lax.psum((output_part, query_part, keyval_part, vectors, first_part), ("rows", "seq"))
    output_sum, query_sum, keyval_sum, vector_sum, first_sum = (s.astype(F32) for s in shared)
    hidden_out = (residual + y_sum.astype(F32)).astype(BF16)
    back = lambda values: lax.all_to_all(
        values.reshape(rows_here, block, width), "seq", 0, 0, tiled=True, axis_index_groups=same_member
    )
    return (
        back(hidden_out),
        back(grad_in).astype(F32),
        first_sum[0],
        query_sum,
        keyval_sum[:, :inner],
        keyval_sum[:, inner:],
        output_sum,
        vector_sum[expert_count],
        vector_sum[:expert_count].T,
        gate_sum.astype(F32),
        up_sum.astype(F32),
        down_sum.astype(F32),
    )


def solution(mesh):
    placed = (
        P("rows", "seq", None),
        P("rows", "seq"),
        P("rows", "seq"),
        P("rows", "seq", None),
        P(),
        P(),
        P(),
        P(),
        P(),
        P(),
        P(),
        P("seq", None, None),
        P("seq", None, None),
        P("seq", None, None),
        P("rows", "seq", None),
    )
    return jax.shard_map(
        local,
        mesh=mesh,
        in_specs=placed,
        out_specs=(
            P("rows", "seq", None),
            P("rows", "seq", None),
            P(),
            P(),
            P(),
            P(),
            P(),
            P(),
            P(),
            P("seq", None, None),
            P("seq", None, None),
            P("seq", None, None),
        ),
        check_vma=False,
    )
```

```python
import functools
import math

import jax
import jax.numpy as jnp
from jax import lax
from jax.experimental import pallas as pl
from jax.experimental.pallas import tpu as pltpu
from jax.sharding import PartitionSpec as P

HEADS = 16
KV_HEADS = 8
HEAD_DIM = 64
TOPK = 8
MOST = 32
BLOCK = 64
LANES = 128
TILES = KV_HEADS * HEAD_DIM // LANES
EXTRA = 128
PAIR = 2
PAD = 16

EPS = 1e-06
THETA = 10000.0
NEG = -1e30
F32 = jnp.float32
BF16 = jnp.bfloat16
EXACT = lax.Precision.HIGHEST
NN = (((1,), (0,)), ((), ()))
NT = (((1,), (1,)), ((), ()))
TN = (((0,), (0,)), ((), ()))


def mul(left, right, dims=NN, precision=None):
    return lax.dot_general(left, right, dims, precision=precision, preferred_element_type=F32)


def params(megabytes):
    return pltpu.CompilerParams(vmem_limit_bytes=megabytes << 20)


def whole():
    return pl.BlockSpec(memory_space=pltpu.VMEM)


def scalars():
    return pl.BlockSpec(memory_space=pltpu.SMEM)


def struct(shape, dtype):
    return jax.ShapeDtypeStruct(shape, dtype)


def took(microseconds):
    return pl.CostEstimate(flops=int(microseconds * 0.5e9), bytes_accessed=0, transcendentals=0)


def low_half(shape):
    return lax.broadcasted_iota(jnp.int32, shape, 1) < HEAD_DIM


def swap_halves(tile):
    lane = lax.broadcasted_iota(jnp.int32, tile.shape, 1)
    quarter = HEAD_DIM // 2
    forward = pltpu.roll(tile, LANES - quarter, 1)
    backward = pltpu.roll(tile, quarter, 1)
    return jnp.where(lane % HEAD_DIM < quarter, forward, backward)


def rotate(tile, cosine, signed_sine):
    return tile * cosine + swap_halves(tile) * signed_sine


def unrotate(tile, cosine, signed_sine):
    return tile * cosine - swap_halves(tile) * signed_sine


def spread_heads(first, second):
    low = low_half(first.shape)
    return jnp.concatenate(
        [
            jnp.where(low, first, 0.0),
            jnp.where(low, pltpu.roll(first, HEAD_DIM, 1), 0.0),
            jnp.where(low, 0.0, pltpu.roll(second, HEAD_DIM, 1)),
            jnp.where(low, 0.0, second),
        ],
        axis=0,
    )


def gather_heads(stacked):
    low = low_half((BLOCK, LANES))
    one, two, three, four = (stacked[i * BLOCK : (i + 1) * BLOCK] for i in range(4))
    first = jnp.where(low, one, pltpu.roll(two, HEAD_DIM, 1))
    second = jnp.where(low, pltpu.roll(three, HEAD_DIM, 1), four)
    return first, second


def allowed_keys(piece, members, member, pos_ref):
    keys = (piece + 1) * members * BLOCK
    start = (piece * members + member) * BLOCK
    place = start + lax.broadcasted_iota(jnp.int32, (BLOCK, keys), 0)
    key = lax.broadcasted_iota(jnp.int32, (BLOCK, keys), 1)
    opening = place - pos_ref[piece * BLOCK : (piece + 1) * BLOCK, :]
    return (key <= place) & (key >= opening)


def probabilities(stacked, key_tile, allowed):
    keys = key_tile.shape[0]
    scores = mul(stacked, key_tile, NT) * HEAD_DIM**-0.5
    scores = scores.reshape(4, BLOCK, keys)
    scores = jnp.where(allowed[None], scores, NEG)
    weights = jnp.exp(scores - jnp.max(scores, axis=-1, keepdims=True))
    probs = weights * (1.0 / jnp.sum(weights, axis=-1, keepdims=True))
    return probs.reshape(4 * BLOCK, keys)


def two_parts(values):
    high = values.astype(BF16).astype(F32)
    return jnp.concatenate([high, values - high], axis=0).astype(BF16)


def front_kernel(
    members,
    blocks,
    me_ref,
    *refs,
):
    front_body(members, me_ref, refs[:blocks], *refs[blocks:])


def front_body(
    members,
    me_ref,
    block_refs,
    cos_ref,
    sin_ref,
    pos_ref,
    ids_ref,
    gain_one_ref,
    wq_ref,
    wk_ref,
    wv_ref,
    wo_ref,
    gain_two_ref,
    router_ref,
    mix_ref,
    own_ref,
    qz_ref,
    k_ref,
    v_ref,
    att_ref,
    res_ref,
    xg_ref,
    gates_ref,
    input_ref,
    h_ref,
):
    member = me_ref[0]
    length, width = h_ref.shape
    tokens = own_ref.shape[0]
    pieces = tokens // BLOCK
    step = 256
    for i, block_ref in enumerate(block_refs):
        h_ref[pl.ds(pl.multiple_of(me_ref[2 + i] * BLOCK, BLOCK), BLOCK), :] = block_ref[...]

    def keys_step(i, carry):
        rows = pl.ds(pl.multiple_of(i * step, step), step)
        x = h_ref[rows, :].astype(F32)
        scale = lax.rsqrt(jnp.mean(x * x, axis=-1, keepdims=True) + EPS)
        mix = (x * scale * gain_one_ref[...]).astype(BF16)
        mix_ref[rows, :] = mix
        v_ref[rows, :] = mul(mix, wv_ref[...]).astype(BF16)
        pre = mul(mix, wk_ref[...])
        cosine, sine = cos_ref[rows, :], sin_ref[rows, :]
        for tile in range(TILES):
            lanes = slice(tile * LANES, (tile + 1) * LANES)
            k_ref[rows, lanes] = rotate(pre[:, lanes], cosine, sine).astype(BF16)
        return carry

    lax.fori_loop(0, length // step, keys_step, 0)
    own = [pl.ds(pl.multiple_of((p * members + member) * BLOCK, BLOCK), BLOCK) for p in range(pieces)]
    for piece in range(pieces):
        rows = slice(piece * BLOCK, (piece + 1) * BLOCK)
        own_ref[rows, :] = mix_ref[own[piece], :]
        input_ref[rows, :] = h_ref[own[piece], :]

    def query_step(tile, carry):
        pre = mul(own_ref[...], wq_ref[:, pl.ds(pl.multiple_of(tile * 256, 256), 256)])
        for piece in range(pieces):
            rows = slice(piece * BLOCK, (piece + 1) * BLOCK)
            cosine, sine = cos_ref[own[piece], :], sin_ref[own[piece], :]
            first = rotate(pre[rows, :LANES], cosine, sine)
            second = rotate(pre[rows, LANES:], cosine, sine)
            qz_ref[piece, tile] = spread_heads(first, second).astype(BF16)
        return carry

    lax.fori_loop(0, TILES, query_step, 0)
    for piece in range(pieces):
        allowed = allowed_keys(piece, members, member, pos_ref)
        keys = allowed.shape[1]
        rows = slice(piece * BLOCK, (piece + 1) * BLOCK)

        def attend(tile, carry):
            lanes = pl.ds(pl.multiple_of(tile * LANES, LANES), LANES)
            probs = probabilities(qz_ref[piece, tile], k_ref[:keys, lanes], allowed)
            first, second = gather_heads(mul(probs.astype(BF16), v_ref[:keys, lanes]))
            at = pl.multiple_of(tile * 256, 256)
            att_ref[rows, pl.ds(at, LANES)] = first.astype(BF16)
            att_ref[rows, pl.ds(at + LANES, LANES)] = second.astype(BF16)
            return carry

        lax.fori_loop(0, TILES, attend, 0)
    mixed = mul(att_ref[...], wo_ref[...])
    residual = input_ref[...].astype(F32) + mixed
    res_ref[...] = residual
    scale = lax.rsqrt(jnp.mean(residual * residual, axis=-1, keepdims=True) + EPS)
    chosen = (residual * scale * gain_two_ref[...]).astype(BF16)
    xg_ref[:tokens, :] = chosen
    logits = mul(router_ref[...], chosen, NT)
    expert = lax.broadcasted_iota(jnp.int32, logits.shape, 0)
    named = expert == ids_ref[0:1, :]
    for k in range(1, TOPK):
        named = named | (expert == ids_ref[k : k + 1, :])
    logits = jnp.where(named, logits, NEG)
    weights = jnp.where(named, jnp.exp(logits - jnp.max(logits, axis=0, keepdims=True)), 0.0)
    gates = weights / jnp.sum(weights, axis=0, keepdims=True)
    gates_ref[...] = gates
    for part in range(logits.shape[0] // 8):
        lanes = slice(part * tokens, (part + 1) * tokens)
        xg_ref[tokens:, lanes] = two_parts(gates[part * 8 : (part + 1) * 8])


def one_hot(slot_row, rows):
    slot = lax.broadcasted_iota(jnp.int32, (rows, slot_row.shape[1]), 0).astype(F32)
    return slot == slot_row


def upstream_kernel(named_ref, u_ref, wd_ref, tied_ref, slot_ref, ug_ref, v_ref):
    experts = wd_ref.shape[0]
    tokens = named_ref.shape[2]
    width = wd_ref.shape[2]
    rows = tokens * MOST // BLOCK
    earlier = lax.broadcasted_iota(jnp.int32, (tokens, tokens), 0)
    later = lax.broadcasted_iota(jnp.int32, (tokens, tokens), 1)
    before = (earlier < later).astype(F32).astype(BF16)
    for c in range(PAIR):
        named = named_ref[c]
        rank = mul(named.astype(BF16), before)
        slot_ref[c] = jnp.where(named > 0, rank, -1.0)

    def expert_step(e, carry):
        at = pl.ds(pl.multiple_of(e * rows, rows), rows)
        both = []
        for c in range(PAIR):
            pick = one_hot(slot_ref[c, pl.ds(e, 1), :], rows).astype(F32).astype(BF16)
            picked = mul(pick, u_ref[:, c, 0].reshape(tokens, width)).astype(BF16)
            ug_ref[c, at, :] = picked
            both.append(picked)
        product = mul(jnp.concatenate(both, axis=0), wd_ref[e], NT)
        for c in range(PAIR):
            v_ref[c, at, :] = product[c * rows : (c + 1) * rows]
        return carry

    lax.fori_loop(0, experts, expert_step, 0)


def expert_kernel(
    kept,
    info_ref,
    xa_ref,
    xb_ref,
    slot_ref,
    v_ref,
    wg_ref,
    wu_ref,
    wd_ref,
    *rest,
):
    (dxa_ref, dxb_ref, ya_ref, yb_ref, xs_ref, hs_ref, dg_ref, du_ref) = rest[kept : kept + 8]
    (dxs_ref, ys_ref, pick_ref, gates_ref, back_ref) = rest[kept + 8 :]
    e = pl.program_id(0)
    experts = pl.num_programs(0)
    tokens = slot_ref.shape[2]
    rows = tokens * MOST // BLOCK
    places = [(info_ref[0] + c) % PAIR for c in range(PAIR)]
    sources = (xa_ref, xb_ref)

    @pl.when(e == 0)
    def _():
        back_ref[...] = jnp.zeros_like(back_ref)

    at = pl.ds(pl.multiple_of(e * rows, rows), rows)
    number = info_ref[1] * experts + e
    row = lax.rem(number, 8)
    lanes = pl.ds(pl.multiple_of(lax.div(number, 8) * tokens, tokens), tokens)
    entering, gate = [], []
    for c in range(PAIR):
        hot = one_hot(slot_ref[places[c], pl.ds(e, 1), :], rows)
        pick = hot.astype(F32).astype(BF16)
        pick_ref[c, at, :] = pick
        picked = mul(pick, sources[c][:tokens, :]).astype(BF16)
        xs_ref[places[c]] = picked
        entering.append(picked)
        sent = sources[c][tokens:, lanes].astype(F32)
        gates_ref[...] = sent[:8] + sent[8:]
        gate.append(jnp.sum(jnp.where(hot, gates_ref[pl.ds(row, 1), :], 0.0), axis=1, keepdims=True))
    entering = jnp.concatenate(entering, axis=0)
    gate = jnp.concatenate(gate, axis=0)
    gate_pre = mul(entering, wg_ref[0])
    up_pre = mul(entering, wu_ref[0])
    share = 1.0 / (1.0 + jnp.exp(-gate_pre))
    silu = gate_pre * share
    hidden = silu * up_pre
    product = jnp.concatenate([v_ref[places[c]] for c in range(PAIR)], axis=0)
    grad_gate = jnp.sum(hidden * product, axis=1, keepdims=True)
    grad_act = gate * product
    grad_gate_pre = (grad_act * up_pre * share * (1.0 + gate_pre * (1.0 - share))).astype(BF16)
    grad_up_pre = (grad_act * silu).astype(BF16)
    gated = (gate * hidden).astype(BF16)
    grad_rows = (mul(grad_gate_pre, wg_ref[0], NT) + mul(grad_up_pre, wu_ref[0], NT)).astype(BF16)
    out_rows = mul(gated, wd_ref[0]).astype(BF16)
    for c in range(PAIR):
        part = slice(c * rows, (c + 1) * rows)
        hs_ref[places[c]] = gated[part]
        dg_ref[places[c]] = grad_gate_pre[part]
        du_ref[places[c]] = grad_up_pre[part]
        dxs_ref[c, at, :] = grad_rows[part]
        ys_ref[c, at, :] = out_rows[part]
        hot = one_hot(slot_ref[places[c], pl.ds(e, 1), :], rows)
        returned = jnp.sum(jnp.where(hot, grad_gate[part], 0.0), axis=0, keepdims=True)
        high = returned.astype(BF16).astype(F32)
        back_ref[c, pl.ds(row, 1), lanes] = high
        back_ref[c, pl.ds(row + 8, 1), lanes] = returned - high

    @pl.when(e == experts - 1)
    def _():
        for c, (dx_ref, y_ref) in enumerate(((dxa_ref, ya_ref), (dxb_ref, yb_ref))):
            dx_ref[:tokens, :] = mul(pick_ref[c], dxs_ref[c], TN).astype(BF16)
            dx_ref[tokens:, :] = back_ref[c].astype(BF16)
            y_ref[...] = mul(pick_ref[c], ys_ref[c], TN).astype(BF16)


def expert_grads_kernel(
    info_ref, xs_ref, us_ref, hs_ref, dg_ref, du_ref, earlier_ref, tied_ref, sent_ref, keep_ref, send_ref
):
    core = info_ref[3]
    group, rows, width = xs_ref.shape
    inner = hs_ref.shape[2]
    flat = lambda ref: ref[...].reshape(group * rows, ref.shape[2])

    for half, out_ref in ((core, keep_ref), (1 - core, send_ref)):
        step = min(256, width // 2)
        for at in range(0, width // 2, step):
            lanes = pl.ds(pl.multiple_of(half * (width // 2) + at, LANES), step)
            entering = xs_ref[:, :, lanes].reshape(group * rows, step)
            out_ref[0, 0, at : at + step, :] = mul(entering, flat(dg_ref), TN).astype(BF16)
            out_ref[0, 1, at : at + step, :] = mul(entering, flat(du_ref), TN).astype(BF16)
        step = inner // 2
        lanes = pl.ds(pl.multiple_of(half * step, LANES), step)
        gated = hs_ref[:, :, lanes].reshape(group * rows, step)
        product = mul(gated, flat(us_ref), TN).astype(BF16)
        out_ref[0, 2, :step, :] = product[:, :inner]
        out_ref[0, 2, step:, :] = product[:, inner:]


def finish_kernel(kept, info_ref, mine_ref, other_ref, *rest):
    gate_ref, up_ref, down_ref = rest[kept:]
    core = info_ref[3]
    half = mine_ref.shape[1]
    inner = mine_ref.shape[2]
    for source, place in ((mine_ref, core), (other_ref, 1 - core)):
        rows = pl.ds(pl.multiple_of(place * half, half), half)
        gate_ref[0, rows, :] = source[0].astype(F32)
        up_ref[0, rows, :] = source[1].astype(F32)
        rows = pl.ds(pl.multiple_of(place * (half // 2), half // 2), half // 2)
        down_ref[0, rows, :inner] = source[2, : half // 2].astype(F32)
        down_ref[0, rows, inner:] = source[2, half // 2 :].astype(F32)


def add(*terms):
    return sum(term.astype(F32) for term in terms).astype(terms[0].dtype)


def after(values, *others):
    anywhere = pl.BlockSpec(memory_space=pl.ANY)
    return pl.pallas_call(
        lambda *refs: None,
        out_shape=[struct(v.shape, v.dtype) for v in values],
        in_specs=[anywhere] * (len(values) + len(others)),
        out_specs=[anywhere] * len(values),
        input_output_aliases={i: i for i in range(len(values))},
        name="after",
    )(*values, *others)


def put_block(whole_array, block, *at):
    for _ in range(whole_array.ndim - block.ndim):
        block = block[None]
    return lax.dynamic_update_slice(
        whole_array, block, tuple(at) + (0,) * (whole_array.ndim - len(at))
    )


def middle_kernel(
    dx_ref,
    u_ref,
    xg_ref,
    res_ref,
    gates_ref,
    gain_two_ref,
    router_ref,
    wo_ref,
    queued_ref,
    vectors_ref,
    mixed_ref,
    gres_ref,
    gaz_ref,
):
    tokens, width = u_ref.shape
    experts = gates_ref.shape[0]
    pieces = tokens // BLOCK
    parts = []
    for part in range(experts // 8):
        sent = dx_ref[tokens:, part * tokens : (part + 1) * tokens].astype(F32)
        parts.append(sent[:8] + sent[8:])
    grad_gates = jnp.concatenate(parts, axis=0)
    gates = gates_ref[...]
    grad_logits = gates * (grad_gates - jnp.sum(gates * grad_gates, axis=0, keepdims=True))
    grad_normed = dx_ref[:tokens, :].astype(F32) + mul(
        grad_logits, router_ref[...].astype(F32), TN, EXACT
    )
    router = mul(grad_logits, xg_ref[:tokens, :].astype(F32), NN, EXACT)
    residual = res_ref[...]
    scale = lax.rsqrt(jnp.mean(residual * residual, axis=-1, keepdims=True) + EPS)
    normed = residual * scale
    second = jnp.sum(grad_normed * normed, axis=0, keepdims=True)
    spare = jnp.zeros((vectors_ref.shape[0] - experts - 1, width), F32)
    vectors_ref[...] = jnp.concatenate([router, second, spare], axis=0).astype(BF16)
    scaled = grad_normed * gain_two_ref[...]
    grad_residual = u_ref[...].astype(F32) + scale * (
        scaled - normed * jnp.mean(scaled * normed, axis=-1, keepdims=True)
    )
    gres_ref[...] = grad_residual
    grad_mixed = grad_residual.astype(BF16)
    mixed_ref[...] = grad_mixed
    for tile in range(TILES):
        grad_att = mul(grad_mixed, wo_ref[tile * 256 : (tile + 1) * 256, :], NT)
        for piece in range(pieces):
            rows = slice(piece * BLOCK, (piece + 1) * BLOCK)
            gaz_ref[piece, tile] = spread_heads(
                grad_att[rows, :LANES], grad_att[rows, LANES:]
            ).astype(BF16)


def attention_back_kernel(
    members,
    me_ref,
    qz_ref,
    gaz_ref,
    k_ref,
    v_ref,
    pos_ref,
    cos_ref,
    sin_ref,
    mix_ref,
    own_ref,
    att_ref,
    mixed_ref,
    vectors_ref,
    queued_ref,
    dq_ref,
    dkv_ref,
    weights_ref,
    dk_acc,
    dv_acc,
    row_ref,
):
    member = me_ref[0]
    tokens = own_ref.shape[0]
    pieces = tokens // BLOCK
    length = k_ref.shape[0]
    inner = k_ref.shape[1]
    dk_acc[...] = jnp.zeros_like(dk_acc)
    dv_acc[...] = jnp.zeros_like(dv_acc)
    for piece in range(pieces):
        allowed = allowed_keys(piece, members, member, pos_ref)
        keys = allowed.shape[1]
        rows = slice(piece * BLOCK, (piece + 1) * BLOCK)
        at = pl.ds(pl.multiple_of((piece * members + member) * BLOCK, BLOCK), BLOCK)

        def step(tile, carry):
            lanes = pl.ds(pl.multiple_of(tile * LANES, LANES), LANES)
            stacked, grads = qz_ref[piece, tile], gaz_ref[piece, tile]
            key_tile = k_ref[:keys, lanes]
            probs = probabilities(stacked, key_tile, allowed)
            grad_probs = mul(grads, v_ref[:keys, lanes], NT)
            delta = jnp.sum(probs * grad_probs, axis=-1, keepdims=True)
            grad_scores = (probs * (grad_probs - delta) * HEAD_DIM**-0.5).astype(BF16)
            dk_acc[:keys, lanes] += mul(grad_scores, stacked, TN)
            dv_acc[:keys, lanes] += mul(probs.astype(BF16), grads, TN)
            first, second = gather_heads(mul(grad_scores, key_tile))
            cosine, sine = cos_ref[at, :], sin_ref[at, :]
            out = pl.multiple_of(tile * 256, 256)
            dq_ref[rows, pl.ds(out, LANES)] = unrotate(first, cosine, sine).astype(BF16)
            dq_ref[rows, pl.ds(out + LANES, LANES)] = unrotate(second, cosine, sine).astype(BF16)
            return carry

        lax.fori_loop(0, TILES, step, 0)
    for block in range(length // BLOCK):
        rows = slice(block * BLOCK, (block + 1) * BLOCK)
        cosine, sine = cos_ref[rows, :], sin_ref[rows, :]
        for tile in range(TILES):
            lanes = slice(tile * LANES, (tile + 1) * LANES)
            row_ref[rows, lanes] = unrotate(dk_acc[rows, lanes], cosine, sine).astype(BF16)
        row_ref[rows, inner:] = dv_acc[rows, :].astype(BF16)
        piece, owner = block // members, block % members
        dkv_ref[owner, piece * BLOCK : (piece + 1) * BLOCK, :] = row_ref[rows, :]
    width = dq_ref.shape[1]
    for i, (left_ref, right_ref) in enumerate(
        ((own_ref, dq_ref), (mix_ref, row_ref), (att_ref, mixed_ref))
    ):
        product = mul(left_ref[...], right_ref[...], TN)
        weights_ref[i * width : (i + 1) * width, :] = product.astype(BF16)
    weights_ref[3 * width :, :] = vectors_ref[...]


def last_kernel(
    members,
    dq_ref,
    dkv_ref,
    wq_ref,
    wk_ref,
    wv_ref,
    input_ref,
    gres_ref,
    gain_one_ref,
    tied_ref,
    gh_ref,
    first_ref,
):
    inner = wk_ref.shape[1]
    grad_kv = dkv_ref[0].astype(F32)
    for other in range(1, members):
        grad_kv = grad_kv + dkv_ref[other].astype(F32)
    grad_kv = grad_kv.astype(BF16)
    grad_mixer = (
        mul(dq_ref[...], wq_ref[...], NT)
        + mul(grad_kv[:, :inner], wk_ref[...], NT)
        + mul(grad_kv[:, inner:], wv_ref[...], NT)
    )
    x = input_ref[...].astype(F32)
    scale = lax.rsqrt(jnp.mean(x * x, axis=-1, keepdims=True) + EPS)
    normed = x * scale
    first_ref[...] = jnp.broadcast_to(
        jnp.sum(grad_mixer * normed, axis=0, keepdims=True), first_ref.shape
    ).astype(first_ref.dtype)
    scaled = grad_mixer * gain_one_ref[...]
    gh_ref[...] = (
        gres_ref[...]
        + scale * (scaled - normed * jnp.mean(scaled * normed, axis=-1, keepdims=True))
    ).astype(gh_ref.dtype)


def rope_tables(places):
    middle = HEAD_DIM // 2
    frequency = jnp.exp(jnp.arange(middle, dtype=F32) * (-2.0 * math.log(THETA) / HEAD_DIM))
    angles = places.astype(F32)[:, None] * frequency
    cosine, sine = jnp.cos(angles), jnp.sin(angles)
    return (
        jnp.concatenate([cosine] * 4, axis=1),
        jnp.concatenate([-sine, sine, -sine, sine], axis=1),
    )


def local(
    hidden_in,
    segment_ids,
    positions,
    expert_ids,
    first_gain,
    query_weight,
    key_weight,
    value_weight,
    output_weight,
    second_gain,
    router_weight,
    gate_weight,
    up_weight,
    down_weight,
    out_grad,
):
    rows_here, block, width = hidden_in.shape
    tokens = rows_here * block
    shards = lax.axis_size("seq")
    members = shards // rows_here
    length = shards * block
    inner = key_weight.shape[1]
    expert_count = router_weight.shape[1]
    experts, _, hidden = gate_weight.shape
    me = lax.axis_index("seq")
    row, member = me // members, me % members
    me_pair = jnp.stack([member, me]).astype(jnp.int32)
    same_member = [[r * members + m for r in range(rows_here)] for m in range(members)]
    same_row = [[r * members + m for m in range(members)] for r in range(rows_here)]
    slots = tokens * MOST // BLOCK
    groups = shards // PAIR

    meta = jnp.concatenate(
        [positions.reshape(1, tokens), expert_ids.reshape(tokens, TOPK).T], axis=0
    )
    row_in = lax.all_to_all(jnp.repeat(hidden_in, members, axis=0), "seq", 0, 0, tiled=True)
    row_in = row_in.reshape(length, width)
    def onward(values, count):
        to = lambda j: (j // members + count) % rows_here * members + j % members
        return lax.ppermute(values, "seq", [(j, to(j)) for j in range(shards)])

    def across(values, other):
        return lax.ppermute(values, "seq", [(j, j ^ other) for j in range(shards)])

    def row_swap(values, other):
        count = lax.axis_size("rows")
        return lax.ppermute(values, "rows", [(j, j ^ other) for j in range(count)])

    def gather(values):
        found = []
        for k in range(rows_here):
            values = onward(values, 1) if k else values
            found.append([values] + [across(values, other) for other in range(1, members)])
        return found

    def joined(part):
        return add(part[0], *(across(part[o], o) for o in range(1, members)))

    def scatter(sums):
        return add(*(onward(total, rows_here - k) if k else total for k, total in enumerate(sums)))

    core = lax.axis_index("rows") % 2

    of_row = lambda k: lax.dynamic_index_in_dim(hidden_in, (row + k) % rows_here, 0, keepdims=False)
    row_in = [of_row(k) for k in range(rows_here)]
    meta = after([jnp.broadcast_to(meta[None], (shards,) + meta.shape)], *row_in)[0]
    meta = lax.all_to_all(meta, "seq", 0, 0, tiled=True)
    row_in = row_in[:1] + [onward(row_in[k], k) for k in range(1, rows_here)]
    row_in = [[v] + [across(v, other) for other in range(1, members)] for v in row_in]
    row_in = [v for blocks in row_in for v in blocks]
    places = [
        (row - k) % rows_here * members + (member ^ other)
        for k in range(rows_here)
        for other in range(members)
    ]
    me_row = jnp.stack([member, me] + places).astype(jnp.int32)
    upstream = lax.all_gather(out_grad, "seq", axis=0, tiled=False)
    upstream = upstream.reshape(rows_here, members, rows_here, block, width)

    meta = meta.reshape(rows_here, members, TOPK + 1, rows_here, block)
    row_meta = lax.dynamic_index_in_dim(meta, row, 3, keepdims=False)
    own_meta = lax.dynamic_index_in_dim(row_meta, member, 1, keepdims=False)
    cosine, sine = rope_tables(row_meta[:, :, 0].reshape(length))
    own_pos = own_meta[:, 0].reshape(tokens, 1)
    own_ids = own_meta[:, 1:].transpose(1, 0, 2).reshape(TOPK, tokens)
    lane = jnp.arange(8, dtype=jnp.int32)
    wanted = jnp.where(lane < experts, me * experts + lane, -1)
    named = jnp.any(
        meta[:, :, 1:, None] == wanted[None, None, None, :, None, None], axis=2
    )
    named = named.transpose(3, 1, 2, 0, 4).reshape(shards, 8, tokens).astype(F32)

    gain_one, gain_two = first_gain.reshape(1, width), second_gain.reshape(1, width)
    router = router_weight.T
    mix, own_mix, qz, k_row, v_row, att, residual, xg, gates, own_in = pl.pallas_call(
        functools.partial(front_kernel, members, shards),
        out_shape=[
            struct((length, width), BF16),
            struct((tokens, width), BF16),
            struct((rows_here, TILES, 4 * BLOCK, LANES), BF16),
            struct((length, inner), BF16),
            struct((length, inner), BF16),
            struct((tokens, width), BF16),
            struct((tokens, width), F32),
            struct((tokens + PAD, width), BF16),
            struct((expert_count, tokens), F32),
            struct((tokens, width), BF16),
        ],
        in_specs=[scalars()] + [whole()] * (shards + 11),
        out_specs=[whole()] * 10,
        scratch_shapes=[pltpu.VMEM((length, width), BF16)],
        compiler_params=params(56),
        cost_estimate=took(19.5),
        name="front",
    )(
        me_row,
        *row_in,
        cosine,
        sine,
        own_pos,
        own_ids,
        gain_one,
        query_weight,
        key_weight,
        value_weight,
        output_weight,
        gain_two,
        router,
    )

    constant = lambda shape: pl.BlockSpec(
        shape, lambda i: (0,) * len(shape), pipeline_mode=pl.Buffered(1)
    )
    grouped = lambda *shape: pl.BlockSpec((PAIR,) + shape, lambda i: (i,) + (0,) * len(shape))
    per_row = members // PAIR
    one_on = onward(xg, 1)
    beside = [across(xg, other) for other in range(1, members)]
    one_on = after([one_on], *beside)[0]
    sets = [[xg] + beside, [one_on] + [across(one_on, other) for other in range(1, members)]]
    two_on = onward(one_on, 1)
    slot, us, product = pl.pallas_call(
        upstream_kernel,
        grid=(groups,),
        out_shape=[
            struct((shards, 8, tokens), F32),
            struct((shards, experts * slots, width), BF16),
            struct((shards, experts * slots, hidden), F32),
        ],
        in_specs=[
            grouped(8, tokens),
            pl.BlockSpec(
                (rows_here, PAIR, 1, block, width),
                lambda i: (0, i % per_row, i // per_row, 0, 0),
            ),
            constant((experts, hidden, width)),
        ]
        + [pl.BlockSpec(memory_space=pl.ANY)],
        out_specs=[
            grouped(8, tokens),
            grouped(experts * slots, width),
            grouped(experts * slots, hidden),
        ],
        compiler_params=params(48),
        cost_estimate=took(15.5),
        name="upstream",
    )(named, upstream, down_weight, one_on)

    wide, narrow = experts * slots, hidden
    kept = []
    values = after([two_on], slot)[0]
    for k in range(2, rows_here):
        values = onward(values, 1) if k > 2 else values
        sets.append([values] + [across(values, other) for other in range(1, members)])
    order = list(range(rows_here))
    dx_parts, y_parts, dx_sums = [[] for _ in sets], [[] for _ in sets], []
    for k in order:
        group = sets[k]
        tied = []
        for later, member_of in ((k + 1, -1), (k + 2, 0)):
            tied += [sets[later][member_of]] if later < rows_here else []
        tied += dx_sums[k - 2 : k - 1] if k > 1 else []
        for q in range(members // PAIR):
            pair = (row - k) % rows_here * per_row + ((member // PAIR) ^ q)
            info = jnp.stack([member % PAIR, me, pair, core]).astype(jnp.int32)
            flat = lambda *shape: pl.BlockSpec(shape, lambda e, info: (0,) * len(shape))
            of_pair = lambda w: pl.BlockSpec((PAIR, slots, w), lambda e, info: (info[2], e, 0))
            of_expert = lambda a, b: pl.BlockSpec((1, a, b), lambda e, info: (e, 0, 0))
            outcome = pl.pallas_call(
                functools.partial(expert_kernel, len(kept) + len(tied)),
                grid_spec=pltpu.PrefetchScalarGridSpec(
                    num_scalar_prefetch=1,
                    grid=(experts,),
                    in_specs=[
                        flat(tokens + PAD, width),
                        flat(tokens + PAD, width),
                        pl.BlockSpec((PAIR, 8, tokens), lambda e, info: (info[2], 0, 0)),
                        of_pair(hidden),
                        of_expert(width, hidden),
                        of_expert(width, hidden),
                        of_expert(hidden, width),
                    ]
                    + [pl.BlockSpec(memory_space=pl.ANY)] * (len(kept) + len(tied)),
                    out_specs=[
                        flat(tokens + PAD, width),
                        flat(tokens + PAD, width),
                        flat(tokens, width),
                        flat(tokens, width),
                        of_pair(width),
                        of_pair(hidden),
                        of_pair(hidden),
                        of_pair(hidden),
                    ],
                    scratch_shapes=[
                        pltpu.VMEM((PAIR, wide, width), BF16),
                        pltpu.VMEM((PAIR, wide, width), BF16),
                        pltpu.VMEM((PAIR, wide, tokens), BF16),
                        pltpu.VMEM((8, tokens), F32),
                        pltpu.VMEM((PAIR, PAD, width), F32),
                    ],
                ),
                out_shape=[
                    struct((tokens + PAD, width), BF16),
                    struct((tokens + PAD, width), BF16),
                    struct((tokens, width), BF16),
                    struct((tokens, width), BF16),
                    struct((shards, wide, width), BF16),
                    struct((shards, wide, hidden), BF16),
                    struct((shards, wide, hidden), BF16),
                    struct((shards, wide, hidden), BF16),
                ],
                input_output_aliases={8 + i: 4 + i for i in range(len(kept))},
                compiler_params=params(40),
                cost_estimate=took(13.3),
                name="experts",
            )(info, group[2 * q], group[2 * q + 1], slot, product, gate_weight, up_weight, down_weight, *kept, *tied)
            dx_parts[k] += outcome[:2]
            y_parts[k] += outcome[2:4]
            kept = outcome[4:]
        dx_sums.append(joined(dx_parts[k]))
    sent = [dx_sums[0]] + [onward(dx_sums[k], rows_here - k) for k in range(1, rows_here)]
    dx_sum = add(*sent)

    info = jnp.stack([member % PAIR, me, me, core]).astype(jnp.int32)
    halves = (3, width // 2, hidden)
    mine, keep = [], us
    for first, count in ((0, 1), (1, experts - 1)):
        if not count:
            continue
        one_expert = lambda w: pl.BlockSpec((shards, slots, w), lambda i, at=first: (0, at + i, 0))
        half = pl.BlockSpec((1,) + halves, lambda i: (i, 0, 0, 0))
        keep, send = pl.pallas_call(
            expert_grads_kernel,
            grid=(count,),
            out_shape=[struct((count,) + halves, BF16)] * 2,
            in_specs=[scalars(), one_expert(width), one_expert(width)]
            + [one_expert(hidden)] * 3
            + [pl.BlockSpec(memory_space=pl.ANY)] * 3,
            out_specs=[half] * 2,
            compiler_params=params(60),
            cost_estimate=took(4.6 * count + 1.5),
            name="expert_grads",
        )(info, kept[0], us, *kept[1:], keep, dx_sums[2 if first == 0 else 3], sent[1 if first == 0 else 2])
        received = row_swap(send, 1)
        mine += [add(keep[i], received[i]) for i in range(count)]
    queued = mine[-1]
    crossed = []
    for e in range(experts):
        bit = 2
        while bit < lax.axis_size("rows"):
            crossed.append(row_swap(mine[e], bit))
            mine[e] = add(mine[e], crossed[-1])
            bit *= 2
    finished = []
    for e in range(experts):
        grad_spec = lambda a, b: pl.BlockSpec((1, a, b), lambda i, e=e: (e, 0, 0))
        half = pl.BlockSpec(halves, lambda i: (0, 0, 0))
        finished = pl.pallas_call(
            functools.partial(finish_kernel, len(finished)),
            grid=(1,),
            out_shape=[
                struct((experts, width, hidden), F32),
                struct((experts, width, hidden), F32),
                struct((experts, hidden, width), F32),
            ],
            in_specs=[scalars(), half, half]
            + [pl.BlockSpec(memory_space=pl.ANY)] * len(finished),
            out_specs=[grad_spec(width, hidden), grad_spec(width, hidden), grad_spec(hidden, width)],
            input_output_aliases={3 + i: i for i in range(len(finished))},
            compiler_params=params(32),
            cost_estimate=took(4.6),
            name="finish",
        )(info, mine[e], row_swap(mine[e], 1), *finished)
    later = after([y for part in y_parts for y in part[1:]], dx_sum)
    later = [later[k * (members - 1) : (k + 1) * (members - 1)] for k in range(rows_here)]
    own_upstream = lax.dynamic_index_in_dim(upstream, row, 2, keepdims=False)
    own_upstream = lax.dynamic_index_in_dim(own_upstream, member, 1, keepdims=False)
    own_upstream = own_upstream.reshape(tokens, width)
    vectors, grad_mixed, grad_residual, gaz = pl.pallas_call(
        middle_kernel,
        out_shape=[
            struct((EXTRA, width), BF16),
            struct((tokens, width), BF16),
            struct((tokens, width), F32),
            struct((rows_here, TILES, 4 * BLOCK, LANES), BF16),
        ],
        in_specs=[whole()] * 8 + [pl.BlockSpec(memory_space=pl.ANY)],
        out_specs=[whole()] * 4,
        compiler_params=params(48),
        cost_estimate=took(6),
        name="middle",
    )(dx_sum, own_upstream, xg, residual, gates, gain_two, router, output_weight, dx_sums[0])

    dq, dkv, weights = pl.pallas_call(
        functools.partial(attention_back_kernel, members),
        out_shape=[
            struct((tokens, width), BF16),
            struct((members, tokens, width), BF16),
            struct((3 * width + EXTRA, width), BF16),
        ],
        in_specs=[scalars()] + [whole()] * 12 + [pl.BlockSpec(memory_space=pl.ANY)],
        out_specs=[whole()] * 3,
        scratch_shapes=[
            pltpu.VMEM((length, inner), F32),
            pltpu.VMEM((length, inner), F32),
            pltpu.VMEM((length, width), BF16),
        ],
        compiler_params=params(58),
        cost_estimate=took(21.5),
        name="attention_back",
    )(me_pair, qz, gaz, k_row, v_row, own_pos, cosine, sine, mix, own_mix, att, grad_mixed, vectors, vectors)
    dkv = lax.all_to_all(dkv, "seq", 0, 0, tiled=True, axis_index_groups=same_row)
    grad_in, first_part = pl.pallas_call(
        functools.partial(last_kernel, members),
        out_shape=[struct((tokens, width), BF16), struct((8, width), F32)],
        in_specs=[whole()] * 8 + [pl.BlockSpec(memory_space=pl.ANY)],
        out_specs=[whole()] * 2,
        compiler_params=params(48),
        cost_estimate=took(3.1),
        name="last",
    )(dq, dkv, query_weight, key_weight, value_weight, own_in, grad_residual, gain_one, crossed[0])

    steps = [crossed[min(i, experts - 1)] for i in range(4)]
    first_sum, bit = after([first_part], steps[2])[0], 1
    while bit < shards:
        first_sum = first_sum + across(first_sum, bit)
        bit *= 2
    bit = 1
    while bit < lax.axis_size("rows"):
        first_sum = first_sum + row_swap(first_sum, bit)
        bit *= 2
    y_sum = scatter(
        [joined([y, *rest]) for y, rest in zip(after([p[0] for p in y_parts], dq), later)]
    )
    steps = [crossed[min(i, experts - 1)] for i in range(4)]
    hidden_out = after([(residual + y_sum.astype(F32)).astype(BF16)], steps[1])[0]
    back = lambda values: lax.all_to_all(
        values.reshape(rows_here, block, width), "seq", 0, 0, tiled=True, axis_index_groups=same_member
    )
    hidden_out, grad_in = back(hidden_out), back(grad_in)
    shared = lax.psum(weights, ("rows", "seq"))
    shared = after([shared], hidden_out, grad_in, first_sum, finished[0])[0]
    query_sum, keyval_sum, output_sum, vector_sum = (
        shared[i * width : (i + 1) * width].astype(F32) for i in range(4)
    )
    return (
        hidden_out,
        grad_in.astype(F32),
        first_sum[0],
        query_sum,
        keyval_sum[:, :inner],
        keyval_sum[:, inner:],
        output_sum,
        vector_sum[expert_count],
        vector_sum[:expert_count].T,
        *finished,
    )


def solution(mesh):
    placed = (
        P("rows", "seq", None),
        P("rows", "seq"),
        P("rows", "seq"),
        P("rows", "seq", None),
        P(),
        P(),
        P(),
        P(),
        P(),
        P(),
        P(),
        P("seq", None, None),
        P("seq", None, None),
        P("seq", None, None),
        P("rows", "seq", None),
    )
    return jax.shard_map(
        local,
        mesh=mesh,
        in_specs=placed,
        out_specs=(
            P("rows", "seq", None),
            P("rows", "seq", None),
            P(),
            P(),
            P(),
            P(),
            P(),
            P(),
            P(),
            P("seq", None, None),
            P("seq", None, None),
            P("seq", None, None),
        ),
        check_vma=False,
    )
```

```python
import functools
import math

import jax
import jax.numpy as jnp
from jax import lax
from jax.experimental import pallas as pl
from jax.experimental.pallas import tpu as pltpu
from jax.sharding import PartitionSpec as P

HEADS = 16
KV_HEADS = 8
HEAD_DIM = 64
TOPK = 8
MOST = 32
BLOCK = 64
LANES = 128
TILES = KV_HEADS * HEAD_DIM // LANES
EXTRA = 128
PAIR = 2
PAD = 16

EPS = 1e-06
THETA = 10000.0
NEG = -1e30
F32 = jnp.float32
BF16 = jnp.bfloat16
EXACT = lax.Precision.HIGHEST
NN = (((1,), (0,)), ((), ()))
NT = (((1,), (1,)), ((), ()))
TN = (((0,), (0,)), ((), ()))


def mul(left, right, dims=NN, precision=None):
    return lax.dot_general(left, right, dims, precision=precision, preferred_element_type=F32)


def params(megabytes):
    return pltpu.CompilerParams(vmem_limit_bytes=megabytes << 20)


def whole():
    return pl.BlockSpec(memory_space=pltpu.VMEM)


def scalars():
    return pl.BlockSpec(memory_space=pltpu.SMEM)


def struct(shape, dtype):
    return jax.ShapeDtypeStruct(shape, dtype)


def took(microseconds):
    return pl.CostEstimate(flops=int(microseconds * 0.5e9), bytes_accessed=0, transcendentals=0)


def low_half(shape):
    return lax.broadcasted_iota(jnp.int32, shape, 1) < HEAD_DIM


def swap_halves(tile):
    lane = lax.broadcasted_iota(jnp.int32, tile.shape, 1)
    quarter = HEAD_DIM // 2
    forward = pltpu.roll(tile, LANES - quarter, 1)
    backward = pltpu.roll(tile, quarter, 1)
    return jnp.where(lane % HEAD_DIM < quarter, forward, backward)


def rotate(tile, cosine, signed_sine):
    return tile * cosine + swap_halves(tile) * signed_sine


def unrotate(tile, cosine, signed_sine):
    return tile * cosine - swap_halves(tile) * signed_sine


def spread_heads(first, second):
    low = low_half(first.shape)
    return jnp.concatenate(
        [
            jnp.where(low, first, 0.0),
            jnp.where(low, pltpu.roll(first, HEAD_DIM, 1), 0.0),
            jnp.where(low, 0.0, pltpu.roll(second, HEAD_DIM, 1)),
            jnp.where(low, 0.0, second),
        ],
        axis=0,
    )


def gather_heads(stacked):
    low = low_half((BLOCK, LANES))
    one, two, three, four = (stacked[i * BLOCK : (i + 1) * BLOCK] for i in range(4))
    first = jnp.where(low, one, pltpu.roll(two, HEAD_DIM, 1))
    second = jnp.where(low, pltpu.roll(three, HEAD_DIM, 1), four)
    return first, second


def allowed_keys(piece, members, member, pos_ref):
    keys = (piece + 1) * members * BLOCK
    start = (piece * members + member) * BLOCK
    place = start + lax.broadcasted_iota(jnp.int32, (BLOCK, keys), 0)
    key = lax.broadcasted_iota(jnp.int32, (BLOCK, keys), 1)
    opening = place - pos_ref[piece * BLOCK : (piece + 1) * BLOCK, :]
    return (key <= place) & (key >= opening)


def probabilities(stacked, key_tile, allowed):
    keys = key_tile.shape[0]
    scores = mul(stacked, key_tile, NT) * HEAD_DIM**-0.5
    scores = scores.reshape(4, BLOCK, keys)
    scores = jnp.where(allowed[None], scores, NEG)
    weights = jnp.exp(scores - jnp.max(scores, axis=-1, keepdims=True))
    probs = weights * (1.0 / jnp.sum(weights, axis=-1, keepdims=True))
    return probs.reshape(4 * BLOCK, keys)


def two_parts(values):
    high = values.astype(BF16).astype(F32)
    return jnp.concatenate([high, values - high], axis=0).astype(BF16)


def front_kernel(
    members,
    blocks,
    me_ref,
    *refs,
):
    front_body(members, me_ref, refs[:blocks], *refs[blocks:])


def front_body(
    members,
    me_ref,
    block_refs,
    cos_ref,
    sin_ref,
    pos_ref,
    ids_ref,
    gain_one_ref,
    wq_ref,
    wk_ref,
    wv_ref,
    wo_ref,
    gain_two_ref,
    router_ref,
    mix_ref,
    own_ref,
    qz_ref,
    k_ref,
    v_ref,
    att_ref,
    res_ref,
    xg_ref,
    gates_ref,
    input_ref,
    h_ref,
):
    member = me_ref[0]
    length, width = h_ref.shape
    tokens = own_ref.shape[0]
    pieces = tokens // BLOCK
    step = 256
    for i, block_ref in enumerate(block_refs):
        h_ref[pl.ds(pl.multiple_of(me_ref[2 + i] * BLOCK, BLOCK), BLOCK), :] = block_ref[...]

    def keys_step(i, carry):
        rows = pl.ds(pl.multiple_of(i * step, step), step)
        x = h_ref[rows, :].astype(F32)
        scale = lax.rsqrt(jnp.mean(x * x, axis=-1, keepdims=True) + EPS)
        mix = (x * scale * gain_one_ref[...]).astype(BF16)
        mix_ref[rows, :] = mix
        v_ref[rows, :] = mul(mix, wv_ref[...]).astype(BF16)
        pre = mul(mix, wk_ref[...])
        cosine, sine = cos_ref[rows, :], sin_ref[rows, :]
        for tile in range(TILES):
            lanes = slice(tile * LANES, (tile + 1) * LANES)
            k_ref[rows, lanes] = rotate(pre[:, lanes], cosine, sine).astype(BF16)
        return carry

    lax.fori_loop(0, length // step, keys_step, 0)
    own = [pl.ds(pl.multiple_of((p * members + member) * BLOCK, BLOCK), BLOCK) for p in range(pieces)]
    for piece in range(pieces):
        rows = slice(piece * BLOCK, (piece + 1) * BLOCK)
        own_ref[rows, :] = mix_ref[own[piece], :]
        input_ref[rows, :] = h_ref[own[piece], :]

    def query_step(tile, carry):
        pre = mul(own_ref[...], wq_ref[:, pl.ds(pl.multiple_of(tile * 256, 256), 256)])
        for piece in range(pieces):
            rows = slice(piece * BLOCK, (piece + 1) * BLOCK)
            cosine, sine = cos_ref[own[piece], :], sin_ref[own[piece], :]
            first = rotate(pre[rows, :LANES], cosine, sine)
            second = rotate(pre[rows, LANES:], cosine, sine)
            qz_ref[piece, tile] = spread_heads(first, second).astype(BF16)
        return carry

    lax.fori_loop(0, TILES, query_step, 0)
    for piece in range(pieces):
        allowed = allowed_keys(piece, members, member, pos_ref)
        keys = allowed.shape[1]
        rows = slice(piece * BLOCK, (piece + 1) * BLOCK)

        def attend(tile, carry):
            lanes = pl.ds(pl.multiple_of(tile * LANES, LANES), LANES)
            probs = probabilities(qz_ref[piece, tile], k_ref[:keys, lanes], allowed)
            first, second = gather_heads(mul(probs.astype(BF16), v_ref[:keys, lanes]))
            at = pl.multiple_of(tile * 256, 256)
            att_ref[rows, pl.ds(at, LANES)] = first.astype(BF16)
            att_ref[rows, pl.ds(at + LANES, LANES)] = second.astype(BF16)
            return carry

        lax.fori_loop(0, TILES, attend, 0)
    mixed = mul(att_ref[...], wo_ref[...])
    residual = input_ref[...].astype(F32) + mixed
    res_ref[...] = residual
    scale = lax.rsqrt(jnp.mean(residual * residual, axis=-1, keepdims=True) + EPS)
    chosen = (residual * scale * gain_two_ref[...]).astype(BF16)
    xg_ref[:tokens, :] = chosen
    logits = mul(router_ref[...], chosen, NT)
    expert = lax.broadcasted_iota(jnp.int32, logits.shape, 0)
    named = expert == ids_ref[0:1, :]
    for k in range(1, TOPK):
        named = named | (expert == ids_ref[k : k + 1, :])
    logits = jnp.where(named, logits, NEG)
    weights = jnp.where(named, jnp.exp(logits - jnp.max(logits, axis=0, keepdims=True)), 0.0)
    gates = weights / jnp.sum(weights, axis=0, keepdims=True)
    gates_ref[...] = gates
    for part in range(logits.shape[0] // 8):
        lanes = slice(part * tokens, (part + 1) * tokens)
        xg_ref[tokens:, lanes] = two_parts(gates[part * 8 : (part + 1) * 8])


def one_hot(slot_row, rows):
    slot = lax.broadcasted_iota(jnp.int32, (rows, slot_row.shape[1]), 0).astype(F32)
    return slot == slot_row


def expert_kernel(
    kept,
    info_ref,
    xa_ref,
    xb_ref,
    named_ref,
    u_ref,
    wg_ref,
    wu_ref,
    wd_ref,
    *rest,
):
    (dxa_ref, dxb_ref) = rest[kept : kept + 2]
    (y_ref, xs_ref, us_ref, hs_ref, dg_ref, du_ref) = rest[kept + 2 : kept + 8]
    (dxs_ref, ys_ref, pick_ref, slot_ref, gates_ref, back_ref) = rest[kept + 8 :]
    e = pl.program_id(0)
    experts = pl.num_programs(0)
    tokens = named_ref.shape[2]
    width = xa_ref.shape[1]
    rows = tokens * MOST // BLOCK
    places = [(info_ref[0] + c) % PAIR for c in range(PAIR)]
    sources = (xa_ref, xb_ref)

    @pl.when(e == 0)
    def _():
        back_ref[...] = jnp.zeros_like(back_ref)
        earlier = lax.broadcasted_iota(jnp.int32, (tokens, tokens), 0)
        later = lax.broadcasted_iota(jnp.int32, (tokens, tokens), 1)
        before = (earlier < later).astype(F32).astype(BF16)
        for c in range(PAIR):
            named = named_ref[places[c]]
            slot_ref[c] = jnp.where(named > 0, mul(named.astype(BF16), before), -1.0)

    at = pl.ds(pl.multiple_of(e * rows, rows), rows)
    number = info_ref[1] * experts + e
    row = lax.rem(number, 8)
    lanes = pl.ds(pl.multiple_of(lax.div(number, 8) * tokens, tokens), tokens)
    entering, leaving, gate = [], [], []
    for c in range(PAIR):
        hot = one_hot(slot_ref[c, pl.ds(e, 1), :], rows)
        pick = hot.astype(F32).astype(BF16)
        pick_ref[c, at, :] = pick
        picked = mul(pick, sources[c][:tokens, :]).astype(BF16)
        xs_ref[places[c]] = picked
        entering.append(picked)
        picked = mul(pick, u_ref[:, places[c], 0].reshape(tokens, width)).astype(BF16)
        us_ref[places[c]] = picked
        leaving.append(picked)
        sent = sources[c][tokens:, lanes].astype(F32)
        gates_ref[...] = sent[:8] + sent[8:]
        gate.append(jnp.sum(jnp.where(hot, gates_ref[pl.ds(row, 1), :], 0.0), axis=1, keepdims=True))
    entering = jnp.concatenate(entering, axis=0)
    gate = jnp.concatenate(gate, axis=0)
    gate_pre = mul(entering, wg_ref[0])
    up_pre = mul(entering, wu_ref[0])
    product = mul(jnp.concatenate(leaving, axis=0), wd_ref[0], NT)
    share = 1.0 / (1.0 + jnp.exp(-gate_pre))
    silu = gate_pre * share
    hidden = silu * up_pre
    grad_gate = jnp.sum(hidden * product, axis=1, keepdims=True)
    grad_act = gate * product
    grad_gate_pre = (grad_act * up_pre * share * (1.0 + gate_pre * (1.0 - share))).astype(BF16)
    grad_up_pre = (grad_act * silu).astype(BF16)
    gated = (gate * hidden).astype(BF16)
    grad_rows = (mul(grad_gate_pre, wg_ref[0], NT) + mul(grad_up_pre, wu_ref[0], NT)).astype(BF16)
    out_rows = mul(gated, wd_ref[0]).astype(BF16)
    for c in range(PAIR):
        part = slice(c * rows, (c + 1) * rows)
        hs_ref[places[c]] = gated[part]
        dg_ref[places[c]] = grad_gate_pre[part]
        du_ref[places[c]] = grad_up_pre[part]
        dxs_ref[c, at, :] = grad_rows[part]
        ys_ref[c, at, :] = out_rows[part]
        hot = one_hot(slot_ref[c, pl.ds(e, 1), :], rows)
        returned = jnp.sum(jnp.where(hot, grad_gate[part], 0.0), axis=0, keepdims=True)
        high = returned.astype(BF16).astype(F32)
        back_ref[c, pl.ds(row, 1), lanes] = high
        back_ref[c, pl.ds(row + 8, 1), lanes] = returned - high

    @pl.when(e == experts - 1)
    def _():
        for c, dx_ref in enumerate((dxa_ref, dxb_ref)):
            dx_ref[:tokens, :] = mul(pick_ref[c], dxs_ref[c], TN).astype(BF16)
            dx_ref[tokens:, :] = back_ref[c].astype(BF16)
            y_ref[places[c]] = mul(pick_ref[c], ys_ref[c], TN).astype(BF16)


def expert_grads_kernel(info_ref, xs_ref, us_ref, hs_ref, dg_ref, du_ref, *rest):
    keep_ref, send_ref = rest[-2:]
    core = info_ref[3]
    group, rows, width = xs_ref.shape
    inner = hs_ref.shape[2]
    flat = lambda ref: ref[...].reshape(group * rows, ref.shape[2])

    for half, out_ref in ((core, keep_ref), (1 - core, send_ref)):
        step = min(256, width // 2)
        for at in range(0, width // 2, step):
            lanes = pl.ds(pl.multiple_of(half * (width // 2) + at, LANES), step)
            entering = xs_ref[:, :, lanes].reshape(group * rows, step)
            out_ref[0, 0, at : at + step, :] = mul(entering, flat(dg_ref), TN).astype(BF16)
            out_ref[0, 1, at : at + step, :] = mul(entering, flat(du_ref), TN).astype(BF16)
        step = inner // 2
        lanes = pl.ds(pl.multiple_of(half * step, LANES), step)
        gated = hs_ref[:, :, lanes].reshape(group * rows, step)
        product = mul(gated, flat(us_ref), TN).astype(BF16)
        out_ref[0, 2, :step, :] = product[:, :inner]
        out_ref[0, 2, step:, :] = product[:, inner:]


def finish_kernel(kept, info_ref, mine_ref, other_ref, *rest):
    gate_ref, up_ref, down_ref = rest[kept:]
    core = info_ref[3]
    half = mine_ref.shape[1]
    inner = mine_ref.shape[2]
    for source, place in ((mine_ref, core), (other_ref, 1 - core)):
        rows = pl.ds(pl.multiple_of(place * half, half), half)
        gate_ref[0, rows, :] = source[0].astype(F32)
        up_ref[0, rows, :] = source[1].astype(F32)
        rows = pl.ds(pl.multiple_of(place * (half // 2), half // 2), half // 2)
        down_ref[0, rows, :inner] = source[2, : half // 2].astype(F32)
        down_ref[0, rows, inner:] = source[2, half // 2 :].astype(F32)


def add(*terms):
    return sum(term.astype(F32) for term in terms).astype(terms[0].dtype)


def after(values, *others):
    anywhere = pl.BlockSpec(memory_space=pl.ANY)
    return pl.pallas_call(
        lambda *refs: None,
        out_shape=[struct(v.shape, v.dtype) for v in values],
        in_specs=[anywhere] * (len(values) + len(others)),
        out_specs=[anywhere] * len(values),
        input_output_aliases={i: i for i in range(len(values))},
        name="after",
    )(*values, *others)


def put_block(whole_array, block, *at):
    for _ in range(whole_array.ndim - block.ndim):
        block = block[None]
    return lax.dynamic_update_slice(
        whole_array, block, tuple(at) + (0,) * (whole_array.ndim - len(at))
    )


def middle_kernel(
    dx_ref,
    u_ref,
    xg_ref,
    res_ref,
    gates_ref,
    gain_two_ref,
    router_ref,
    wo_ref,
    queued_ref,
    vectors_ref,
    mixed_ref,
    gres_ref,
    gaz_ref,
):
    tokens, width = u_ref.shape
    experts = gates_ref.shape[0]
    pieces = tokens // BLOCK
    parts = []
    for part in range(experts // 8):
        sent = dx_ref[tokens:, part * tokens : (part + 1) * tokens].astype(F32)
        parts.append(sent[:8] + sent[8:])
    grad_gates = jnp.concatenate(parts, axis=0)
    gates = gates_ref[...]
    grad_logits = gates * (grad_gates - jnp.sum(gates * grad_gates, axis=0, keepdims=True))
    grad_normed = dx_ref[:tokens, :].astype(F32) + mul(
        grad_logits, router_ref[...].astype(F32), TN, EXACT
    )
    router = mul(grad_logits, xg_ref[:tokens, :].astype(F32), NN, EXACT)
    residual = res_ref[...]
    scale = lax.rsqrt(jnp.mean(residual * residual, axis=-1, keepdims=True) + EPS)
    normed = residual * scale
    second = jnp.sum(grad_normed * normed, axis=0, keepdims=True)
    spare = jnp.zeros((vectors_ref.shape[0] - experts - 1, width), F32)
    vectors_ref[...] = jnp.concatenate([router, second, spare], axis=0).astype(BF16)
    scaled = grad_normed * gain_two_ref[...]
    grad_residual = u_ref[...].astype(F32) + scale * (
        scaled - normed * jnp.mean(scaled * normed, axis=-1, keepdims=True)
    )
    gres_ref[...] = grad_residual
    grad_mixed = grad_residual.astype(BF16)
    mixed_ref[...] = grad_mixed
    for tile in range(TILES):
        grad_att = mul(grad_mixed, wo_ref[tile * 256 : (tile + 1) * 256, :], NT)
        for piece in range(pieces):
            rows = slice(piece * BLOCK, (piece + 1) * BLOCK)
            gaz_ref[piece, tile] = spread_heads(
                grad_att[rows, :LANES], grad_att[rows, LANES:]
            ).astype(BF16)


def attention_back_kernel(
    members,
    me_ref,
    qz_ref,
    gaz_ref,
    k_ref,
    v_ref,
    pos_ref,
    cos_ref,
    sin_ref,
    mix_ref,
    own_ref,
    att_ref,
    mixed_ref,
    vectors_ref,
    queued_ref,
    dq_ref,
    dkv_ref,
    weights_ref,
    dk_acc,
    dv_acc,
    row_ref,
):
    member = me_ref[0]
    tokens = own_ref.shape[0]
    pieces = tokens // BLOCK
    length = k_ref.shape[0]
    inner = k_ref.shape[1]
    dk_acc[...] = jnp.zeros_like(dk_acc)
    dv_acc[...] = jnp.zeros_like(dv_acc)
    for piece in range(pieces):
        allowed = allowed_keys(piece, members, member, pos_ref)
        keys = allowed.shape[1]
        rows = slice(piece * BLOCK, (piece + 1) * BLOCK)
        at = pl.ds(pl.multiple_of((piece * members + member) * BLOCK, BLOCK), BLOCK)

        def step(tile, carry):
            lanes = pl.ds(pl.multiple_of(tile * LANES, LANES), LANES)
            stacked, grads = qz_ref[piece, tile], gaz_ref[piece, tile]
            key_tile = k_ref[:keys, lanes]
            probs = probabilities(stacked, key_tile, allowed)
            grad_probs = mul(grads, v_ref[:keys, lanes], NT)
            delta = jnp.sum(probs * grad_probs, axis=-1, keepdims=True)
            grad_scores = (probs * (grad_probs - delta) * HEAD_DIM**-0.5).astype(BF16)
            dk_acc[:keys, lanes] += mul(grad_scores, stacked, TN)
            dv_acc[:keys, lanes] += mul(probs.astype(BF16), grads, TN)
            first, second = gather_heads(mul(grad_scores, key_tile))
            cosine, sine = cos_ref[at, :], sin_ref[at, :]
            out = pl.multiple_of(tile * 256, 256)
            dq_ref[rows, pl.ds(out, LANES)] = unrotate(first, cosine, sine).astype(BF16)
            dq_ref[rows, pl.ds(out + LANES, LANES)] = unrotate(second, cosine, sine).astype(BF16)
            return carry

        lax.fori_loop(0, TILES, step, 0)
    for block in range(length // BLOCK):
        rows = slice(block * BLOCK, (block + 1) * BLOCK)
        cosine, sine = cos_ref[rows, :], sin_ref[rows, :]
        for tile in range(TILES):
            lanes = slice(tile * LANES, (tile + 1) * LANES)
            row_ref[rows, lanes] = unrotate(dk_acc[rows, lanes], cosine, sine).astype(BF16)
        row_ref[rows, inner:] = dv_acc[rows, :].astype(BF16)
        piece, owner = block // members, block % members
        dkv_ref[owner, piece * BLOCK : (piece + 1) * BLOCK, :] = row_ref[rows, :]
    width = dq_ref.shape[1]
    for i, (left_ref, right_ref) in enumerate(
        ((own_ref, dq_ref), (mix_ref, row_ref), (att_ref, mixed_ref))
    ):
        product = mul(left_ref[...], right_ref[...], TN)
        weights_ref[i * width : (i + 1) * width, :] = product.astype(BF16)
    weights_ref[3 * width :, :] = vectors_ref[...]


def last_kernel(
    members,
    dq_ref,
    dkv_ref,
    wq_ref,
    wk_ref,
    wv_ref,
    input_ref,
    gres_ref,
    gain_one_ref,
    tied_ref,
    gh_ref,
    first_ref,
):
    inner = wk_ref.shape[1]
    grad_kv = dkv_ref[0].astype(F32)
    for other in range(1, members):
        grad_kv = grad_kv + dkv_ref[other].astype(F32)
    grad_kv = grad_kv.astype(BF16)
    grad_mixer = (
        mul(dq_ref[...], wq_ref[...], NT)
        + mul(grad_kv[:, :inner], wk_ref[...], NT)
        + mul(grad_kv[:, inner:], wv_ref[...], NT)
    )
    x = input_ref[...].astype(F32)
    scale = lax.rsqrt(jnp.mean(x * x, axis=-1, keepdims=True) + EPS)
    normed = x * scale
    first_ref[...] = jnp.broadcast_to(
        jnp.sum(grad_mixer * normed, axis=0, keepdims=True), first_ref.shape
    ).astype(first_ref.dtype)
    scaled = grad_mixer * gain_one_ref[...]
    gh_ref[...] = (
        gres_ref[...]
        + scale * (scaled - normed * jnp.mean(scaled * normed, axis=-1, keepdims=True))
    ).astype(gh_ref.dtype)


def rope_tables(places):
    middle = HEAD_DIM // 2
    frequency = jnp.exp(jnp.arange(middle, dtype=F32) * (-2.0 * math.log(THETA) / HEAD_DIM))
    angles = places.astype(F32)[:, None] * frequency
    cosine, sine = jnp.cos(angles), jnp.sin(angles)
    return (
        jnp.concatenate([cosine] * 4, axis=1),
        jnp.concatenate([-sine, sine, -sine, sine], axis=1),
    )


def local(
    hidden_in,
    segment_ids,
    positions,
    expert_ids,
    first_gain,
    query_weight,
    key_weight,
    value_weight,
    output_weight,
    second_gain,
    router_weight,
    gate_weight,
    up_weight,
    down_weight,
    out_grad,
):
    rows_here, block, width = hidden_in.shape
    tokens = rows_here * block
    shards = lax.axis_size("seq")
    members = shards // rows_here
    length = shards * block
    inner = key_weight.shape[1]
    expert_count = router_weight.shape[1]
    experts, _, hidden = gate_weight.shape
    me = lax.axis_index("seq")
    row, member = me // members, me % members
    me_pair = jnp.stack([member, me]).astype(jnp.int32)
    same_member = [[r * members + m for r in range(rows_here)] for m in range(members)]
    same_row = [[r * members + m for m in range(members)] for r in range(rows_here)]
    slots = tokens * MOST // BLOCK

    meta = jnp.concatenate(
        [positions.reshape(1, tokens), expert_ids.reshape(tokens, TOPK).T], axis=0
    )
    row_in = lax.all_to_all(jnp.repeat(hidden_in, members, axis=0), "seq", 0, 0, tiled=True)
    row_in = row_in.reshape(length, width)
    def onward(values, count):
        to = lambda j: (j // members + count) % rows_here * members + j % members
        return lax.ppermute(values, "seq", [(j, to(j)) for j in range(shards)])

    def across(values, other):
        return lax.ppermute(values, "seq", [(j, j ^ other) for j in range(shards)])

    def row_swap(values, other):
        count = lax.axis_size("rows")
        return lax.ppermute(values, "rows", [(j, j ^ other) for j in range(count)])

    def gather(values):
        found = []
        for k in range(rows_here):
            values = onward(values, 1) if k else values
            found.append([values] + [across(values, other) for other in range(1, members)])
        return found

    def joined(part):
        return add(part[0], *(across(part[o], o) for o in range(1, members)))

    def scatter(sums):
        return add(*(onward(total, rows_here - k) if k else total for k, total in enumerate(sums)))

    core = lax.axis_index("rows") % 2

    of_row = lambda k: lax.dynamic_index_in_dim(hidden_in, (row + k) % rows_here, 0, keepdims=False)
    row_in = [of_row(k) for k in range(rows_here)]
    meta = after([jnp.broadcast_to(meta[None], (shards,) + meta.shape)], *row_in)[0]
    meta = lax.all_to_all(meta, "seq", 0, 0, tiled=True)
    row_in = row_in[:1] + [onward(row_in[k], k) for k in range(1, rows_here)]
    row_in = [[v] + [across(v, other) for other in range(1, members)] for v in row_in]
    row_in = [v for blocks in row_in for v in blocks]
    places = [
        (row - k) % rows_here * members + (member ^ other)
        for k in range(rows_here)
        for other in range(members)
    ]
    me_row = jnp.stack([member, me] + places).astype(jnp.int32)
    upstream = lax.all_gather(out_grad, "seq", axis=0, tiled=False)
    upstream = upstream.reshape(rows_here, members, rows_here, block, width)
    stored = [
        pltpu.with_memory_space_constraint(v, pltpu.HBM)
        for v in (upstream, gate_weight, up_weight, down_weight)
    ]

    meta = meta.reshape(rows_here, members, TOPK + 1, rows_here, block)
    row_meta = lax.dynamic_index_in_dim(meta, row, 3, keepdims=False)
    own_meta = lax.dynamic_index_in_dim(row_meta, member, 1, keepdims=False)
    cosine, sine = rope_tables(row_meta[:, :, 0].reshape(length))
    own_pos = own_meta[:, 0].reshape(tokens, 1)
    own_ids = own_meta[:, 1:].transpose(1, 0, 2).reshape(TOPK, tokens)
    lane = jnp.arange(8, dtype=jnp.int32)
    wanted = jnp.where(lane < experts, me * experts + lane, -1)
    named = jnp.any(
        meta[:, :, 1:, None] == wanted[None, None, None, :, None, None], axis=2
    )
    named = named.transpose(3, 1, 2, 0, 4).reshape(shards, 8, tokens).astype(F32)

    gain_one, gain_two = first_gain.reshape(1, width), second_gain.reshape(1, width)
    router = router_weight.T
    mix, own_mix, qz, k_row, v_row, att, residual, xg, gates, own_in = pl.pallas_call(
        functools.partial(front_kernel, members, shards),
        out_shape=[
            struct((length, width), BF16),
            struct((tokens, width), BF16),
            struct((rows_here, TILES, 4 * BLOCK, LANES), BF16),
            struct((length, inner), BF16),
            struct((length, inner), BF16),
            struct((tokens, width), BF16),
            struct((tokens, width), F32),
            struct((tokens + PAD, width), BF16),
            struct((expert_count, tokens), F32),
            struct((tokens, width), BF16),
        ],
        in_specs=[scalars()] + [whole()] * (shards + 11),
        out_specs=[whole()] * 10,
        scratch_shapes=[pltpu.VMEM((length, width), BF16)],
        compiler_params=params(56),
        cost_estimate=took(19.5),
        name="front",
    )(
        me_row,
        *row_in,
        cosine,
        sine,
        own_pos,
        own_ids,
        gain_one,
        query_weight,
        key_weight,
        value_weight,
        output_weight,
        gain_two,
        router,
    )

    per_row = members // PAIR
    one_on = onward(xg, 1)
    beside = [across(xg, other) for other in range(1, members)]
    one_on = after([one_on], *beside)[0]
    sets = [[xg] + beside, [one_on] + [across(one_on, other) for other in range(1, members)]]
    two_on = onward(one_on, 1)
    wide, narrow = experts * slots, hidden
    kept = []
    order = list(range(rows_here))
    dx_parts, dx_sums = [[] for _ in order], []
    for k in order:
        if k == 1:
            values = after([two_on], dx_parts[0][0])[0]
            for i in range(2, rows_here):
                values = onward(values, 1) if i > 2 else values
                sets.append([values] + [across(values, other) for other in range(1, members)])
        group = sets[k]
        tied = dx_sums[k - 2 : k - 1] if k > 1 else []
        for q in range(members // PAIR):
            pair = (row - k) % rows_here * per_row + ((member // PAIR) ^ q)
            info = [member % PAIR, me, pair, (row - k) % rows_here, (member // PAIR) ^ q]
            info = jnp.stack(info).astype(jnp.int32)
            flat = lambda *shape: pl.BlockSpec(shape, lambda e, info: (0,) * len(shape))
            of_pair = lambda w: pl.BlockSpec((PAIR, slots, w), lambda e, info: (info[2], e, 0))
            of_expert = lambda a, b: pl.BlockSpec((1, a, b), lambda e, info: (e, 0, 0))
            outcome = pl.pallas_call(
                functools.partial(expert_kernel, len(kept) + len(tied)),
                grid_spec=pltpu.PrefetchScalarGridSpec(
                    num_scalar_prefetch=1,
                    grid=(experts,),
                    in_specs=[
                        flat(tokens + PAD, width),
                        flat(tokens + PAD, width),
                        pl.BlockSpec((PAIR, 8, tokens), lambda e, info: (info[2], 0, 0)),
                        pl.BlockSpec(
                            (rows_here, PAIR, 1, block, width),
                            lambda e, info: (0, info[4], info[3], 0, 0),
                        ),
                        of_expert(width, hidden),
                        of_expert(width, hidden),
                        of_expert(hidden, width),
                    ]
                    + [pl.BlockSpec(memory_space=pl.ANY)] * (len(kept) + len(tied)),
                    out_specs=[
                        flat(tokens + PAD, width),
                        flat(tokens + PAD, width),
                        pl.BlockSpec((PAIR, tokens, width), lambda e, info: (info[2], 0, 0)),
                        of_pair(width),
                        of_pair(width),
                        of_pair(hidden),
                        of_pair(hidden),
                        of_pair(hidden),
                    ],
                    scratch_shapes=[
                        pltpu.VMEM((PAIR, wide, width), BF16),
                        pltpu.VMEM((PAIR, wide, width), BF16),
                        pltpu.VMEM((PAIR, wide, tokens), BF16),
                        pltpu.VMEM((PAIR, 8, tokens), F32),
                        pltpu.VMEM((8, tokens), F32),
                        pltpu.VMEM((PAIR, PAD, width), F32),
                    ],
                ),
                out_shape=[
                    struct((tokens + PAD, width), BF16),
                    struct((tokens + PAD, width), BF16),
                    pltpu.HBM((shards, tokens, width), BF16),
                    pltpu.HBM((shards, wide, width), BF16),
                    pltpu.HBM((shards, wide, width), BF16),
                    pltpu.HBM((shards, wide, hidden), BF16),
                    pltpu.HBM((shards, wide, hidden), BF16),
                    pltpu.HBM((shards, wide, hidden), BF16),
                ],
                input_output_aliases={8 + i: 2 + i for i in range(len(kept))},
                compiler_params=params(40),
                cost_estimate=took(16),
                name="experts",
            )(
                info,
                group[2 * q],
                group[2 * q + 1],
                named,
                *stored,
                *kept,
                *tied,
            )
            dx_parts[k] += outcome[:2]
            kept = outcome[2:]
        dx_sums.append(joined(dx_parts[k]))
    sent = [dx_sums[0]] + [onward(dx_sums[k], rows_here - k) for k in range(1, rows_here)]
    dx_sum = add(*sent)

    info = jnp.stack([member % PAIR, me, me, core]).astype(jnp.int32)
    halves = (3, width // 2, hidden)
    one_expert = lambda w: pl.BlockSpec((shards, slots, w), lambda i: (0, i, 0))
    half = pl.BlockSpec((1,) + halves, lambda i: (i, 0, 0, 0))
    keep, send = pl.pallas_call(
        expert_grads_kernel,
        grid=(experts,),
        out_shape=[struct((experts,) + halves, BF16)] * 2,
        in_specs=[scalars(), one_expert(width), one_expert(width)]
        + [one_expert(hidden)] * 3
        + [pl.BlockSpec(memory_space=pl.ANY)] * 2,
        out_specs=[half] * 2,
        compiler_params=params(60),
        cost_estimate=took(60),
        name="expert_grads",
    )(info, *kept[1:], dx_sums[2], dx_sums[3])
    received = row_swap(after([send], dx_sum)[0], 1)
    y_sum = lax.psum_scatter(
        after([kept[0]], dx_sums[3])[0], "seq", scatter_dimension=0, tiled=False
    )
    own_upstream = lax.dynamic_index_in_dim(upstream, row, 2, keepdims=False)
    own_upstream = lax.dynamic_index_in_dim(own_upstream, member, 1, keepdims=False)
    own_upstream = own_upstream.reshape(tokens, width)
    vectors, grad_mixed, grad_residual, gaz = pl.pallas_call(
        middle_kernel,
        out_shape=[
            struct((EXTRA, width), BF16),
            struct((tokens, width), BF16),
            struct((tokens, width), F32),
            struct((rows_here, TILES, 4 * BLOCK, LANES), BF16),
        ],
        in_specs=[whole()] * 8 + [pl.BlockSpec(memory_space=pl.ANY)],
        out_specs=[whole()] * 4,
        compiler_params=params(48),
        cost_estimate=took(6),
        name="middle",
    )(dx_sum, own_upstream, xg, residual, gates, gain_two, router, output_weight, keep)

    dq, dkv, weights = pl.pallas_call(
        functools.partial(attention_back_kernel, members),
        out_shape=[
            struct((tokens, width), BF16),
            struct((members, tokens, width), BF16),
            struct((3 * width + EXTRA, width), BF16),
        ],
        in_specs=[scalars()] + [whole()] * 12 + [pl.BlockSpec(memory_space=pl.ANY)],
        out_specs=[whole()] * 3,
        scratch_shapes=[
            pltpu.VMEM((length, inner), F32),
            pltpu.VMEM((length, inner), F32),
            pltpu.VMEM((length, width), BF16),
        ],
        compiler_params=params(58),
        cost_estimate=took(21.5),
        name="attention_back",
    )(me_pair, qz, gaz, k_row, v_row, own_pos, cosine, sine, mix, own_mix, att, grad_mixed, vectors, vectors)
    kept_half = after([keep], dq)[0]
    mine = [add(kept_half[i], received[i]) for i in range(experts)]
    crossed = []
    for e in range(experts):
        bit = 2
        while bit < lax.axis_size("rows"):
            crossed.append(row_swap(mine[e], bit))
            mine[e] = add(mine[e], crossed[-1])
            bit *= 2
    finished = []
    for e in range(experts):
        grad_spec = lambda a, b: pl.BlockSpec((1, a, b), lambda i, e=e: (e, 0, 0))
        half = pl.BlockSpec(halves, lambda i: (0, 0, 0))
        finished = pl.pallas_call(
            functools.partial(finish_kernel, len(finished)),
            grid=(1,),
            out_shape=[
                struct((experts, width, hidden), F32),
                struct((experts, width, hidden), F32),
                struct((experts, hidden, width), F32),
            ],
            in_specs=[scalars(), half, half]
            + [pl.BlockSpec(memory_space=pl.ANY)] * len(finished),
            out_specs=[grad_spec(width, hidden), grad_spec(width, hidden), grad_spec(hidden, width)],
            input_output_aliases={3 + i: i for i in range(len(finished))},
            compiler_params=params(32),
            cost_estimate=took(0.1),
            name="finish",
        )(info, mine[e], row_swap(mine[e], 1), *finished)
    dkv = lax.all_to_all(dkv, "seq", 0, 0, tiled=True, axis_index_groups=same_row)
    grad_in, first_part = pl.pallas_call(
        functools.partial(last_kernel, members),
        out_shape=[struct((tokens, width), BF16), struct((8, width), F32)],
        in_specs=[whole()] * 8 + [pl.BlockSpec(memory_space=pl.ANY)],
        out_specs=[whole()] * 2,
        compiler_params=params(48),
        cost_estimate=took(0.1),
        name="last",
    )(dq, dkv, query_weight, key_weight, value_weight, own_in, grad_residual, gain_one, crossed[0])

    steps = [crossed[min(i, experts - 1)] for i in range(4)]
    first_sum, bit = after([first_part], steps[2])[0], 1
    while bit < shards:
        first_sum = first_sum + across(first_sum, bit)
        bit *= 2
    bit = 1
    while bit < lax.axis_size("rows"):
        first_sum = first_sum + row_swap(first_sum, bit)
        bit *= 2
    steps = [crossed[min(i, experts - 1)] for i in range(4)]
    hidden_out = after([(residual + y_sum.astype(F32)).astype(BF16)], steps[1])[0]
    back = lambda values: lax.all_to_all(
        values.reshape(rows_here, block, width), "seq", 0, 0, tiled=True, axis_index_groups=same_member
    )
    hidden_out, grad_in = back(hidden_out), back(grad_in)
    shared = lax.psum(weights, ("rows", "seq"))
    shared = after([shared], hidden_out, grad_in, first_sum, finished[0])[0]
    query_sum, keyval_sum, output_sum, vector_sum = (
        shared[i * width : (i + 1) * width].astype(F32) for i in range(4)
    )
    return (
        hidden_out,
        grad_in.astype(F32),
        first_sum[0],
        query_sum,
        keyval_sum[:, :inner],
        keyval_sum[:, inner:],
        output_sum,
        vector_sum[expert_count],
        vector_sum[:expert_count].T,
        *finished,
    )


def solution(mesh):
    placed = (
        P("rows", "seq", None),
        P("rows", "seq"),
        P("rows", "seq"),
        P("rows", "seq", None),
        P(),
        P(),
        P(),
        P(),
        P(),
        P(),
        P(),
        P("seq", None, None),
        P("seq", None, None),
        P("seq", None, None),
        P("rows", "seq", None),
    )
    return jax.shard_map(
        local,
        mesh=mesh,
        in_specs=placed,
        out_specs=(
            P("rows", "seq", None),
            P("rows", "seq", None),
            P(),
            P(),
            P(),
            P(),
            P(),
            P(),
            P(),
            P("seq", None, None),
            P("seq", None, None),
            P("seq", None, None),
        ),
        check_vma=False,
    )
```

```python
import functools
import math

import jax
import jax.numpy as jnp
from jax import lax
from jax.experimental import pallas as pl
from jax.experimental.pallas import tpu as pltpu
from jax.sharding import PartitionSpec as P

HEADS = 16
KV_HEADS = 8
HEAD_DIM = 64
TOPK = 8
MOST = 32
BLOCK = 64
LANES = 128
TILES = KV_HEADS * HEAD_DIM // LANES
EXTRA = 128
PAIR = 2
PAD = 16

EPS = 1e-06
THETA = 10000.0
NEG = -1e30
F32 = jnp.float32
BF16 = jnp.bfloat16
EXACT = lax.Precision.HIGHEST
NN = (((1,), (0,)), ((), ()))
NT = (((1,), (1,)), ((), ()))
TN = (((0,), (0,)), ((), ()))


def mul(left, right, dims=NN, precision=None):
    return lax.dot_general(left, right, dims, precision=precision, preferred_element_type=F32)


def params(megabytes):
    return pltpu.CompilerParams(vmem_limit_bytes=megabytes << 20)


def whole():
    return pl.BlockSpec(memory_space=pltpu.VMEM)


def scalars():
    return pl.BlockSpec(memory_space=pltpu.SMEM)


def struct(shape, dtype):
    return jax.ShapeDtypeStruct(shape, dtype)


def took(microseconds):
    return pl.CostEstimate(flops=int(microseconds * 0.5e9), bytes_accessed=0, transcendentals=0)


def low_half(shape):
    return lax.broadcasted_iota(jnp.int32, shape, 1) < HEAD_DIM


def swap_halves(tile):
    lane = lax.broadcasted_iota(jnp.int32, tile.shape, 1)
    quarter = HEAD_DIM // 2
    forward = pltpu.roll(tile, LANES - quarter, 1)
    backward = pltpu.roll(tile, quarter, 1)
    return jnp.where(lane % HEAD_DIM < quarter, forward, backward)


def rotate(tile, cosine, signed_sine):
    return tile * cosine + swap_halves(tile) * signed_sine


def unrotate(tile, cosine, signed_sine):
    return tile * cosine - swap_halves(tile) * signed_sine


def spread_heads(first, second):
    low = low_half(first.shape)
    return jnp.concatenate(
        [
            jnp.where(low, first, 0.0),
            jnp.where(low, pltpu.roll(first, HEAD_DIM, 1), 0.0),
            jnp.where(low, 0.0, pltpu.roll(second, HEAD_DIM, 1)),
            jnp.where(low, 0.0, second),
        ],
        axis=0,
    )


def gather_heads(stacked):
    low = low_half((BLOCK, LANES))
    one, two, three, four = (stacked[i * BLOCK : (i + 1) * BLOCK] for i in range(4))
    first = jnp.where(low, one, pltpu.roll(two, HEAD_DIM, 1))
    second = jnp.where(low, pltpu.roll(three, HEAD_DIM, 1), four)
    return first, second


def allowed_keys(piece, members, member, pos_ref):
    keys = (piece + 1) * members * BLOCK
    start = (piece * members + member) * BLOCK
    place = start + lax.broadcasted_iota(jnp.int32, (BLOCK, keys), 0)
    key = lax.broadcasted_iota(jnp.int32, (BLOCK, keys), 1)
    opening = place - pos_ref[piece * BLOCK : (piece + 1) * BLOCK, :]
    return (key <= place) & (key >= opening)


def probabilities(stacked, key_tile, allowed):
    keys = key_tile.shape[0]
    scores = mul(stacked, key_tile, NT) * HEAD_DIM**-0.5
    scores = scores.reshape(4, BLOCK, keys)
    scores = jnp.where(allowed[None], scores, NEG)
    weights = jnp.exp(scores - jnp.max(scores, axis=-1, keepdims=True))
    probs = weights * (1.0 / jnp.sum(weights, axis=-1, keepdims=True))
    return probs.reshape(4 * BLOCK, keys)


def two_parts(values):
    high = values.astype(BF16).astype(F32)
    return jnp.concatenate([high, values - high], axis=0).astype(BF16)


def front_kernel(
    members,
    blocks,
    me_ref,
    *refs,
):
    front_body(members, me_ref, refs[:blocks], *refs[blocks:])


def front_body(
    members,
    me_ref,
    block_refs,
    cos_ref,
    sin_ref,
    pos_ref,
    ids_ref,
    gain_one_ref,
    wq_ref,
    wk_ref,
    wv_ref,
    wo_ref,
    gain_two_ref,
    router_ref,
    mix_ref,
    own_ref,
    qz_ref,
    k_ref,
    v_ref,
    att_ref,
    res_ref,
    xg_ref,
    gates_ref,
    input_ref,
    h_ref,
):
    member = me_ref[0]
    length, width = h_ref.shape
    tokens = own_ref.shape[0]
    pieces = tokens // BLOCK
    step = 256
    for i, block_ref in enumerate(block_refs):
        h_ref[pl.ds(pl.multiple_of(me_ref[2 + i] * BLOCK, BLOCK), BLOCK), :] = block_ref[...]

    def keys_step(i, carry):
        rows = pl.ds(pl.multiple_of(i * step, step), step)
        x = h_ref[rows, :].astype(F32)
        scale = lax.rsqrt(jnp.mean(x * x, axis=-1, keepdims=True) + EPS)
        mix = (x * scale * gain_one_ref[...]).astype(BF16)
        mix_ref[rows, :] = mix
        v_ref[rows, :] = mul(mix, wv_ref[...]).astype(BF16)
        pre = mul(mix, wk_ref[...])
        cosine, sine = cos_ref[rows, :], sin_ref[rows, :]
        for tile in range(TILES):
            lanes = slice(tile * LANES, (tile + 1) * LANES)
            k_ref[rows, lanes] = rotate(pre[:, lanes], cosine, sine).astype(BF16)
        return carry

    lax.fori_loop(0, length // step, keys_step, 0)
    own = [pl.ds(pl.multiple_of((p * members + member) * BLOCK, BLOCK), BLOCK) for p in range(pieces)]
    for piece in range(pieces):
        rows = slice(piece * BLOCK, (piece + 1) * BLOCK)
        own_ref[rows, :] = mix_ref[own[piece], :]
        input_ref[rows, :] = h_ref[own[piece], :]

    def query_step(tile, carry):
        pre = mul(own_ref[...], wq_ref[:, pl.ds(pl.multiple_of(tile * 256, 256), 256)])
        for piece in range(pieces):
            rows = slice(piece * BLOCK, (piece + 1) * BLOCK)
            cosine, sine = cos_ref[own[piece], :], sin_ref[own[piece], :]
            first = rotate(pre[rows, :LANES], cosine, sine)
            second = rotate(pre[rows, LANES:], cosine, sine)
            qz_ref[piece, tile] = spread_heads(first, second).astype(BF16)
        return carry

    lax.fori_loop(0, TILES, query_step, 0)
    for piece in range(pieces):
        allowed = allowed_keys(piece, members, member, pos_ref)
        keys = allowed.shape[1]
        rows = slice(piece * BLOCK, (piece + 1) * BLOCK)

        def attend(tile, carry):
            lanes = pl.ds(pl.multiple_of(tile * LANES, LANES), LANES)
            probs = probabilities(qz_ref[piece, tile], k_ref[:keys, lanes], allowed)
            first, second = gather_heads(mul(probs.astype(BF16), v_ref[:keys, lanes]))
            at = pl.multiple_of(tile * 256, 256)
            att_ref[rows, pl.ds(at, LANES)] = first.astype(BF16)
            att_ref[rows, pl.ds(at + LANES, LANES)] = second.astype(BF16)
            return carry

        lax.fori_loop(0, TILES, attend, 0)
    mixed = mul(att_ref[...], wo_ref[...])
    residual = input_ref[...].astype(F32) + mixed
    res_ref[...] = residual
    scale = lax.rsqrt(jnp.mean(residual * residual, axis=-1, keepdims=True) + EPS)
    chosen = (residual * scale * gain_two_ref[...]).astype(BF16)
    xg_ref[:tokens, :] = chosen
    logits = mul(router_ref[...], chosen, NT)
    expert = lax.broadcasted_iota(jnp.int32, logits.shape, 0)
    named = expert == ids_ref[0:1, :]
    for k in range(1, TOPK):
        named = named | (expert == ids_ref[k : k + 1, :])
    logits = jnp.where(named, logits, NEG)
    weights = jnp.where(named, jnp.exp(logits - jnp.max(logits, axis=0, keepdims=True)), 0.0)
    gates = weights / jnp.sum(weights, axis=0, keepdims=True)
    gates_ref[...] = gates
    for part in range(logits.shape[0] // 8):
        lanes = slice(part * tokens, (part + 1) * tokens)
        xg_ref[tokens:, lanes] = two_parts(gates[part * 8 : (part + 1) * 8])


def one_hot(slot_row, rows):
    slot = lax.broadcasted_iota(jnp.int32, (rows, slot_row.shape[1]), 0).astype(F32)
    return slot == slot_row


def expert_kernel(
    kept,
    info_ref,
    xa_ref,
    xb_ref,
    named_ref,
    u_ref,
    wg_ref,
    wu_ref,
    wd_ref,
    *rest,
):
    (dxa_ref, dxb_ref) = rest[kept : kept + 2]
    (y_ref, xs_ref, us_ref, hs_ref, dg_ref, du_ref) = rest[kept + 2 : kept + 8]
    (dxs_ref, ys_ref, pick_ref, slot_ref, gates_ref, back_ref) = rest[kept + 8 :]
    e = pl.program_id(0)
    experts = pl.num_programs(0)
    tokens = named_ref.shape[2]
    width = xa_ref.shape[1]
    rows = tokens * MOST // BLOCK
    places = [(info_ref[0] + c) % PAIR for c in range(PAIR)]
    sources = (xa_ref, xb_ref)

    @pl.when(e == 0)
    def _():
        back_ref[...] = jnp.zeros_like(back_ref)
        earlier = lax.broadcasted_iota(jnp.int32, (tokens, tokens), 0)
        later = lax.broadcasted_iota(jnp.int32, (tokens, tokens), 1)
        before = (earlier < later).astype(F32).astype(BF16)
        for c in range(PAIR):
            named = named_ref[places[c]]
            slot_ref[c] = jnp.where(named > 0, mul(named.astype(BF16), before), -1.0)

    at = pl.ds(pl.multiple_of(e * rows, rows), rows)
    number = info_ref[1] * experts + e
    row = lax.rem(number, 8)
    lanes = pl.ds(pl.multiple_of(lax.div(number, 8) * tokens, tokens), tokens)
    entering, leaving, gate = [], [], []
    for c in range(PAIR):
        hot = one_hot(slot_ref[c, pl.ds(e, 1), :], rows)
        pick = hot.astype(F32).astype(BF16)
        pick_ref[c, at, :] = pick
        picked = mul(pick, sources[c][:tokens, :]).astype(BF16)
        xs_ref[places[c]] = picked
        entering.append(picked)
        picked = mul(pick, u_ref[:, places[c], 0].reshape(tokens, width)).astype(BF16)
        us_ref[places[c]] = picked
        leaving.append(picked)
        sent = sources[c][tokens:, lanes].astype(F32)
        gates_ref[...] = sent[:8] + sent[8:]
        gate.append(jnp.sum(jnp.where(hot, gates_ref[pl.ds(row, 1), :], 0.0), axis=1, keepdims=True))
    entering = jnp.concatenate(entering, axis=0)
    gate = jnp.concatenate(gate, axis=0)
    gate_pre = mul(entering, wg_ref[0])
    up_pre = mul(entering, wu_ref[0])
    product = mul(jnp.concatenate(leaving, axis=0), wd_ref[0], NT)
    share = 1.0 / (1.0 + jnp.exp(-gate_pre))
    silu = gate_pre * share
    hidden = silu * up_pre
    grad_gate = jnp.sum(hidden * product, axis=1, keepdims=True)
    grad_act = gate * product
    grad_gate_pre = (grad_act * up_pre * share * (1.0 + gate_pre * (1.0 - share))).astype(BF16)
    grad_up_pre = (grad_act * silu).astype(BF16)
    gated = (gate * hidden).astype(BF16)
    grad_rows = (mul(grad_gate_pre, wg_ref[0], NT) + mul(grad_up_pre, wu_ref[0], NT)).astype(BF16)
    out_rows = mul(gated, wd_ref[0]).astype(BF16)
    for c in range(PAIR):
        part = slice(c * rows, (c + 1) * rows)
        hs_ref[places[c]] = gated[part]
        dg_ref[places[c]] = grad_gate_pre[part]
        du_ref[places[c]] = grad_up_pre[part]
        dxs_ref[c, at, :] = grad_rows[part]
        ys_ref[c, at, :] = out_rows[part]
        hot = one_hot(slot_ref[c, pl.ds(e, 1), :], rows)
        returned = jnp.sum(jnp.where(hot, grad_gate[part], 0.0), axis=0, keepdims=True)
        high = returned.astype(BF16).astype(F32)
        back_ref[c, pl.ds(row, 1), lanes] = high
        back_ref[c, pl.ds(row + 8, 1), lanes] = returned - high

    @pl.when(e == experts - 1)
    def _():
        for c, dx_ref in enumerate((dxa_ref, dxb_ref)):
            dx_ref[:tokens, :] = mul(pick_ref[c], dxs_ref[c], TN).astype(BF16)
            dx_ref[tokens:, :] = back_ref[c].astype(BF16)
            y_ref[places[c], 0] = mul(pick_ref[c], ys_ref[c], TN).astype(BF16)


def expert_grads_kernel(info_ref, xs_ref, us_ref, hs_ref, dg_ref, du_ref, *rest):
    keep_ref, send_ref = rest[-2:]
    core = info_ref[3]
    group, rows, width = xs_ref.shape
    inner = hs_ref.shape[2]
    flat = lambda ref: ref[...].reshape(group * rows, ref.shape[2])

    for half, out_ref in ((core, keep_ref), (1 - core, send_ref)):
        step = min(256, width // 2)
        for at in range(0, width // 2, step):
            lanes = pl.ds(pl.multiple_of(half * (width // 2) + at, LANES), step)
            entering = xs_ref[:, :, lanes].reshape(group * rows, step)
            out_ref[0, 0, at : at + step, :] = mul(entering, flat(dg_ref), TN).astype(BF16)
            out_ref[0, 1, at : at + step, :] = mul(entering, flat(du_ref), TN).astype(BF16)
        step = inner // 2
        lanes = pl.ds(pl.multiple_of(half * step, LANES), step)
        gated = hs_ref[:, :, lanes].reshape(group * rows, step)
        product = mul(gated, flat(us_ref), TN).astype(BF16)
        out_ref[0, 2, :step, :] = product[:, :inner]
        out_ref[0, 2, step:, :] = product[:, inner:]


def finish_kernel(kept, info_ref, mine_ref, other_ref, *rest):
    gate_ref, up_ref, down_ref = rest[kept:]
    core = info_ref[3]
    half = mine_ref.shape[1]
    inner = mine_ref.shape[2]
    for source, place in ((mine_ref, core), (other_ref, 1 - core)):
        rows = pl.ds(pl.multiple_of(place * half, half), half)
        gate_ref[0, rows, :] = source[0].astype(F32)
        up_ref[0, rows, :] = source[1].astype(F32)
        rows = pl.ds(pl.multiple_of(place * (half // 2), half // 2), half // 2)
        down_ref[0, rows, :inner] = source[2, : half // 2].astype(F32)
        down_ref[0, rows, inner:] = source[2, half // 2 :].astype(F32)


def spread_kernel(query_ref, keyval_ref, output_ref, vectors_ref, *rest):
    sums = rest[-5:]
    inner = sums[1].shape[1]
    sums[0][...] = query_ref[...].astype(F32)
    sums[1][...] = keyval_ref[:, :inner].astype(F32)
    sums[2][...] = keyval_ref[:, inner:].astype(F32)
    sums[3][...] = output_ref[...].astype(F32)

    @pl.when(pl.program_id(0) == 0)
    def _():
        sums[4][...] = vectors_ref[...].astype(F32)


def add(*terms):
    return sum(term.astype(F32) for term in terms).astype(terms[0].dtype)


def plus_kernel(left_ref, right_ref, out_ref):
    total = left_ref[...].astype(F32) + right_ref[...].astype(F32)
    out_ref[...] = total.reshape(out_ref.shape).astype(out_ref.dtype)


def plus(left, right, at=None):
    parts, rows, columns = left.shape[-3:]
    entry = pl.BlockSpec((1, rows, columns), lambda i: (i, 0, 0))
    source = entry if at is None else pl.BlockSpec((1, 1, rows, columns), lambda i: (at, i, 0, 0))
    return pl.pallas_call(
        plus_kernel,
        grid=(parts,),
        out_shape=struct((parts, rows, columns), left.dtype),
        in_specs=[source, source],
        out_specs=entry,
        compiler_params=params(16),
        cost_estimate=took(0.1),
        name="plus",
    )(left, right)


def after(values, *others):
    anywhere = pl.BlockSpec(memory_space=pl.ANY)
    return pl.pallas_call(
        lambda *refs: None,
        out_shape=[struct(v.shape, v.dtype) for v in values],
        in_specs=[anywhere] * (len(values) + len(others)),
        out_specs=[anywhere] * len(values),
        input_output_aliases={i: i for i in range(len(values))},
        name="after",
    )(*values, *others)


def put_block(whole_array, block, *at):
    for _ in range(whole_array.ndim - block.ndim):
        block = block[None]
    return lax.dynamic_update_slice(
        whole_array, block, tuple(at) + (0,) * (whole_array.ndim - len(at))
    )


def middle_kernel(
    dx_ref,
    u_ref,
    xg_ref,
    res_ref,
    gates_ref,
    gain_two_ref,
    router_ref,
    wo_ref,
    *rest,
):
    vectors_ref, mixed_ref, gres_ref, gaz_ref = rest[-4:]
    tokens, width = u_ref.shape
    experts = gates_ref.shape[0]
    pieces = tokens // BLOCK
    parts = []
    for part in range(experts // 8):
        sent = dx_ref[tokens:, part * tokens : (part + 1) * tokens].astype(F32)
        parts.append(sent[:8] + sent[8:])
    grad_gates = jnp.concatenate(parts, axis=0)
    gates = gates_ref[...]
    grad_logits = gates * (grad_gates - jnp.sum(gates * grad_gates, axis=0, keepdims=True))
    grad_normed = dx_ref[:tokens, :].astype(F32) + mul(
        grad_logits, router_ref[...].astype(F32), TN, EXACT
    )
    router = mul(grad_logits, xg_ref[:tokens, :].astype(F32), NN, EXACT)
    residual = res_ref[...]
    scale = lax.rsqrt(jnp.mean(residual * residual, axis=-1, keepdims=True) + EPS)
    normed = residual * scale
    second = jnp.sum(grad_normed * normed, axis=0, keepdims=True)
    spare = jnp.zeros((vectors_ref.shape[0] - experts - 1, width), F32)
    vectors_ref[...] = jnp.concatenate([router, second, spare], axis=0).astype(BF16)
    scaled = grad_normed * gain_two_ref[...]
    grad_residual = u_ref[...].astype(F32) + scale * (
        scaled - normed * jnp.mean(scaled * normed, axis=-1, keepdims=True)
    )
    gres_ref[...] = grad_residual
    grad_mixed = grad_residual.astype(BF16)
    mixed_ref[...] = grad_mixed
    for tile in range(TILES):
        grad_att = mul(grad_mixed, wo_ref[tile * 256 : (tile + 1) * 256, :], NT)
        for piece in range(pieces):
            rows = slice(piece * BLOCK, (piece + 1) * BLOCK)
            gaz_ref[piece, tile] = spread_heads(
                grad_att[rows, :LANES], grad_att[rows, LANES:]
            ).astype(BF16)


def attention_back_kernel(
    members,
    experts,
    me_ref,
    qz_ref,
    gaz_ref,
    k_ref,
    v_ref,
    pos_ref,
    cos_ref,
    sin_ref,
    mix_ref,
    own_ref,
    att_ref,
    mixed_ref,
    vectors_ref,
    wq_ref,
    wk_ref,
    wv_ref,
    gain_one_ref,
    *rest,
):
    dq_ref, dkv_ref, weights_ref, dk_acc, dv_acc, row_ref = rest[-6:]
    member = me_ref[0]
    tokens = own_ref.shape[0]
    pieces = tokens // BLOCK
    length = k_ref.shape[0]
    inner = k_ref.shape[1]
    dk_acc[...] = jnp.zeros_like(dk_acc)
    dv_acc[...] = jnp.zeros_like(dv_acc)
    for piece in range(pieces):
        allowed = allowed_keys(piece, members, member, pos_ref)
        keys = allowed.shape[1]
        rows = slice(piece * BLOCK, (piece + 1) * BLOCK)
        at = pl.ds(pl.multiple_of((piece * members + member) * BLOCK, BLOCK), BLOCK)

        def step(tile, carry):
            lanes = pl.ds(pl.multiple_of(tile * LANES, LANES), LANES)
            stacked, grads = qz_ref[piece, tile], gaz_ref[piece, tile]
            key_tile = k_ref[:keys, lanes]
            probs = probabilities(stacked, key_tile, allowed)
            grad_probs = mul(grads, v_ref[:keys, lanes], NT)
            delta = jnp.sum(probs * grad_probs, axis=-1, keepdims=True)
            grad_scores = (probs * (grad_probs - delta) * HEAD_DIM**-0.5).astype(BF16)
            dk_acc[:keys, lanes] += mul(grad_scores, stacked, TN)
            dv_acc[:keys, lanes] += mul(probs.astype(BF16), grads, TN)
            first, second = gather_heads(mul(grad_scores, key_tile))
            cosine, sine = cos_ref[at, :], sin_ref[at, :]
            out = pl.multiple_of(tile * 256, 256)
            dq_ref[rows, pl.ds(out, LANES)] = unrotate(first, cosine, sine).astype(BF16)
            dq_ref[rows, pl.ds(out + LANES, LANES)] = unrotate(second, cosine, sine).astype(BF16)
            return carry

        lax.fori_loop(0, TILES, step, 0)
    for block in range(length // BLOCK):
        rows = slice(block * BLOCK, (block + 1) * BLOCK)
        cosine, sine = cos_ref[rows, :], sin_ref[rows, :]
        for tile in range(TILES):
            lanes = slice(tile * LANES, (tile + 1) * LANES)
            row_ref[rows, lanes] = unrotate(dk_acc[rows, lanes], cosine, sine).astype(BF16)
        row_ref[rows, inner:] = dv_acc[rows, :].astype(BF16)
        piece, owner = block // members, block % members
        dkv_ref[owner, piece * BLOCK : (piece + 1) * BLOCK, :] = row_ref[rows, :]
    width = dq_ref.shape[1]
    for i, (left_ref, right_ref) in enumerate(
        ((own_ref, dq_ref), (mix_ref, row_ref), (att_ref, mixed_ref))
    ):
        product = mul(left_ref[...], right_ref[...], TN)
        weights_ref[i * width : (i + 1) * width, :] = product.astype(BF16)
    first = jnp.sum(mul(dq_ref[...], wq_ref[...], NT) * own_ref[...].astype(F32), axis=0, keepdims=True)
    for at in range(0, length, tokens):
        rows = slice(at, at + tokens)
        grad_mixer = mul(row_ref[rows, :inner], wk_ref[...], NT)
        grad_mixer += mul(row_ref[rows, inner:], wv_ref[...], NT)
        first += jnp.sum(grad_mixer * mix_ref[rows, :].astype(F32), axis=0, keepdims=True)
    first = first / gain_one_ref[...]
    vectors = vectors_ref[...].astype(F32)
    place = lax.broadcasted_iota(jnp.int32, vectors.shape, 0)
    weights_ref[3 * width :, :] = jnp.where(place == experts + 1, first, vectors).astype(BF16)


def last_kernel(
    members,
    dq_ref,
    *refs,
):
    last_body(dq_ref, refs[:members], *refs[members:])


def last_body(
    dq_ref,
    dkv_refs,
    wq_ref,
    wk_ref,
    wv_ref,
    input_ref,
    gres_ref,
    gain_one_ref,
    *rest,
):
    gh_ref = rest[-1]
    inner = wk_ref.shape[1]
    grad_kv = sum(dkv_ref[...].astype(F32) for dkv_ref in dkv_refs).astype(BF16)
    grad_mixer = (
        mul(dq_ref[...], wq_ref[...], NT)
        + mul(grad_kv[:, :inner], wk_ref[...], NT)
        + mul(grad_kv[:, inner:], wv_ref[...], NT)
    )
    x = input_ref[...].astype(F32)
    scale = lax.rsqrt(jnp.mean(x * x, axis=-1, keepdims=True) + EPS)
    normed = x * scale
    scaled = grad_mixer * gain_one_ref[...]
    gh_ref[...] = (
        gres_ref[...]
        + scale * (scaled - normed * jnp.mean(scaled * normed, axis=-1, keepdims=True))
    ).astype(gh_ref.dtype)


def rope_tables(places):
    middle = HEAD_DIM // 2
    frequency = jnp.exp(jnp.arange(middle, dtype=F32) * (-2.0 * math.log(THETA) / HEAD_DIM))
    angles = places.astype(F32)[:, None] * frequency
    cosine, sine = jnp.cos(angles), jnp.sin(angles)
    return (
        jnp.concatenate([cosine] * 4, axis=1),
        jnp.concatenate([-sine, sine, -sine, sine], axis=1),
    )


def local(
    hidden_in,
    segment_ids,
    positions,
    expert_ids,
    first_gain,
    query_weight,
    key_weight,
    value_weight,
    output_weight,
    second_gain,
    router_weight,
    gate_weight,
    up_weight,
    down_weight,
    out_grad,
):
    rows_here, block, width = hidden_in.shape
    tokens = rows_here * block
    shards = lax.axis_size("seq")
    members = shards // rows_here
    length = shards * block
    inner = key_weight.shape[1]
    expert_count = router_weight.shape[1]
    experts, _, hidden = gate_weight.shape
    me = lax.axis_index("seq")
    row, member = me // members, me % members
    me_pair = jnp.stack([member, me]).astype(jnp.int32)
    same_member = [[r * members + m for r in range(rows_here)] for m in range(members)]
    same_row = [[r * members + m for m in range(members)] for r in range(rows_here)]
    slots = tokens * MOST // BLOCK

    meta = jnp.concatenate(
        [positions.reshape(1, tokens), expert_ids.reshape(tokens, TOPK).T], axis=0
    )
    row_in = lax.all_to_all(jnp.repeat(hidden_in, members, axis=0), "seq", 0, 0, tiled=True)
    row_in = row_in.reshape(length, width)
    def onward(values, count):
        to = lambda j: (j // members + count) % rows_here * members + j % members
        return lax.ppermute(values, "seq", [(j, to(j)) for j in range(shards)])

    def across(values, other):
        return lax.ppermute(values, "seq", [(j, j ^ other) for j in range(shards)])

    def row_swap(values, other):
        count = lax.axis_size("rows")
        return lax.ppermute(values, "rows", [(j, j ^ other) for j in range(count)])

    def gather(values):
        found = []
        for k in range(rows_here):
            values = onward(values, 1) if k else values
            found.append([values] + [across(values, other) for other in range(1, members)])
        return found

    def joined(part):
        return add(part[0], *(across(part[o], o) for o in range(1, members)))

    def scatter(sums):
        return add(*(onward(total, rows_here - k) if k else total for k, total in enumerate(sums)))

    core = lax.axis_index("rows") % 2

    of_row = lambda k: lax.dynamic_index_in_dim(hidden_in, (row + k) % rows_here, 0, keepdims=False)
    row_in = [of_row(k) for k in range(rows_here)]
    meta = after([jnp.broadcast_to(meta[None], (shards,) + meta.shape)], *row_in)[0]
    meta = lax.all_to_all(meta, "seq", 0, 0, tiled=True)
    row_in = row_in[:1] + [onward(row_in[k], k) for k in range(1, rows_here)]
    row_in = [[v] + [across(v, other) for other in range(1, members)] for v in row_in]
    row_in = [v for blocks in row_in for v in blocks]
    places = [
        (row - k) % rows_here * members + (member ^ other)
        for k in range(rows_here)
        for other in range(members)
    ]
    me_row = jnp.stack([member, me] + places).astype(jnp.int32)
    upstream = lax.all_gather(out_grad, "seq", axis=0, tiled=False)
    upstream = upstream.reshape(rows_here, members, rows_here, block, width)
    stored = [
        pltpu.with_memory_space_constraint(v, pltpu.HBM)
        for v in (upstream, gate_weight, up_weight, down_weight)
    ]

    meta = meta.reshape(rows_here, members, TOPK + 1, rows_here, block)
    row_meta = lax.dynamic_index_in_dim(meta, row, 3, keepdims=False)
    own_meta = lax.dynamic_index_in_dim(row_meta, member, 1, keepdims=False)
    cosine, sine = rope_tables(row_meta[:, :, 0].reshape(length))
    own_pos = own_meta[:, 0].reshape(tokens, 1)
    own_ids = own_meta[:, 1:].transpose(1, 0, 2).reshape(TOPK, tokens)
    lane = jnp.arange(8, dtype=jnp.int32)
    wanted = jnp.where(lane < experts, me * experts + lane, -1)
    named = jnp.any(
        meta[:, :, 1:, None] == wanted[None, None, None, :, None, None], axis=2
    )
    named = named.transpose(3, 1, 2, 0, 4).reshape(shards, 8, tokens).astype(F32)

    gain_one, gain_two = first_gain.reshape(1, width), second_gain.reshape(1, width)
    router = router_weight.T
    mix, own_mix, qz, k_row, v_row, att, residual, xg, gates, own_in = pl.pallas_call(
        functools.partial(front_kernel, members, shards),
        out_shape=[
            struct((length, width), BF16),
            struct((tokens, width), BF16),
            struct((rows_here, TILES, 4 * BLOCK, LANES), BF16),
            struct((length, inner), BF16),
            struct((length, inner), BF16),
            struct((tokens, width), BF16),
            struct((tokens, width), F32),
            struct((tokens + PAD, width), BF16),
            struct((expert_count, tokens), F32),
            struct((tokens, width), BF16),
        ],
        in_specs=[scalars()] + [whole()] * (shards + 11),
        out_specs=[whole()] * 10,
        scratch_shapes=[pltpu.VMEM((length, width), BF16)],
        compiler_params=params(56),
        cost_estimate=took(19.5),
        name="front",
    )(
        me_row,
        *row_in,
        cosine,
        sine,
        own_pos,
        own_ids,
        gain_one,
        query_weight,
        key_weight,
        value_weight,
        output_weight,
        gain_two,
        router,
    )

    per_row = members // PAIR
    one_on = onward(xg, 1)
    beside = [across(xg, other) for other in range(1, members)]
    one_on = after([one_on], *beside)[0]
    sets = [[xg] + beside, [one_on] + [across(one_on, other) for other in range(1, members)]]
    two_on = onward(one_on, 1)
    wide, narrow = experts * slots, hidden
    kept = []
    order = list(range(rows_here))
    dx_parts, dx_sums = [[] for _ in order], []
    for k in order:
        group = sets[k]
        tied = []
        for q in range(members // PAIR):
            pair = (row - k) % rows_here * per_row + ((member // PAIR) ^ q)
            info = [member % PAIR, me, pair, (row - k) % rows_here, (member // PAIR) ^ q]
            info = jnp.stack(info).astype(jnp.int32)
            flat = lambda *shape: pl.BlockSpec(shape, lambda e, info: (0,) * len(shape))
            of_pair = lambda w: pl.BlockSpec((PAIR, slots, w), lambda e, info: (info[2], e, 0))
            of_expert = lambda a, b: pl.BlockSpec((1, a, b), lambda e, info: (e, 0, 0))
            outcome = pl.pallas_call(
                functools.partial(expert_kernel, len(kept) + len(tied)),
                grid_spec=pltpu.PrefetchScalarGridSpec(
                    num_scalar_prefetch=1,
                    grid=(experts,),
                    in_specs=[
                        flat(tokens + PAD, width),
                        flat(tokens + PAD, width),
                        pl.BlockSpec((PAIR, 8, tokens), lambda e, info: (info[2], 0, 0)),
                        pl.BlockSpec(
                            (rows_here, PAIR, 1, block, width),
                            lambda e, info: (0, info[4], info[3], 0, 0),
                        ),
                        of_expert(width, hidden),
                        of_expert(width, hidden),
                        of_expert(hidden, width),
                    ]
                    + [pl.BlockSpec(memory_space=pl.ANY)] * (len(kept) + len(tied)),
                    out_specs=[
                        flat(tokens + PAD, width),
                        flat(tokens + PAD, width),
                        pl.BlockSpec(
                            (PAIR, 1, tokens, width), lambda e, info: (info[4], info[3], 0, 0)
                        ),
                        of_pair(width),
                        of_pair(width),
                        of_pair(hidden),
                        of_pair(hidden),
                        of_pair(hidden),
                    ],
                    scratch_shapes=[
                        pltpu.VMEM((PAIR, wide, width), BF16),
                        pltpu.VMEM((PAIR, wide, width), BF16),
                        pltpu.VMEM((PAIR, wide, tokens), BF16),
                        pltpu.VMEM((PAIR, 8, tokens), F32),
                        pltpu.VMEM((8, tokens), F32),
                        pltpu.VMEM((PAIR, PAD, width), F32),
                    ],
                ),
                out_shape=[
                    struct((tokens + PAD, width), BF16),
                    struct((tokens + PAD, width), BF16),
                    pltpu.HBM((members, rows_here, tokens, width), BF16),
                    pltpu.HBM((shards, wide, width), BF16),
                    pltpu.HBM((shards, wide, width), BF16),
                    pltpu.HBM((shards, wide, hidden), BF16),
                    pltpu.HBM((shards, wide, hidden), BF16),
                    pltpu.HBM((shards, wide, hidden), BF16),
                ],
                input_output_aliases={8 + i: 2 + i for i in range(len(kept))},
                compiler_params=params(40),
                cost_estimate=took(16),
                name="experts",
            )(
                info,
                group[2 * q],
                group[2 * q + 1],
                named,
                *stored,
                *kept,
                *tied,
            )
            dx_parts[k] += outcome[:2]
            kept = outcome[2:]
        part = dx_parts[k]
        if k == 0:
            values = after([two_on], part[0])[0]
            for i in range(2, rows_here):
                values = onward(values, 1) if i > 2 else values
                sets.append([values] + [across(values, other) for other in range(1, members)])
        if k < 2:
            part = part[:1] + list(after(part[1:], *sets[rows_here - 1][1:]))
        dx_sums.append(joined(part))
    sent = [dx_sums[0]] + [onward(dx_sums[k], rows_here - k) for k in range(1, rows_here)]
    dx_sum = add(*sent)

    info = jnp.stack([member % PAIR, me, me, core]).astype(jnp.int32)
    halves = (3, width // 2, hidden)
    one_expert = lambda w: pl.BlockSpec((shards, slots, w), lambda i: (0, i, 0))
    half = pl.BlockSpec((1,) + halves, lambda i: (i, 0, 0, 0))
    keep, send = pl.pallas_call(
        expert_grads_kernel,
        grid=(experts,),
        out_shape=[struct((experts,) + halves, BF16)] * 2,
        in_specs=[scalars(), one_expert(width), one_expert(width)]
        + [one_expert(hidden)] * 3
        + [pl.BlockSpec(memory_space=pl.ANY)] * 2,
        out_specs=[half] * 2,
        compiler_params=params(60),
        cost_estimate=took(60),
        name="expert_grads",
    )(info, *kept[1:], dx_sums[2], dx_sums[3])
    part_of = lambda values, m: lax.dynamic_index_in_dim(values, m, 0, keepdims=False)
    y_all = after([kept[0]], dx_sums[3])[0]
    middle_row = rows_here // 2
    y_near = [
        [across(part_of(y_all, member ^ o)[:middle_row], o) for o in range(1, members)],
        [across(part_of(y_all, member ^ o)[middle_row:], o) for o in range(1, members)],
    ]
    soon = y_near[0]
    own_upstream = lax.dynamic_index_in_dim(upstream, row, 2, keepdims=False)
    own_upstream = lax.dynamic_index_in_dim(own_upstream, member, 1, keepdims=False)
    own_upstream = own_upstream.reshape(tokens, width)
    vectors, grad_mixed, grad_residual, gaz = pl.pallas_call(
        middle_kernel,
        out_shape=[
            struct((EXTRA, width), BF16),
            struct((tokens, width), BF16),
            struct((tokens, width), F32),
            struct((rows_here, TILES, 4 * BLOCK, LANES), BF16),
        ],
        in_specs=[whole()] * 8 + [pl.BlockSpec(memory_space=pl.ANY)] * (1 + len(soon)),
        out_specs=[whole()] * 4,
        compiler_params=params(48),
        cost_estimate=took(6),
        name="middle",
    )(dx_sum, own_upstream, xg, residual, gates, gain_two, router, output_weight, keep, *soon)

    dq, dkv, weights = pl.pallas_call(
        functools.partial(attention_back_kernel, members, expert_count),
        out_shape=[
            struct((tokens, width), BF16),
            struct((members, tokens, width), BF16),
            struct((3 * width + EXTRA, width), BF16),
        ],
        in_specs=[scalars()]
        + [whole()] * 16
        + [pl.BlockSpec(memory_space=pl.ANY)],
        out_specs=[whole()] * 3,
        scratch_shapes=[
            pltpu.VMEM((length, inner), F32),
            pltpu.VMEM((length, inner), F32),
            pltpu.VMEM((length, width), BF16),
        ],
        compiler_params=params(58),
        cost_estimate=took(0.1),
        name="attention_back",
    )(
        me_pair,
        qz,
        gaz,
        k_row,
        v_row,
        own_pos,
        cosine,
        sine,
        mix,
        own_mix,
        att,
        grad_mixed,
        vectors,
        query_weight,
        key_weight,
        value_weight,
        gain_one,
        gain_one,
    )
    received = row_swap(after([send], gaz)[0], 1)
    kept_half = after([keep], dq)[0]
    mine = [plus(kept_half, received, i) for i in range(experts)]
    crossed = [row_swap(m, 2) for m in mine]
    dkv = [part_of(dkv, member)] + [across(part_of(dkv, member ^ o), o) for o in range(1, members)]
    grad_in = pl.pallas_call(
        functools.partial(last_kernel, members),
        out_shape=struct((tokens, width), BF16),
        in_specs=[whole()] * (7 + members) + [pl.BlockSpec(memory_space=pl.ANY)] * len(y_near[1]),
        out_specs=whole(),
        compiler_params=params(48),
        cost_estimate=took(0.1),
        name="last",
    )(dq, *dkv, query_weight, key_weight, value_weight, own_in, grad_residual, gain_one, *y_near[1])

    y_near = [jnp.concatenate(halves, axis=0) for halves in zip(*y_near)]
    y_far = lax.all_to_all(
        add(after([part_of(y_all, member)], dq)[0], *y_near), "seq", 0, 0, tiled=True, axis_index_groups=same_member
    )
    y_sum = jnp.sum(y_far.astype(F32), axis=0)
    hidden_out = (residual + y_sum).astype(BF16)
    back = lambda values: lax.all_to_all(
        values.reshape(rows_here, block, width), "seq", 0, 0, tiled=True, axis_index_groups=same_member
    )
    hidden_out, grad_in = back(hidden_out), back(grad_in)
    finished = []
    for e in range(experts):
        served = {1: y_far, 2: grad_in, 3: hidden_out}.get(e)
        crossed[e] = after([crossed[e]], served)[0] if e in (1, 2, 3) else crossed[e]
        mine[e] = plus(mine[e], crossed[e])
        grad_spec = lambda a, b: pl.BlockSpec((1, a, b), lambda i, e=e: (e, 0, 0))
        half = pl.BlockSpec(halves, lambda i: (0, 0, 0))
        finished = pl.pallas_call(
            functools.partial(finish_kernel, len(finished)),
            grid=(1,),
            out_shape=[
                pltpu.HBM((experts, width, hidden), F32),
                pltpu.HBM((experts, width, hidden), F32),
                pltpu.HBM((experts, hidden, width), F32),
            ],
            in_specs=[scalars(), half, half]
            + [pl.BlockSpec(memory_space=pl.ANY)] * len(finished),
            out_specs=[grad_spec(width, hidden), grad_spec(width, hidden), grad_spec(hidden, width)],
            input_output_aliases={3 + i: i for i in range(len(finished))},
            compiler_params=params(32),
            cost_estimate=took(0.1),
            name="finish",
        )(info, mine[e], row_swap(mine[e], 1), *finished)
    shared = lax.psum(weights, ("rows", "seq"))
    step = 128
    part = lambda i: pl.BlockSpec((step, width), lambda r, i=i: (i * (width // step) + r, 0))
    rows_of = lambda w: pl.BlockSpec((step, w), lambda r: (r, 0))
    query_sum, key_sum, value_sum, output_sum, vector_sum = pl.pallas_call(
        spread_kernel,
        grid=(width // step,),
        out_shape=[
            pltpu.HBM((width, width), F32),
            pltpu.HBM((width, inner), F32),
            pltpu.HBM((width, inner), F32),
            pltpu.HBM((width, width), F32),
            struct((EXTRA, width), F32),
        ],
        in_specs=[part(0), part(1), part(2), pl.BlockSpec((EXTRA, width), lambda r: (3 * width // EXTRA, 0))]
        + [pl.BlockSpec(memory_space=pl.ANY)] * 3,
        out_specs=[
            rows_of(width),
            rows_of(inner),
            rows_of(inner),
            rows_of(width),
            pl.BlockSpec((EXTRA, width), lambda r: (0, 0)),
        ],
        compiler_params=params(24),
        cost_estimate=took(0.1),
        name="spread",
    )(*[pltpu.with_memory_space_constraint(shared, pltpu.HBM)] * 4, hidden_out, grad_in, finished[0])
    return (
        hidden_out,
        grad_in.astype(F32),
        vector_sum[expert_count + 1],
        query_sum,
        key_sum,
        value_sum,
        output_sum,
        vector_sum[expert_count],
        vector_sum[:expert_count].T,
        *finished,
    )


def solution(mesh):
    placed = (
        P("rows", "seq", None),
        P("rows", "seq"),
        P("rows", "seq"),
        P("rows", "seq", None),
        P(),
        P(),
        P(),
        P(),
        P(),
        P(),
        P(),
        P("seq", None, None),
        P("seq", None, None),
        P("seq", None, None),
        P("rows", "seq", None),
    )
    return jax.shard_map(
        local,
        mesh=mesh,
        in_specs=placed,
        out_specs=(
            P("rows", "seq", None),
            P("rows", "seq", None),
            P(),
            P(),
            P(),
            P(),
            P(),
            P(),
            P(),
            P("seq", None, None),
            P("seq", None, None),
            P("seq", None, None),
        ),
        check_vma=False,
    )
```

```python
import functools
import math

import jax
import jax.numpy as jnp
from jax import lax
from jax.experimental import pallas as pl
from jax.experimental.pallas import tpu as pltpu
from jax.sharding import PartitionSpec as P

HEADS = 16
KV_HEADS = 8
HEAD_DIM = 64
TOPK = 8
MOST = 32
BLOCK = 64
LANES = 128
TILES = KV_HEADS * HEAD_DIM // LANES
EXTRA = 128
PAIR = 2
PAD = 16

EPS = 1e-06
THETA = 10000.0
NEG = -1e30
F32 = jnp.float32
BF16 = jnp.bfloat16
EXACT = lax.Precision.HIGHEST
NN = (((1,), (0,)), ((), ()))
NT = (((1,), (1,)), ((), ()))
TN = (((0,), (0,)), ((), ()))


def mul(left, right, dims=NN, precision=None):
    return lax.dot_general(left, right, dims, precision=precision, preferred_element_type=F32)


def params(megabytes):
    return pltpu.CompilerParams(vmem_limit_bytes=megabytes << 20)


def whole():
    return pl.BlockSpec(memory_space=pltpu.VMEM)


def scalars():
    return pl.BlockSpec(memory_space=pltpu.SMEM)


def struct(shape, dtype):
    return jax.ShapeDtypeStruct(shape, dtype)


def took(microseconds):
    return pl.CostEstimate(flops=int(microseconds * 0.5e9), bytes_accessed=0, transcendentals=0)


def low_half(shape):
    return lax.broadcasted_iota(jnp.int32, shape, 1) < HEAD_DIM


def swap_halves(tile):
    lane = lax.broadcasted_iota(jnp.int32, tile.shape, 1)
    quarter = HEAD_DIM // 2
    forward = pltpu.roll(tile, LANES - quarter, 1)
    backward = pltpu.roll(tile, quarter, 1)
    return jnp.where(lane % HEAD_DIM < quarter, forward, backward)


def rotate(tile, cosine, signed_sine):
    return tile * cosine + swap_halves(tile) * signed_sine


def unrotate(tile, cosine, signed_sine):
    return tile * cosine - swap_halves(tile) * signed_sine


def spread_heads(first, second):
    low = low_half(first.shape)
    return jnp.concatenate(
        [
            jnp.where(low, first, 0.0),
            jnp.where(low, pltpu.roll(first, HEAD_DIM, 1), 0.0),
            jnp.where(low, 0.0, pltpu.roll(second, HEAD_DIM, 1)),
            jnp.where(low, 0.0, second),
        ],
        axis=0,
    )


def gather_heads(stacked):
    low = low_half((BLOCK, LANES))
    one, two, three, four = (stacked[i * BLOCK : (i + 1) * BLOCK] for i in range(4))
    first = jnp.where(low, one, pltpu.roll(two, HEAD_DIM, 1))
    second = jnp.where(low, pltpu.roll(three, HEAD_DIM, 1), four)
    return first, second


def allowed_keys(piece, members, member, pos_ref):
    keys = (piece + 1) * members * BLOCK
    start = (piece * members + member) * BLOCK
    place = start + lax.broadcasted_iota(jnp.int32, (BLOCK, keys), 0)
    key = lax.broadcasted_iota(jnp.int32, (BLOCK, keys), 1)
    opening = place - pos_ref[piece * BLOCK : (piece + 1) * BLOCK, :]
    return (key <= place) & (key >= opening)


def probabilities(stacked, key_tile, allowed):
    keys = key_tile.shape[0]
    scores = mul(stacked, key_tile, NT)
    scores = scores.reshape(4, BLOCK, keys)
    scores = jnp.where(allowed[None], scores, NEG)
    weights = jnp.exp(scores - jnp.max(scores, axis=-1, keepdims=True))
    probs = weights * (1.0 / jnp.sum(weights, axis=-1, keepdims=True))
    return probs.reshape(4 * BLOCK, keys)


def two_parts(values):
    high = values.astype(BF16).astype(F32)
    return jnp.concatenate([high, values - high], axis=0).astype(BF16)


def front_kernel(
    members,
    blocks,
    me_ref,
    *refs,
):
    front_body(members, me_ref, refs[:blocks], *refs[blocks:])


def front_body(
    members,
    me_ref,
    block_refs,
    cos_ref,
    sin_ref,
    pos_ref,
    ids_ref,
    gain_one_ref,
    wq_ref,
    wk_ref,
    wv_ref,
    wo_ref,
    gain_two_ref,
    router_ref,
    mix_ref,
    own_ref,
    qz_ref,
    k_ref,
    v_ref,
    att_ref,
    res_ref,
    xg_ref,
    gates_ref,
    input_ref,
    *rest,
):
    probs_refs, h_ref = rest[:-1], rest[-1]
    member = me_ref[0]
    length, width = h_ref.shape
    tokens = own_ref.shape[0]
    pieces = tokens // BLOCK
    step = 256
    for i, block_ref in enumerate(block_refs):
        h_ref[pl.ds(pl.multiple_of(me_ref[2 + i] * BLOCK, BLOCK), BLOCK), :] = block_ref[...]

    def keys_step(i, carry):
        rows = pl.ds(pl.multiple_of(i * step, step), step)
        x = h_ref[rows, :].astype(F32)
        scale = lax.rsqrt(jnp.mean(x * x, axis=-1, keepdims=True) + EPS)
        mix = (x * scale * gain_one_ref[...]).astype(BF16)
        mix_ref[rows, :] = mix
        v_ref[rows, :] = mul(mix, wv_ref[...]).astype(BF16)
        pre = mul(mix, wk_ref[...])
        cosine, sine = cos_ref[rows, :], sin_ref[rows, :]
        for tile in range(TILES):
            lanes = slice(tile * LANES, (tile + 1) * LANES)
            k_ref[rows, lanes] = rotate(pre[:, lanes], cosine, sine).astype(BF16)
        return carry

    lax.fori_loop(0, length // step, keys_step, 0)
    own = [pl.ds(pl.multiple_of((p * members + member) * BLOCK, BLOCK), BLOCK) for p in range(pieces)]
    for piece in range(pieces):
        rows = slice(piece * BLOCK, (piece + 1) * BLOCK)
        own_ref[rows, :] = mix_ref[own[piece], :]
        input_ref[rows, :] = h_ref[own[piece], :]

    def query_step(tile, carry):
        pre = mul(own_ref[...], wq_ref[:, pl.ds(pl.multiple_of(tile * 256, 256), 256)])
        for piece in range(pieces):
            rows = slice(piece * BLOCK, (piece + 1) * BLOCK)
            cosine, sine = cos_ref[own[piece], :], sin_ref[own[piece], :]
            first = rotate(pre[rows, :LANES], cosine, sine)
            second = rotate(pre[rows, LANES:], cosine, sine)
            qz_ref[piece, tile] = (spread_heads(first, second) * HEAD_DIM**-0.5).astype(BF16)
        return carry

    lax.fori_loop(0, TILES, query_step, 0)
    for piece in range(pieces):
        allowed = allowed_keys(piece, members, member, pos_ref)
        keys = allowed.shape[1]
        rows = slice(piece * BLOCK, (piece + 1) * BLOCK)

        def attend(tile, carry):
            lanes = pl.ds(pl.multiple_of(tile * LANES, LANES), LANES)
            probs = probabilities(qz_ref[piece, tile], k_ref[:keys, lanes], allowed)
            probs = probs.astype(BF16)
            probs_refs[piece][tile] = probs
            first, second = gather_heads(mul(probs, v_ref[:keys, lanes]))
            at = pl.multiple_of(tile * 256, 256)
            att_ref[rows, pl.ds(at, LANES)] = first.astype(BF16)
            att_ref[rows, pl.ds(at + LANES, LANES)] = second.astype(BF16)
            return carry

        lax.fori_loop(0, TILES, attend, 0)
    mixed = mul(att_ref[...], wo_ref[...])
    residual = input_ref[...].astype(F32) + mixed
    res_ref[...] = residual
    scale = lax.rsqrt(jnp.mean(residual * residual, axis=-1, keepdims=True) + EPS)
    chosen = (residual * scale * gain_two_ref[...]).astype(BF16)
    xg_ref[:tokens, :] = chosen
    logits = mul(router_ref[...], chosen, NT)
    expert = lax.broadcasted_iota(jnp.int32, logits.shape, 0)
    named = expert == ids_ref[0:1, :]
    for k in range(1, TOPK):
        named = named | (expert == ids_ref[k : k + 1, :])
    logits = jnp.where(named, logits, NEG)
    weights = jnp.where(named, jnp.exp(logits - jnp.max(logits, axis=0, keepdims=True)), 0.0)
    gates = weights / jnp.sum(weights, axis=0, keepdims=True)
    gates_ref[...] = gates
    for part in range(logits.shape[0] // 8):
        lanes = slice(part * tokens, (part + 1) * tokens)
        xg_ref[tokens:, lanes] = two_parts(gates[part * 8 : (part + 1) * 8])


def one_hot(slot_row, rows):
    slot = lax.broadcasted_iota(jnp.int32, (rows, slot_row.shape[1]), 0).astype(F32)
    return slot == slot_row


def expert_kernel(
    kept,
    info_ref,
    xa_ref,
    xb_ref,
    named_ref,
    u_ref,
    wg_ref,
    wu_ref,
    wd_ref,
    *rest,
):
    (dxa_ref, dxb_ref) = rest[kept : kept + 2]
    (y_ref, xs_ref, us_ref, hs_ref, dg_ref, du_ref) = rest[kept + 2 : kept + 8]
    (dxs_ref, ys_ref, pick_ref, slot_ref, gates_ref, back_ref) = rest[kept + 8 :]
    e = pl.program_id(0)
    experts = pl.num_programs(0)
    tokens = named_ref.shape[2]
    width = xa_ref.shape[1]
    rows = tokens * MOST // BLOCK
    places = [(info_ref[0] + c) % PAIR for c in range(PAIR)]
    sources = (xa_ref, xb_ref)

    @pl.when(e == 0)
    def _():
        back_ref[...] = jnp.zeros_like(back_ref)
        earlier = lax.broadcasted_iota(jnp.int32, (tokens, tokens), 0)
        later = lax.broadcasted_iota(jnp.int32, (tokens, tokens), 1)
        before = (earlier < later).astype(F32).astype(BF16)
        for c in range(PAIR):
            named = named_ref[places[c]]
            slot_ref[c] = jnp.where(named > 0, mul(named.astype(BF16), before), -1.0)

    at = pl.ds(pl.multiple_of(e * rows, rows), rows)
    number = info_ref[1] * experts + e
    row = lax.rem(number, 8)
    lanes = pl.ds(pl.multiple_of(lax.div(number, 8) * tokens, tokens), tokens)
    entering, leaving, gate = [], [], []
    for c in range(PAIR):
        hot = one_hot(slot_ref[c, pl.ds(e, 1), :], rows)
        pick = hot.astype(F32).astype(BF16)
        pick_ref[c, at, :] = pick
        picked = mul(pick, sources[c][:tokens, :]).astype(BF16)
        xs_ref[places[c]] = picked
        entering.append(picked)
        picked = mul(pick, u_ref[:, places[c], 0].reshape(tokens, width)).astype(BF16)
        us_ref[places[c]] = picked
        leaving.append(picked)
        sent = sources[c][tokens:, lanes].astype(F32)
        gates_ref[...] = sent[:8] + sent[8:]
        gate.append(jnp.sum(jnp.where(hot, gates_ref[pl.ds(row, 1), :], 0.0), axis=1, keepdims=True))
    entering = jnp.concatenate(entering, axis=0)
    gate = jnp.concatenate(gate, axis=0)
    gate_pre = mul(entering, wg_ref[0])
    up_pre = mul(entering, wu_ref[0])
    product = mul(jnp.concatenate(leaving, axis=0), wd_ref[0], NT)
    share = 0.5 * jnp.tanh(0.5 * gate_pre) + 0.5
    silu = gate_pre * share
    hidden = silu * up_pre
    grad_gate = jnp.sum(hidden * product, axis=1, keepdims=True)
    grad_act = gate * product
    grad_gate_pre = (grad_act * up_pre * share * (1.0 + gate_pre * (1.0 - share))).astype(BF16)
    grad_up_pre = (grad_act * silu).astype(BF16)
    gated = (gate * hidden).astype(BF16)
    grad_rows = (mul(grad_gate_pre, wg_ref[0], NT) + mul(grad_up_pre, wu_ref[0], NT)).astype(BF16)
    out_rows = mul(gated, wd_ref[0]).astype(BF16)
    for c in range(PAIR):
        part = slice(c * rows, (c + 1) * rows)
        hs_ref[places[c]] = gated[part]
        dg_ref[places[c]] = grad_gate_pre[part]
        du_ref[places[c]] = grad_up_pre[part]
        dxs_ref[c, at, :] = grad_rows[part]
        ys_ref[c, at, :] = out_rows[part]
        hot = one_hot(slot_ref[c, pl.ds(e, 1), :], rows)
        returned = jnp.sum(jnp.where(hot, grad_gate[part], 0.0), axis=0, keepdims=True)
        high = returned.astype(BF16).astype(F32)
        back_ref[c, pl.ds(row, 1), lanes] = high
        back_ref[c, pl.ds(row + 8, 1), lanes] = returned - high

    @pl.when(e == experts - 1)
    def _():
        for c, dx_ref in enumerate((dxa_ref, dxb_ref)):
            dx_ref[:tokens, :] = mul(pick_ref[c], dxs_ref[c], TN).astype(BF16)
            dx_ref[tokens:, :] = back_ref[c].astype(BF16)
            y_ref[places[c], 0] = mul(pick_ref[c], ys_ref[c], TN).astype(BF16)


def expert_grads_kernel(info_ref, xs_ref, us_ref, hs_ref, dg_ref, du_ref, *rest):
    keep_ref, send_ref = rest[-2:]
    core = info_ref[3]
    group, rows, width = xs_ref.shape
    inner = hs_ref.shape[2]
    flat = lambda ref: ref[...].reshape(group * rows, ref.shape[2])

    for half, out_ref in ((core, keep_ref), (1 - core, send_ref)):
        step = min(256, width // 2)
        for at in range(0, width // 2, step):
            lanes = pl.ds(pl.multiple_of(half * (width // 2) + at, LANES), step)
            entering = xs_ref[:, :, lanes].reshape(group * rows, step)
            out_ref[0, 0, at : at + step, :] = mul(entering, flat(dg_ref), TN).astype(BF16)
            out_ref[0, 1, at : at + step, :] = mul(entering, flat(du_ref), TN).astype(BF16)
        step = inner // 2
        lanes = pl.ds(pl.multiple_of(half * step, LANES), step)
        gated = hs_ref[:, :, lanes].reshape(group * rows, step)
        product = mul(gated, flat(us_ref), TN).astype(BF16)
        out_ref[0, 2, :step, :] = product[:, :inner]
        out_ref[0, 2, step:, :] = product[:, inner:]


def finish_kernel(kept, info_ref, mine_ref, other_ref, *rest):
    gate_ref, up_ref, down_ref = rest[kept:]
    core = info_ref[3]
    half = mine_ref.shape[1]
    inner = mine_ref.shape[2]
    for source, place in ((mine_ref, core), (other_ref, 1 - core)):
        rows = pl.ds(pl.multiple_of(place * half, half), half)
        gate_ref[0, rows, :] = source[0].astype(F32)
        up_ref[0, rows, :] = source[1].astype(F32)
        rows = pl.ds(pl.multiple_of(place * (half // 2), half // 2), half // 2)
        down_ref[0, rows, :inner] = source[2, : half // 2].astype(F32)
        down_ref[0, rows, inner:] = source[2, half // 2 :].astype(F32)


def spread_kernel(query_ref, keyval_ref, output_ref, vectors_ref, *rest):
    sums = rest[-5:]
    inner = sums[1].shape[1]
    sums[0][...] = query_ref[...].astype(F32)
    sums[1][...] = keyval_ref[:, :inner].astype(F32)
    sums[2][...] = keyval_ref[:, inner:].astype(F32)
    sums[3][...] = output_ref[...].astype(F32)

    @pl.when(pl.program_id(0) == 0)
    def _():
        sums[4][...] = vectors_ref[...].astype(F32)


def add(*terms):
    return sum(term.astype(F32) for term in terms).astype(terms[0].dtype)


def plus_kernel(left_ref, right_ref, out_ref):
    total = left_ref[...].astype(F32) + right_ref[...].astype(F32)
    out_ref[...] = total.reshape(out_ref.shape).astype(out_ref.dtype)


def plus(left, right, at=None):
    parts, rows, columns = left.shape[-3:]
    entry = pl.BlockSpec((1, rows, columns), lambda i: (i, 0, 0))
    source = entry if at is None else pl.BlockSpec((1, 1, rows, columns), lambda i: (at, i, 0, 0))
    return pl.pallas_call(
        plus_kernel,
        grid=(parts,),
        out_shape=struct((parts, rows, columns), left.dtype),
        in_specs=[source, source],
        out_specs=entry,
        compiler_params=params(56),
        cost_estimate=took(0.1),
        name="plus",
    )(left, right)


def after(values, *others):
    anywhere = pl.BlockSpec(memory_space=pl.ANY)
    return pl.pallas_call(
        lambda *refs: None,
        out_shape=[struct(v.shape, v.dtype) for v in values],
        in_specs=[anywhere] * (len(values) + len(others)),
        out_specs=[anywhere] * len(values),
        input_output_aliases={i: i for i in range(len(values))},
        name="after",
    )(*values, *others)


def put_block(whole_array, block, *at):
    for _ in range(whole_array.ndim - block.ndim):
        block = block[None]
    return lax.dynamic_update_slice(
        whole_array, block, tuple(at) + (0,) * (whole_array.ndim - len(at))
    )


def middle_kernel(
    dx_ref,
    u_ref,
    xg_ref,
    res_ref,
    gates_ref,
    gain_two_ref,
    router_ref,
    wo_ref,
    *rest,
):
    vectors_ref, mixed_ref, gres_ref, gaz_ref = rest[-4:]
    tokens, width = u_ref.shape
    experts = gates_ref.shape[0]
    pieces = tokens // BLOCK
    parts = []
    for part in range(experts // 8):
        sent = dx_ref[tokens:, part * tokens : (part + 1) * tokens].astype(F32)
        parts.append(sent[:8] + sent[8:])
    grad_gates = jnp.concatenate(parts, axis=0)
    gates = gates_ref[...]
    grad_logits = gates * (grad_gates - jnp.sum(gates * grad_gates, axis=0, keepdims=True))
    grad_normed = dx_ref[:tokens, :].astype(F32) + mul(
        grad_logits, router_ref[...].astype(F32), TN, EXACT
    )
    router = mul(grad_logits, xg_ref[:tokens, :].astype(F32), NN, EXACT)
    residual = res_ref[...]
    scale = lax.rsqrt(jnp.mean(residual * residual, axis=-1, keepdims=True) + EPS)
    normed = residual * scale
    second = jnp.sum(grad_normed * normed, axis=0, keepdims=True)
    spare = jnp.zeros((vectors_ref.shape[0] - experts - 1, width), F32)
    vectors_ref[...] = jnp.concatenate([router, second, spare], axis=0).astype(BF16)
    scaled = grad_normed * gain_two_ref[...]
    grad_residual = u_ref[...].astype(F32) + scale * (
        scaled - normed * jnp.mean(scaled * normed, axis=-1, keepdims=True)
    )
    gres_ref[...] = grad_residual
    grad_mixed = grad_residual.astype(BF16)
    mixed_ref[...] = grad_mixed
    for tile in range(TILES):
        grad_att = mul(grad_mixed, wo_ref[tile * 256 : (tile + 1) * 256, :], NT)
        for piece in range(pieces):
            rows = slice(piece * BLOCK, (piece + 1) * BLOCK)
            gaz_ref[piece, tile] = spread_heads(
                grad_att[rows, :LANES], grad_att[rows, LANES:]
            ).astype(BF16)


def attention_back_kernel(
    members,
    experts,
    me_ref,
    qz_ref,
    gaz_ref,
    k_ref,
    v_ref,
    *refs,
):
    pieces = gaz_ref.shape[0]
    attention_back_body(
        members, experts, me_ref, qz_ref, gaz_ref, k_ref, v_ref, refs[:pieces], *refs[pieces:]
    )


def attention_back_body(
    members,
    experts,
    me_ref,
    qz_ref,
    gaz_ref,
    k_ref,
    v_ref,
    probs_refs,
    cos_ref,
    sin_ref,
    mix_ref,
    own_ref,
    att_ref,
    mixed_ref,
    vectors_ref,
    wq_ref,
    wk_ref,
    wv_ref,
    gain_one_ref,
    *rest,
):
    dq_ref, dkv_ref, weights_ref, dk_acc, dv_acc, row_ref = rest[-6:]
    member = me_ref[0]
    tokens = own_ref.shape[0]
    pieces = tokens // BLOCK
    length = k_ref.shape[0]
    inner = k_ref.shape[1]
    dk_acc[...] = jnp.zeros_like(dk_acc)
    dv_acc[...] = jnp.zeros_like(dv_acc)
    for piece in range(pieces):
        keys = (piece + 1) * members * BLOCK
        rows = slice(piece * BLOCK, (piece + 1) * BLOCK)
        at = pl.ds(pl.multiple_of((piece * members + member) * BLOCK, BLOCK), BLOCK)

        def step(tile, carry):
            lanes = pl.ds(pl.multiple_of(tile * LANES, LANES), LANES)
            stacked, grads = qz_ref[piece, tile], gaz_ref[piece, tile]
            key_tile = k_ref[:keys, lanes]
            low_probs = probs_refs[piece][tile]
            probs = low_probs.astype(F32)
            weighted = probs * mul(grads, v_ref[:keys, lanes], NT)
            delta = jnp.sum(weighted, axis=-1, keepdims=True)
            grad_scores = (weighted - probs * delta).astype(BF16)
            dk_acc[:keys, lanes] += mul(grad_scores, stacked, TN)
            dv_acc[:keys, lanes] += mul(low_probs, grads, TN)
            first, second = gather_heads(mul(grad_scores, key_tile) * HEAD_DIM**-0.5)
            cosine, sine = cos_ref[at, :], sin_ref[at, :]
            out = pl.multiple_of(tile * 256, 256)
            dq_ref[rows, pl.ds(out, LANES)] = unrotate(first, cosine, sine).astype(BF16)
            dq_ref[rows, pl.ds(out + LANES, LANES)] = unrotate(second, cosine, sine).astype(BF16)
            return carry

        lax.fori_loop(0, TILES, step, 0)
    for block in range(length // BLOCK):
        rows = slice(block * BLOCK, (block + 1) * BLOCK)
        cosine, sine = cos_ref[rows, :], sin_ref[rows, :]
        for tile in range(TILES):
            lanes = slice(tile * LANES, (tile + 1) * LANES)
            row_ref[rows, lanes] = unrotate(dk_acc[rows, lanes], cosine, sine).astype(BF16)
        row_ref[rows, inner:] = dv_acc[rows, :].astype(BF16)
        piece, owner = block // members, block % members
        dkv_ref[owner, piece * BLOCK : (piece + 1) * BLOCK, :] = row_ref[rows, :]
    width = dq_ref.shape[1]
    for i, (left_ref, right_ref) in enumerate(
        ((own_ref, dq_ref), (mix_ref, row_ref), (att_ref, mixed_ref))
    ):
        product = mul(left_ref[...], right_ref[...], TN)
        weights_ref[i * width : (i + 1) * width, :] = product.astype(BF16)
    first = jnp.sum(mul(dq_ref[...], wq_ref[...], NT) * own_ref[...].astype(F32), axis=0, keepdims=True)
    for at in range(0, length, tokens):
        rows = slice(at, at + tokens)
        grad_mixer = mul(row_ref[rows, :inner], wk_ref[...], NT)
        grad_mixer += mul(row_ref[rows, inner:], wv_ref[...], NT)
        first += jnp.sum(grad_mixer * mix_ref[rows, :].astype(F32), axis=0, keepdims=True)
    first = first / gain_one_ref[...]
    vectors = vectors_ref[...].astype(F32)
    place = lax.broadcasted_iota(jnp.int32, vectors.shape, 0)
    weights_ref[3 * width :, :] = jnp.where(place == experts + 1, first, vectors).astype(BF16)


def last_kernel(
    members,
    dq_ref,
    *refs,
):
    last_body(dq_ref, refs[:members], *refs[members:])


def last_body(
    dq_ref,
    dkv_refs,
    wq_ref,
    wk_ref,
    wv_ref,
    input_ref,
    gres_ref,
    gain_one_ref,
    *rest,
):
    gh_ref = rest[-1]
    inner = wk_ref.shape[1]
    grad_kv = sum(dkv_ref[...].astype(F32) for dkv_ref in dkv_refs).astype(BF16)
    grad_mixer = (
        mul(dq_ref[...], wq_ref[...], NT)
        + mul(grad_kv[:, :inner], wk_ref[...], NT)
        + mul(grad_kv[:, inner:], wv_ref[...], NT)
    )
    x = input_ref[...].astype(F32)
    scale = lax.rsqrt(jnp.mean(x * x, axis=-1, keepdims=True) + EPS)
    normed = x * scale
    scaled = grad_mixer * gain_one_ref[...]
    gh_ref[...] = (
        gres_ref[...]
        + scale * (scaled - normed * jnp.mean(scaled * normed, axis=-1, keepdims=True))
    ).astype(gh_ref.dtype)


def rope_tables(places):
    middle = HEAD_DIM // 2
    frequency = jnp.exp(jnp.arange(middle, dtype=F32) * (-2.0 * math.log(THETA) / HEAD_DIM))
    angles = places.astype(F32)[:, None] * frequency
    cosine, sine = jnp.cos(angles), jnp.sin(angles)
    return (
        jnp.concatenate([cosine] * 4, axis=1),
        jnp.concatenate([-sine, sine, -sine, sine], axis=1),
    )


def local(
    hidden_in,
    segment_ids,
    positions,
    expert_ids,
    first_gain,
    query_weight,
    key_weight,
    value_weight,
    output_weight,
    second_gain,
    router_weight,
    gate_weight,
    up_weight,
    down_weight,
    out_grad,
):
    rows_here, block, width = hidden_in.shape
    tokens = rows_here * block
    shards = lax.axis_size("seq")
    members = shards // rows_here
    length = shards * block
    inner = key_weight.shape[1]
    expert_count = router_weight.shape[1]
    experts, _, hidden = gate_weight.shape
    me = lax.axis_index("seq")
    row, member = me // members, me % members
    me_pair = jnp.stack([member, me]).astype(jnp.int32)
    same_member = [[r * members + m for r in range(rows_here)] for m in range(members)]
    same_row = [[r * members + m for m in range(members)] for r in range(rows_here)]
    slots = tokens * MOST // BLOCK

    meta = jnp.concatenate(
        [positions.reshape(1, tokens), expert_ids.reshape(tokens, TOPK).T], axis=0
    )
    row_in = lax.all_to_all(jnp.repeat(hidden_in, members, axis=0), "seq", 0, 0, tiled=True)
    row_in = row_in.reshape(length, width)
    def onward(values, count):
        to = lambda j: (j // members + count) % rows_here * members + j % members
        return lax.ppermute(values, "seq", [(j, to(j)) for j in range(shards)])

    def across(values, other):
        return lax.ppermute(values, "seq", [(j, j ^ other) for j in range(shards)])

    def row_swap(values, other):
        count = lax.axis_size("rows")
        return lax.ppermute(values, "rows", [(j, j ^ other) for j in range(count)])

    def gather(values):
        found = []
        for k in range(rows_here):
            values = onward(values, 1) if k else values
            found.append([values] + [across(values, other) for other in range(1, members)])
        return found

    def joined(part):
        return add(part[0], *(across(part[o], o) for o in range(1, members)))

    def scatter(sums):
        return add(*(onward(total, rows_here - k) if k else total for k, total in enumerate(sums)))

    core = lax.axis_index("rows") % 2

    of_row = lambda k: lax.dynamic_index_in_dim(hidden_in, (row + k) % rows_here, 0, keepdims=False)
    row_in = [of_row(k) for k in range(rows_here)]
    meta = after([jnp.broadcast_to(meta[None], (shards,) + meta.shape)], *row_in)[0]
    meta = lax.all_to_all(meta, "seq", 0, 0, tiled=True)
    row_in = row_in[:1] + [onward(row_in[k], k) for k in range(1, rows_here)]
    row_in = [[v] + [across(v, other) for other in range(1, members)] for v in row_in]
    row_in = [v for blocks in row_in for v in blocks]
    places = [
        (row - k) % rows_here * members + (member ^ other)
        for k in range(rows_here)
        for other in range(members)
    ]
    me_row = jnp.stack([member, me] + places).astype(jnp.int32)
    upstream = lax.all_gather(out_grad, "seq", axis=0, tiled=False)
    upstream = upstream.reshape(rows_here, members, rows_here, block, width)
    stored = [
        pltpu.with_memory_space_constraint(v, pltpu.HBM)
        for v in (upstream, gate_weight, up_weight, down_weight)
    ]

    meta = meta.reshape(rows_here, members, TOPK + 1, rows_here, block)
    row_meta = lax.dynamic_index_in_dim(meta, row, 3, keepdims=False)
    own_meta = lax.dynamic_index_in_dim(row_meta, member, 1, keepdims=False)
    cosine, sine = rope_tables(row_meta[:, :, 0].reshape(length))
    own_pos = own_meta[:, 0].reshape(tokens, 1)
    own_ids = own_meta[:, 1:].transpose(1, 0, 2).reshape(TOPK, tokens)
    lane = jnp.arange(8, dtype=jnp.int32)
    wanted = jnp.where(lane < experts, me * experts + lane, -1)
    named = jnp.any(
        meta[:, :, 1:, None] == wanted[None, None, None, :, None, None], axis=2
    )
    named = named.transpose(3, 1, 2, 0, 4).reshape(shards, 8, tokens).astype(F32)

    gain_one, gain_two = first_gain.reshape(1, width), second_gain.reshape(1, width)
    router = router_weight.T
    mix, own_mix, qz, k_row, v_row, att, residual, xg, gates, own_in, *probs = pl.pallas_call(
        functools.partial(front_kernel, members, shards),
        out_shape=[
            struct((length, width), BF16),
            struct((tokens, width), BF16),
            struct((rows_here, TILES, 4 * BLOCK, LANES), BF16),
            struct((length, inner), BF16),
            struct((length, inner), BF16),
            struct((tokens, width), BF16),
            struct((tokens, width), F32),
            struct((tokens + PAD, width), BF16),
            struct((expert_count, tokens), F32),
            struct((tokens, width), BF16),
        ]
        + [
            struct((TILES, 4 * BLOCK, (piece + 1) * members * BLOCK), BF16)
            for piece in range(rows_here)
        ],
        in_specs=[scalars()] + [whole()] * (shards + 11),
        out_specs=[whole()] * (10 + rows_here),
        scratch_shapes=[pltpu.VMEM((length, width), BF16)],
        compiler_params=params(56),
        cost_estimate=took(19.5),
        name="front",
    )(
        me_row,
        *row_in,
        cosine,
        sine,
        own_pos,
        own_ids,
        gain_one,
        query_weight,
        key_weight,
        value_weight,
        output_weight,
        gain_two,
        router,
    )

    per_row = members // PAIR
    one_on = onward(xg, 1)
    beside = [across(xg, other) for other in range(1, members)]
    one_on = after([one_on], *beside)[0]
    sets = [[xg] + beside, [one_on] + [across(one_on, other) for other in range(1, members)]]
    two_on = onward(one_on, 1)
    wide, narrow = experts * slots, hidden
    kept = []
    order = list(range(rows_here))
    dx_parts, dx_sums = [[] for _ in order], []
    for k in order:
        group = sets[k]
        tied = []
        for q in range(members // PAIR):
            pair = (row - k) % rows_here * per_row + ((member // PAIR) ^ q)
            info = [member % PAIR, me, pair, (row - k) % rows_here, (member // PAIR) ^ q]
            info = jnp.stack(info).astype(jnp.int32)
            flat = lambda *shape: pl.BlockSpec(shape, lambda e, info: (0,) * len(shape))
            of_pair = lambda w: pl.BlockSpec((PAIR, slots, w), lambda e, info: (info[2], e, 0))
            of_expert = lambda a, b: pl.BlockSpec((1, a, b), lambda e, info: (e, 0, 0))
            outcome = pl.pallas_call(
                functools.partial(expert_kernel, len(kept) + len(tied)),
                grid_spec=pltpu.PrefetchScalarGridSpec(
                    num_scalar_prefetch=1,
                    grid=(experts,),
                    in_specs=[
                        flat(tokens + PAD, width),
                        flat(tokens + PAD, width),
                        pl.BlockSpec((PAIR, 8, tokens), lambda e, info: (info[2], 0, 0)),
                        pl.BlockSpec(
                            (rows_here, PAIR, 1, block, width),
                            lambda e, info: (0, info[4], info[3], 0, 0),
                        ),
                        of_expert(width, hidden),
                        of_expert(width, hidden),
                        of_expert(hidden, width),
                    ]
                    + [pl.BlockSpec(memory_space=pl.ANY)] * (len(kept) + len(tied)),
                    out_specs=[
                        flat(tokens + PAD, width),
                        flat(tokens + PAD, width),
                        pl.BlockSpec(
                            (PAIR, 1, tokens, width), lambda e, info: (info[4], info[3], 0, 0)
                        ),
                        of_pair(width),
                        of_pair(width),
                        of_pair(hidden),
                        of_pair(hidden),
                        of_pair(hidden),
                    ],
                    scratch_shapes=[
                        pltpu.VMEM((PAIR, wide, width), BF16),
                        pltpu.VMEM((PAIR, wide, width), BF16),
                        pltpu.VMEM((PAIR, wide, tokens), BF16),
                        pltpu.VMEM((PAIR, 8, tokens), F32),
                        pltpu.VMEM((8, tokens), F32),
                        pltpu.VMEM((PAIR, PAD, width), F32),
                    ],
                ),
                out_shape=[
                    struct((tokens + PAD, width), BF16),
                    struct((tokens + PAD, width), BF16),
                    pltpu.HBM((members, rows_here, tokens, width), BF16),
                    pltpu.HBM((shards, wide, width), BF16),
                    pltpu.HBM((shards, wide, width), BF16),
                    pltpu.HBM((shards, wide, hidden), BF16),
                    pltpu.HBM((shards, wide, hidden), BF16),
                    pltpu.HBM((shards, wide, hidden), BF16),
                ],
                input_output_aliases={8 + i: 2 + i for i in range(len(kept))},
                compiler_params=params(40),
                cost_estimate=took(16),
                name="experts",
            )(
                info,
                group[2 * q],
                group[2 * q + 1],
                named,
                *stored,
                *kept,
                *tied,
            )
            dx_parts[k] += outcome[:2]
            kept = outcome[2:]
        part = dx_parts[k]
        if k == 0:
            values = after([two_on], part[0])[0]
            for i in range(2, rows_here):
                values = onward(values, 1) if i > 2 else values
                sets.append([values] + [across(values, other) for other in range(1, members)])
        if k < 2:
            part = part[:1] + list(after(part[1:], *sets[rows_here - 1][1:]))
        dx_sums.append(joined(part))
    sent = [dx_sums[0]] + [onward(dx_sums[k], rows_here - k) for k in range(1, rows_here)]
    dx_sum = add(*sent)

    info = jnp.stack([member % PAIR, me, me, core]).astype(jnp.int32)
    halves = (3, width // 2, hidden)
    one_expert = lambda w: pl.BlockSpec((shards, slots, w), lambda i: (0, i, 0))
    half = pl.BlockSpec((1,) + halves, lambda i: (i, 0, 0, 0))
    keep, send = pl.pallas_call(
        expert_grads_kernel,
        grid=(experts,),
        out_shape=[struct((experts,) + halves, BF16)] * 2,
        in_specs=[scalars(), one_expert(width), one_expert(width)]
        + [one_expert(hidden)] * 3
        + [pl.BlockSpec(memory_space=pl.ANY)] * 2,
        out_specs=[half] * 2,
        compiler_params=params(60),
        cost_estimate=took(60),
        name="expert_grads",
    )(info, *kept[1:], dx_sums[2], dx_sums[3])
    part_of = lambda values, m: lax.dynamic_index_in_dim(values, m, 0, keepdims=False)
    y_all = after([kept[0]], dx_sums[3])[0]
    middle_row = rows_here // 2
    y_near = [
        [across(part_of(y_all, member ^ o)[:middle_row], o) for o in range(1, members)],
        [across(part_of(y_all, member ^ o)[middle_row:], o) for o in range(1, members)],
    ]
    soon = y_near[0]
    own_upstream = lax.dynamic_index_in_dim(upstream, row, 2, keepdims=False)
    own_upstream = lax.dynamic_index_in_dim(own_upstream, member, 1, keepdims=False)
    own_upstream = own_upstream.reshape(tokens, width)
    vectors, grad_mixed, grad_residual, gaz = pl.pallas_call(
        middle_kernel,
        out_shape=[
            struct((EXTRA, width), BF16),
            struct((tokens, width), BF16),
            struct((tokens, width), F32),
            struct((rows_here, TILES, 4 * BLOCK, LANES), BF16),
        ],
        in_specs=[whole()] * 8 + [pl.BlockSpec(memory_space=pl.ANY)] * (1 + len(soon)),
        out_specs=[whole()] * 4,
        compiler_params=params(48),
        cost_estimate=took(6),
        name="middle",
    )(dx_sum, own_upstream, xg, residual, gates, gain_two, router, output_weight, keep, *soon)

    dq, dkv, weights = pl.pallas_call(
        functools.partial(attention_back_kernel, members, expert_count),
        out_shape=[
            struct((tokens, width), BF16),
            struct((members, tokens, width), BF16),
            struct((3 * width + EXTRA, width), BF16),
        ],
        in_specs=[scalars()]
        + [whole()] * (15 + rows_here)
        + [pl.BlockSpec(memory_space=pl.ANY)],
        out_specs=[whole()] * 3,
        scratch_shapes=[
            pltpu.VMEM((length, inner), F32),
            pltpu.VMEM((length, inner), F32),
            pltpu.VMEM((length, width), BF16),
        ],
        compiler_params=params(58),
        cost_estimate=took(0.1),
        name="attention_back",
    )(
        me_pair,
        qz,
        gaz,
        k_row,
        v_row,
        *probs,
        cosine,
        sine,
        mix,
        own_mix,
        att,
        grad_mixed,
        vectors,
        query_weight,
        key_weight,
        value_weight,
        gain_one,
        gain_one,
    )
    received = row_swap(after([send], gaz)[0], 1)
    kept_half = after([keep], dq)[0]
    mine = [plus(kept_half, received, i) for i in range(experts)]
    crossed = [row_swap(m, 2) for m in mine]
    dkv = [part_of(dkv, member)] + [across(part_of(dkv, member ^ o), o) for o in range(1, members)]
    grad_in = pl.pallas_call(
        functools.partial(last_kernel, members),
        out_shape=struct((tokens, width), BF16),
        in_specs=[whole()] * (7 + members) + [pl.BlockSpec(memory_space=pl.ANY)] * len(y_near[1]),
        out_specs=whole(),
        compiler_params=params(48),
        cost_estimate=took(0.1),
        name="last",
    )(dq, *dkv, query_weight, key_weight, value_weight, own_in, grad_residual, gain_one, *y_near[1])

    y_near = [jnp.concatenate(halves, axis=0) for halves in zip(*y_near)]
    y_total = add(after([part_of(y_all, member)], dq)[0], *y_near)
    y_parts = [part_of(y_total, (row - k) % rows_here) for k in range(rows_here)]
    y_sum = scatter(y_parts)
    hidden_out = (residual + y_sum.astype(F32)).astype(BF16)
    back = lambda values: lax.all_to_all(
        values.reshape(rows_here, block, width), "seq", 0, 0, tiled=True, axis_index_groups=same_member
    )
    hidden_out, grad_in = back(hidden_out), back(grad_in)
    finished = []
    for e in range(experts):
        crossed[e] = after([crossed[e]], grad_in)[0] if e == 3 else crossed[e]
        mine[e] = plus(mine[e], crossed[e])
        grad_spec = lambda a, b: pl.BlockSpec((1, a, b), lambda i, e=e: (e, 0, 0))
        half = pl.BlockSpec(halves, lambda i: (0, 0, 0))
        finished = pl.pallas_call(
            functools.partial(finish_kernel, len(finished)),
            grid=(1,),
            out_shape=[
                pltpu.HBM((experts, width, hidden), F32),
                pltpu.HBM((experts, width, hidden), F32),
                pltpu.HBM((experts, hidden, width), F32),
            ],
            in_specs=[scalars(), half, half]
            + [pl.BlockSpec(memory_space=pl.ANY)] * len(finished),
            out_specs=[grad_spec(width, hidden), grad_spec(width, hidden), grad_spec(hidden, width)],
            input_output_aliases={3 + i: i for i in range(len(finished))},
            compiler_params=params(60),
            cost_estimate=took(0.1),
            name="finish",
        )(info, mine[e], row_swap(mine[e], 1), *finished)
    shared = lax.psum(weights, ("rows", "seq"))
    step = 128
    part = lambda i: pl.BlockSpec((step, width), lambda r, i=i: (i * (width // step) + r, 0))
    rows_of = lambda w: pl.BlockSpec((step, w), lambda r: (r, 0))
    query_sum, key_sum, value_sum, output_sum, vector_sum = pl.pallas_call(
        spread_kernel,
        grid=(width // step,),
        out_shape=[
            pltpu.HBM((width, width), F32),
            pltpu.HBM((width, inner), F32),
            pltpu.HBM((width, inner), F32),
            pltpu.HBM((width, width), F32),
            struct((EXTRA, width), F32),
        ],
        in_specs=[part(0), part(1), part(2), pl.BlockSpec((EXTRA, width), lambda r: (3 * width // EXTRA, 0))]
        + [pl.BlockSpec(memory_space=pl.ANY)] * 2,
        out_specs=[
            rows_of(width),
            rows_of(inner),
            rows_of(inner),
            rows_of(width),
            pl.BlockSpec((EXTRA, width), lambda r: (0, 0)),
        ],
        compiler_params=params(24),
        cost_estimate=took(0.1),
        name="spread",
    )(*[pltpu.with_memory_space_constraint(shared, pltpu.HBM)] * 4, grad_in, finished[0])
    hidden_out = after([hidden_out], finished[0])[0]
    return (
        hidden_out,
        grad_in.astype(F32),
        vector_sum[expert_count + 1],
        query_sum,
        key_sum,
        value_sum,
        output_sum,
        vector_sum[expert_count],
        vector_sum[:expert_count].T,
        *finished,
    )


def solution(mesh):
    placed = (
        P("rows", "seq", None),
        P("rows", "seq"),
        P("rows", "seq"),
        P("rows", "seq", None),
        P(),
        P(),
        P(),
        P(),
        P(),
        P(),
        P(),
        P("seq", None, None),
        P("seq", None, None),
        P("seq", None, None),
        P("rows", "seq", None),
    )
    return jax.shard_map(
        local,
        mesh=mesh,
        in_specs=placed,
        out_specs=(
            P("rows", "seq", None),
            P("rows", "seq", None),
            P(),
            P(),
            P(),
            P(),
            P(),
            P(),
            P(),
            P("seq", None, None),
            P("seq", None, None),
            P("seq", None, None),
        ),
        check_vma=False,
    )
```

```python
import functools
import math

import jax
import jax.numpy as jnp
from jax import lax
from jax.experimental import pallas as pl
from jax.experimental.pallas import tpu as pltpu
from jax.sharding import PartitionSpec as P

HEADS = 16
KV_HEADS = 8
HEAD_DIM = 64
TOPK = 8
MOST = 32
BLOCK = 64
LANES = 128
TILES = KV_HEADS * HEAD_DIM // LANES
EXTRA = 128
PAIR = 2
PAD = 16

EPS = 1e-06
THETA = 10000.0
NEG = -1e30
F32 = jnp.float32
BF16 = jnp.bfloat16
EXACT = lax.Precision.HIGHEST
NN = (((1,), (0,)), ((), ()))
NT = (((1,), (1,)), ((), ()))
TN = (((0,), (0,)), ((), ()))


def mul(left, right, dims=NN, precision=None):
    return lax.dot_general(left, right, dims, precision=precision, preferred_element_type=F32)


def params(megabytes):
    return pltpu.CompilerParams(vmem_limit_bytes=megabytes << 20)


def whole():
    return pl.BlockSpec(memory_space=pltpu.VMEM)


def scalars():
    return pl.BlockSpec(memory_space=pltpu.SMEM)


def struct(shape, dtype):
    return jax.ShapeDtypeStruct(shape, dtype)


def took(microseconds):
    return pl.CostEstimate(flops=int(microseconds * 0.5e9), bytes_accessed=0, transcendentals=0)


def low_half(shape):
    return lax.broadcasted_iota(jnp.int32, shape, 1) < HEAD_DIM


def swap_halves(tile):
    lane = lax.broadcasted_iota(jnp.int32, tile.shape, 1)
    quarter = HEAD_DIM // 2
    forward = pltpu.roll(tile, LANES - quarter, 1)
    backward = pltpu.roll(tile, quarter, 1)
    return jnp.where(lane % HEAD_DIM < quarter, forward, backward)


def rotate(tile, cosine, signed_sine):
    return tile * cosine + swap_halves(tile) * signed_sine


def unrotate(tile, cosine, signed_sine):
    return tile * cosine - swap_halves(tile) * signed_sine


def spread_heads(first, second):
    low = low_half(first.shape)
    return jnp.concatenate(
        [
            jnp.where(low, first, 0.0),
            jnp.where(low, pltpu.roll(first, HEAD_DIM, 1), 0.0),
            jnp.where(low, 0.0, pltpu.roll(second, HEAD_DIM, 1)),
            jnp.where(low, 0.0, second),
        ],
        axis=0,
    )


def gather_heads(stacked):
    low = low_half((BLOCK, LANES))
    one, two, three, four = (stacked[i * BLOCK : (i + 1) * BLOCK] for i in range(4))
    first = jnp.where(low, one, pltpu.roll(two, HEAD_DIM, 1))
    second = jnp.where(low, pltpu.roll(three, HEAD_DIM, 1), four)
    return first, second


def allowed_keys(piece, members, member, pos_ref):
    keys = (piece + 1) * members * BLOCK
    start = (piece * members + member) * BLOCK
    place = start + lax.broadcasted_iota(jnp.int32, (BLOCK, keys), 0)
    key = lax.broadcasted_iota(jnp.int32, (BLOCK, keys), 1)
    opening = place - pos_ref[piece * BLOCK : (piece + 1) * BLOCK, :]
    return (key <= place) & (key >= opening)


def probabilities(stacked, key_tile, allowed):
    keys = key_tile.shape[0]
    scores = mul(stacked, key_tile, NT)
    scores = scores.reshape(4, BLOCK, keys)
    scores = jnp.where(allowed[None], scores, NEG)
    weights = jnp.exp(scores - jnp.max(scores, axis=-1, keepdims=True))
    probs = weights * (1.0 / jnp.sum(weights, axis=-1, keepdims=True))
    return probs.reshape(4 * BLOCK, keys)


def two_parts(values):
    high = values.astype(BF16).astype(F32)
    return jnp.concatenate([high, values - high], axis=0).astype(BF16)


def front_kernel(
    members,
    blocks,
    me_ref,
    *refs,
):
    front_body(members, me_ref, refs[:blocks], *refs[blocks:])


def front_body(
    members,
    me_ref,
    block_refs,
    cos_ref,
    sin_ref,
    pos_ref,
    ids_ref,
    gain_one_ref,
    wq_ref,
    wk_ref,
    wv_ref,
    wo_ref,
    gain_two_ref,
    router_ref,
    mix_ref,
    own_ref,
    qz_ref,
    k_ref,
    v_ref,
    att_ref,
    res_ref,
    xg_ref,
    gates_ref,
    input_ref,
    *rest,
):
    probs_refs, h_ref = rest[:-1], rest[-1]
    member = me_ref[0]
    length, width = h_ref.shape
    tokens = own_ref.shape[0]
    pieces = tokens // BLOCK
    step = 256
    for i, block_ref in enumerate(block_refs):
        h_ref[pl.ds(pl.multiple_of(me_ref[2 + i] * BLOCK, BLOCK), BLOCK), :] = block_ref[...]

    def keys_step(i, carry):
        rows = pl.ds(pl.multiple_of(i * step, step), step)
        x = h_ref[rows, :].astype(F32)
        scale = lax.rsqrt(jnp.mean(x * x, axis=-1, keepdims=True) + EPS)
        mix = (x * scale * gain_one_ref[...]).astype(BF16)
        mix_ref[rows, :] = mix
        v_ref[rows, :] = mul(mix, wv_ref[...]).astype(BF16)
        pre = mul(mix, wk_ref[...])
        cosine, sine = cos_ref[rows, :], sin_ref[rows, :]
        for tile in range(TILES):
            lanes = slice(tile * LANES, (tile + 1) * LANES)
            k_ref[rows, lanes] = rotate(pre[:, lanes], cosine, sine).astype(BF16)
        return carry

    lax.fori_loop(0, length // step, keys_step, 0)
    own = [pl.ds(pl.multiple_of((p * members + member) * BLOCK, BLOCK), BLOCK) for p in range(pieces)]
    for piece in range(pieces):
        rows = slice(piece * BLOCK, (piece + 1) * BLOCK)
        own_ref[rows, :] = mix_ref[own[piece], :]
        input_ref[rows, :] = h_ref[own[piece], :]

    def query_step(tile, carry):
        pre = mul(own_ref[...], wq_ref[:, pl.ds(pl.multiple_of(tile * 256, 256), 256)])
        for piece in range(pieces):
            rows = slice(piece * BLOCK, (piece + 1) * BLOCK)
            cosine, sine = cos_ref[own[piece], :], sin_ref[own[piece], :]
            first = rotate(pre[rows, :LANES], cosine, sine)
            second = rotate(pre[rows, LANES:], cosine, sine)
            qz_ref[piece, tile] = (spread_heads(first, second) * HEAD_DIM**-0.5).astype(BF16)
        return carry

    lax.fori_loop(0, TILES, query_step, 0)
    for piece in range(pieces):
        allowed = allowed_keys(piece, members, member, pos_ref)
        keys = allowed.shape[1]
        rows = slice(piece * BLOCK, (piece + 1) * BLOCK)

        def attend(tile, carry):
            lanes = pl.ds(pl.multiple_of(tile * LANES, LANES), LANES)
            probs = probabilities(qz_ref[piece, tile], k_ref[:keys, lanes], allowed)
            probs = probs.astype(BF16)
            probs_refs[piece][tile] = probs
            first, second = gather_heads(mul(probs, v_ref[:keys, lanes]))
            at = pl.multiple_of(tile * 256, 256)
            att_ref[rows, pl.ds(at, LANES)] = first.astype(BF16)
            att_ref[rows, pl.ds(at + LANES, LANES)] = second.astype(BF16)
            return carry

        lax.fori_loop(0, TILES, attend, 0)
    mixed = mul(att_ref[...], wo_ref[...])
    residual = input_ref[...].astype(F32) + mixed
    res_ref[...] = residual
    scale = lax.rsqrt(jnp.mean(residual * residual, axis=-1, keepdims=True) + EPS)
    chosen = (residual * scale * gain_two_ref[...]).astype(BF16)
    xg_ref[:tokens, :] = chosen
    logits = mul(router_ref[...], chosen, NT)
    expert = lax.broadcasted_iota(jnp.int32, logits.shape, 0)
    named = expert == ids_ref[0:1, :]
    for k in range(1, TOPK):
        named = named | (expert == ids_ref[k : k + 1, :])
    logits = jnp.where(named, logits, NEG)
    weights = jnp.where(named, jnp.exp(logits - jnp.max(logits, axis=0, keepdims=True)), 0.0)
    gates = weights / jnp.sum(weights, axis=0, keepdims=True)
    gates_ref[...] = gates
    for part in range(logits.shape[0] // 8):
        lanes = slice(part * tokens, (part + 1) * tokens)
        xg_ref[tokens:, lanes] = two_parts(gates[part * 8 : (part + 1) * 8])


def one_hot(slot_row, rows):
    slot = lax.broadcasted_iota(jnp.int32, (rows, slot_row.shape[1]), 0).astype(F32)
    return slot == slot_row


def expert_kernel(
    kept,
    info_ref,
    xa_ref,
    xb_ref,
    named_ref,
    u_ref,
    wg_ref,
    wu_ref,
    wd_ref,
    *rest,
):
    (dxa_ref, dxb_ref) = rest[kept : kept + 2]
    (y_ref, xs_ref, us_ref, hs_ref, dg_ref, du_ref) = rest[kept + 2 : kept + 8]
    (dxs_ref, ys_ref, pick_ref, slot_ref, gates_ref, back_ref) = rest[kept + 8 :]
    e = pl.program_id(0)
    experts = pl.num_programs(0)
    tokens = named_ref.shape[2]
    width = xa_ref.shape[1]
    rows = tokens * MOST // BLOCK
    places = [(info_ref[0] + c) % PAIR for c in range(PAIR)]
    sources = (xa_ref, xb_ref)

    @pl.when(e == 0)
    def _():
        back_ref[...] = jnp.zeros_like(back_ref)
        earlier = lax.broadcasted_iota(jnp.int32, (tokens, tokens), 0)
        later = lax.broadcasted_iota(jnp.int32, (tokens, tokens), 1)
        before = (earlier < later).astype(F32).astype(BF16)
        for c in range(PAIR):
            named = named_ref[places[c]]
            slot_ref[c] = jnp.where(named > 0, mul(named.astype(BF16), before), -1.0)

    at = pl.ds(pl.multiple_of(e * rows, rows), rows)
    number = info_ref[1] * experts + e
    row = lax.rem(number, 8)
    lanes = pl.ds(pl.multiple_of(lax.div(number, 8) * tokens, tokens), tokens)
    entering, leaving, gate = [], [], []
    for c in range(PAIR):
        hot = one_hot(slot_ref[c, pl.ds(e, 1), :], rows)
        pick = hot.astype(F32).astype(BF16)
        pick_ref[c, at, :] = pick
        picked = mul(pick, sources[c][:tokens, :]).astype(BF16)
        xs_ref[places[c]] = picked
        entering.append(picked)
        picked = mul(pick, u_ref[:, places[c], 0].reshape(tokens, width)).astype(BF16)
        us_ref[places[c]] = picked
        leaving.append(picked)
        sent = sources[c][tokens:, lanes].astype(F32)
        gates_ref[...] = sent[:8] + sent[8:]
        gate.append(jnp.sum(jnp.where(hot, gates_ref[pl.ds(row, 1), :], 0.0), axis=1, keepdims=True))
    entering = jnp.concatenate(entering, axis=0)
    gate = jnp.concatenate(gate, axis=0)
    gate_pre = mul(entering, wg_ref[0])
    up_pre = mul(entering, wu_ref[0])
    product = mul(jnp.concatenate(leaving, axis=0), wd_ref[0], NT)
    share = 0.5 * jnp.tanh(0.5 * gate_pre) + 0.5
    silu = gate_pre * share
    hidden = silu * up_pre
    grad_gate = jnp.sum(hidden * product, axis=1, keepdims=True)
    grad_act = gate * product
    grad_gate_pre = (grad_act * up_pre * share * (1.0 + gate_pre * (1.0 - share))).astype(BF16)
    grad_up_pre = (grad_act * silu).astype(BF16)
    gated = (gate * hidden).astype(BF16)
    grad_rows = (mul(grad_gate_pre, wg_ref[0], NT) + mul(grad_up_pre, wu_ref[0], NT)).astype(BF16)
    out_rows = mul(gated, wd_ref[0]).astype(BF16)
    for c in range(PAIR):
        part = slice(c * rows, (c + 1) * rows)
        hs_ref[places[c]] = gated[part]
        dg_ref[places[c]] = grad_gate_pre[part]
        du_ref[places[c]] = grad_up_pre[part]
        dxs_ref[c, at, :] = grad_rows[part]
        ys_ref[c, at, :] = out_rows[part]
        hot = one_hot(slot_ref[c, pl.ds(e, 1), :], rows)
        returned = jnp.sum(jnp.where(hot, grad_gate[part], 0.0), axis=0, keepdims=True)
        high = returned.astype(BF16).astype(F32)
        back_ref[c, pl.ds(row, 1), lanes] = high
        back_ref[c, pl.ds(row + 8, 1), lanes] = returned - high

    @pl.when(e == experts - 1)
    def _():
        for c, dx_ref in enumerate((dxa_ref, dxb_ref)):
            dx_ref[:tokens, :] = mul(pick_ref[c], dxs_ref[c], TN).astype(BF16)
            dx_ref[tokens:, :] = back_ref[c].astype(BF16)
            y_ref[places[c], 0] = mul(pick_ref[c], ys_ref[c], TN).astype(BF16)


def expert_grads_kernel(info_ref, xs_ref, us_ref, hs_ref, dg_ref, du_ref, *rest):
    keep_ref, send_ref = rest[-2:]
    core = info_ref[3]
    group, rows, width = xs_ref.shape
    inner = hs_ref.shape[2]
    flat = lambda ref: ref[...].reshape(group * rows, ref.shape[2])

    for half, out_ref in ((core, keep_ref), (1 - core, send_ref)):
        step = min(256, width // 2)
        for at in range(0, width // 2, step):
            lanes = pl.ds(pl.multiple_of(half * (width // 2) + at, LANES), step)
            entering = xs_ref[:, :, lanes].reshape(group * rows, step)
            out_ref[0, 0, at : at + step, :] = mul(entering, flat(dg_ref), TN).astype(BF16)
            out_ref[0, 1, at : at + step, :] = mul(entering, flat(du_ref), TN).astype(BF16)
        step = inner // 2
        lanes = pl.ds(pl.multiple_of(half * step, LANES), step)
        gated = hs_ref[:, :, lanes].reshape(group * rows, step)
        product = mul(gated, flat(us_ref), TN).astype(BF16)
        out_ref[0, 2, :step, :] = product[:, :inner]
        out_ref[0, 2, step:, :] = product[:, inner:]


def finish_kernel(kept, info_ref, mine_ref, other_ref, *rest):
    gate_ref, up_ref, down_ref = rest[kept:]
    core = info_ref[3]
    half = mine_ref.shape[1]
    inner = mine_ref.shape[2]
    for source, place in ((mine_ref, core), (other_ref, 1 - core)):
        rows = pl.ds(pl.multiple_of(place * half, half), half)
        gate_ref[0, rows, :] = source[0].astype(F32)
        up_ref[0, rows, :] = source[1].astype(F32)
        rows = pl.ds(pl.multiple_of(place * (half // 2), half // 2), half // 2)
        down_ref[0, rows, :inner] = source[2, : half // 2].astype(F32)
        down_ref[0, rows, inner:] = source[2, half // 2 :].astype(F32)


def spread_kernel(query_ref, keyval_ref, output_ref, vectors_ref, *rest):
    sums = rest[-5:]
    inner = sums[1].shape[1]
    sums[0][...] = query_ref[...].astype(F32)
    sums[1][...] = keyval_ref[:, :inner].astype(F32)
    sums[2][...] = keyval_ref[:, inner:].astype(F32)
    sums[3][...] = output_ref[...].astype(F32)

    @pl.when(pl.program_id(0) == 0)
    def _():
        sums[4][...] = vectors_ref[...].astype(F32)


def add(*terms):
    return sum(term.astype(F32) for term in terms).astype(terms[0].dtype)


def plus_kernel(left_ref, right_ref, out_ref):
    total = left_ref[...].astype(F32) + right_ref[...].astype(F32)
    out_ref[...] = total.reshape(out_ref.shape).astype(out_ref.dtype)


def plus(left, right, at=None):
    parts, rows, columns = left.shape[-3:]
    entry = pl.BlockSpec((1, rows, columns), lambda i: (i, 0, 0))
    source = entry if at is None else pl.BlockSpec((1, 1, rows, columns), lambda i: (at, i, 0, 0))
    return pl.pallas_call(
        plus_kernel,
        grid=(parts,),
        out_shape=struct((parts, rows, columns), left.dtype),
        in_specs=[source, source],
        out_specs=entry,
        compiler_params=params(56),
        cost_estimate=took(0.1),
        name="plus",
    )(left, right)


def after(values, *others):
    anywhere = pl.BlockSpec(memory_space=pl.ANY)
    return pl.pallas_call(
        lambda *refs: None,
        out_shape=[struct(v.shape, v.dtype) for v in values],
        in_specs=[anywhere] * (len(values) + len(others)),
        out_specs=[anywhere] * len(values),
        input_output_aliases={i: i for i in range(len(values))},
        name="after",
    )(*values, *others)


def put_block(whole_array, block, *at):
    for _ in range(whole_array.ndim - block.ndim):
        block = block[None]
    return lax.dynamic_update_slice(
        whole_array, block, tuple(at) + (0,) * (whole_array.ndim - len(at))
    )


def middle_kernel(
    dx_ref,
    u_ref,
    xg_ref,
    res_ref,
    gates_ref,
    gain_two_ref,
    router_ref,
    wo_ref,
    *rest,
):
    vectors_ref, mixed_ref, gres_ref, gaz_ref = rest[-4:]
    tokens, width = u_ref.shape
    experts = gates_ref.shape[0]
    pieces = tokens // BLOCK
    parts = []
    for part in range(experts // 8):
        sent = dx_ref[tokens:, part * tokens : (part + 1) * tokens].astype(F32)
        parts.append(sent[:8] + sent[8:])
    grad_gates = jnp.concatenate(parts, axis=0)
    gates = gates_ref[...]
    grad_logits = gates * (grad_gates - jnp.sum(gates * grad_gates, axis=0, keepdims=True))
    grad_normed = dx_ref[:tokens, :].astype(F32) + mul(
        grad_logits, router_ref[...].astype(F32), TN, EXACT
    )
    router = mul(grad_logits, xg_ref[:tokens, :].astype(F32), NN, EXACT)
    residual = res_ref[...]
    scale = lax.rsqrt(jnp.mean(residual * residual, axis=-1, keepdims=True) + EPS)
    normed = residual * scale
    second = jnp.sum(grad_normed * normed, axis=0, keepdims=True)
    spare = jnp.zeros((vectors_ref.shape[0] - experts - 1, width), F32)
    vectors_ref[...] = jnp.concatenate([router, second, spare], axis=0).astype(BF16)
    scaled = grad_normed * gain_two_ref[...]
    grad_residual = u_ref[...].astype(F32) + scale * (
        scaled - normed * jnp.mean(scaled * normed, axis=-1, keepdims=True)
    )
    gres_ref[...] = grad_residual
    grad_mixed = grad_residual.astype(BF16)
    mixed_ref[...] = grad_mixed
    for tile in range(TILES):
        grad_att = mul(grad_mixed, wo_ref[tile * 256 : (tile + 1) * 256, :], NT)
        for piece in range(pieces):
            rows = slice(piece * BLOCK, (piece + 1) * BLOCK)
            gaz_ref[piece, tile] = spread_heads(
                grad_att[rows, :LANES], grad_att[rows, LANES:]
            ).astype(BF16)


def attention_back_kernel(
    members,
    experts,
    me_ref,
    qz_ref,
    gaz_ref,
    k_ref,
    v_ref,
    *refs,
):
    pieces = gaz_ref.shape[0]
    attention_back_body(
        members, experts, me_ref, qz_ref, gaz_ref, k_ref, v_ref, refs[:pieces], *refs[pieces:]
    )


def attention_back_body(
    members,
    experts,
    me_ref,
    qz_ref,
    gaz_ref,
    k_ref,
    v_ref,
    probs_refs,
    cos_ref,
    sin_ref,
    mix_ref,
    own_ref,
    att_ref,
    mixed_ref,
    vectors_ref,
    wq_ref,
    wk_ref,
    wv_ref,
    gain_one_ref,
    *rest,
):
    dq_ref, dkv_ref, weights_ref, dk_acc, dv_acc, row_ref = rest[-6:]
    member = me_ref[0]
    tokens = own_ref.shape[0]
    pieces = tokens // BLOCK
    length = k_ref.shape[0]
    inner = k_ref.shape[1]
    dk_acc[...] = jnp.zeros_like(dk_acc)
    dv_acc[...] = jnp.zeros_like(dv_acc)
    for piece in range(pieces):
        keys = (piece + 1) * members * BLOCK
        rows = slice(piece * BLOCK, (piece + 1) * BLOCK)
        at = pl.ds(pl.multiple_of((piece * members + member) * BLOCK, BLOCK), BLOCK)

        def step(tile, carry):
            lanes = pl.ds(pl.multiple_of(tile * LANES, LANES), LANES)
            stacked, grads = qz_ref[piece, tile], gaz_ref[piece, tile]
            key_tile = k_ref[:keys, lanes]
            low_probs = probs_refs[piece][tile]
            probs = low_probs.astype(F32)
            weighted = probs * mul(grads, v_ref[:keys, lanes], NT)
            delta = jnp.sum(weighted, axis=-1, keepdims=True)
            grad_scores = (weighted - probs * delta).astype(BF16)
            dk_acc[:keys, lanes] += mul(grad_scores, stacked, TN)
            dv_acc[:keys, lanes] += mul(low_probs, grads, TN)
            first, second = gather_heads(mul(grad_scores, key_tile) * HEAD_DIM**-0.5)
            cosine, sine = cos_ref[at, :], sin_ref[at, :]
            out = pl.multiple_of(tile * 256, 256)
            dq_ref[rows, pl.ds(out, LANES)] = unrotate(first, cosine, sine).astype(BF16)
            dq_ref[rows, pl.ds(out + LANES, LANES)] = unrotate(second, cosine, sine).astype(BF16)
            return carry

        lax.fori_loop(0, TILES, step, 0)
    for block in range(length // BLOCK):
        rows = slice(block * BLOCK, (block + 1) * BLOCK)
        cosine, sine = cos_ref[rows, :], sin_ref[rows, :]
        for tile in range(TILES):
            lanes = slice(tile * LANES, (tile + 1) * LANES)
            row_ref[rows, lanes] = unrotate(dk_acc[rows, lanes], cosine, sine).astype(BF16)
        row_ref[rows, inner:] = dv_acc[rows, :].astype(BF16)
        piece, owner = block // members, block % members
        dkv_ref[owner, piece * BLOCK : (piece + 1) * BLOCK, :] = row_ref[rows, :]
    width = dq_ref.shape[1]
    for i, (left_ref, right_ref) in enumerate(
        ((own_ref, dq_ref), (mix_ref, row_ref), (att_ref, mixed_ref))
    ):
        product = mul(left_ref[...], right_ref[...], TN)
        weights_ref[i * width : (i + 1) * width, :] = product.astype(BF16)
    first = jnp.sum(mul(dq_ref[...], wq_ref[...], NT) * own_ref[...].astype(F32), axis=0, keepdims=True)
    for at in range(0, length, tokens):
        rows = slice(at, at + tokens)
        grad_mixer = mul(row_ref[rows, :inner], wk_ref[...], NT)
        grad_mixer += mul(row_ref[rows, inner:], wv_ref[...], NT)
        first += jnp.sum(grad_mixer * mix_ref[rows, :].astype(F32), axis=0, keepdims=True)
    first = first / gain_one_ref[...]
    vectors = vectors_ref[...].astype(F32)
    place = lax.broadcasted_iota(jnp.int32, vectors.shape, 0)
    weights_ref[3 * width :, :] = jnp.where(place == experts + 1, first, vectors).astype(BF16)


def last_kernel(
    members,
    dq_ref,
    *refs,
):
    last_body(dq_ref, refs[:members], *refs[members:])


def last_body(
    dq_ref,
    dkv_refs,
    wq_ref,
    wk_ref,
    wv_ref,
    input_ref,
    gres_ref,
    gain_one_ref,
    *rest,
):
    gh_ref = rest[-1]
    inner = wk_ref.shape[1]
    grad_kv = sum(dkv_ref[...].astype(F32) for dkv_ref in dkv_refs).astype(BF16)
    grad_mixer = (
        mul(dq_ref[...], wq_ref[...], NT)
        + mul(grad_kv[:, :inner], wk_ref[...], NT)
        + mul(grad_kv[:, inner:], wv_ref[...], NT)
    )
    x = input_ref[...].astype(F32)
    scale = lax.rsqrt(jnp.mean(x * x, axis=-1, keepdims=True) + EPS)
    normed = x * scale
    scaled = grad_mixer * gain_one_ref[...]
    gh_ref[...] = (
        gres_ref[...]
        + scale * (scaled - normed * jnp.mean(scaled * normed, axis=-1, keepdims=True))
    ).astype(gh_ref.dtype)


def rope_tables(places):
    middle = HEAD_DIM // 2
    frequency = jnp.exp(jnp.arange(middle, dtype=F32) * (-2.0 * math.log(THETA) / HEAD_DIM))
    angles = places.astype(F32)[:, None] * frequency
    cosine, sine = jnp.cos(angles), jnp.sin(angles)
    return (
        jnp.concatenate([cosine] * 4, axis=1),
        jnp.concatenate([-sine, sine, -sine, sine], axis=1),
    )


def local(
    hidden_in,
    segment_ids,
    positions,
    expert_ids,
    first_gain,
    query_weight,
    key_weight,
    value_weight,
    output_weight,
    second_gain,
    router_weight,
    gate_weight,
    up_weight,
    down_weight,
    out_grad,
):
    rows_here, block, width = hidden_in.shape
    tokens = rows_here * block
    shards = lax.axis_size("seq")
    members = shards // rows_here
    length = shards * block
    inner = key_weight.shape[1]
    expert_count = router_weight.shape[1]
    experts, _, hidden = gate_weight.shape
    me = lax.axis_index("seq")
    row, member = me // members, me % members
    me_pair = jnp.stack([member, me]).astype(jnp.int32)
    same_member = [[r * members + m for r in range(rows_here)] for m in range(members)]
    same_row = [[r * members + m for m in range(members)] for r in range(rows_here)]
    slots = tokens * MOST // BLOCK

    meta = jnp.concatenate(
        [positions.reshape(1, tokens), expert_ids.reshape(tokens, TOPK).T], axis=0
    )
    row_in = lax.all_to_all(jnp.repeat(hidden_in, members, axis=0), "seq", 0, 0, tiled=True)
    row_in = row_in.reshape(length, width)
    def onward(values, count):
        to = lambda j: (j // members + count) % rows_here * members + j % members
        return lax.ppermute(values, "seq", [(j, to(j)) for j in range(shards)])

    def across(values, other):
        return lax.ppermute(values, "seq", [(j, j ^ other) for j in range(shards)])

    def row_swap(values, other):
        count = lax.axis_size("rows")
        return lax.ppermute(values, "rows", [(j, j ^ other) for j in range(count)])

    def gather(values):
        found = []
        for k in range(rows_here):
            values = onward(values, 1) if k else values
            found.append([values] + [across(values, other) for other in range(1, members)])
        return found

    def joined(part):
        return add(part[0], *(across(part[o], o) for o in range(1, members)))

    def scatter(sums):
        return add(*(onward(total, rows_here - k) if k else total for k, total in enumerate(sums)))

    core = lax.axis_index("rows") % 2

    of_row = lambda k: lax.dynamic_index_in_dim(hidden_in, (row + k) % rows_here, 0, keepdims=False)
    row_in = [of_row(k) for k in range(rows_here)]
    meta = after([jnp.broadcast_to(meta[None], (shards,) + meta.shape)], *row_in)[0]
    meta = lax.all_to_all(meta, "seq", 0, 0, tiled=True)
    row_in = row_in[:1] + [onward(row_in[k], k) for k in range(1, rows_here)]
    row_in = [[v] + [across(v, other) for other in range(1, members)] for v in row_in]
    row_in = [v for blocks in row_in for v in blocks]
    places = [
        (row - k) % rows_here * members + (member ^ other)
        for k in range(rows_here)
        for other in range(members)
    ]
    me_row = jnp.stack([member, me] + places).astype(jnp.int32)
    upstream = lax.all_gather(out_grad, "seq", axis=0, tiled=False)
    upstream = upstream.reshape(rows_here, members, rows_here, block, width)
    stored = [
        pltpu.with_memory_space_constraint(v, pltpu.HBM)
        for v in (upstream, gate_weight, up_weight, down_weight)
    ]

    meta = meta.reshape(rows_here, members, TOPK + 1, rows_here, block)
    row_meta = lax.dynamic_index_in_dim(meta, row, 3, keepdims=False)
    own_meta = lax.dynamic_index_in_dim(row_meta, member, 1, keepdims=False)
    cosine, sine = rope_tables(row_meta[:, :, 0].reshape(length))
    own_pos = own_meta[:, 0].reshape(tokens, 1)
    own_ids = own_meta[:, 1:].transpose(1, 0, 2).reshape(TOPK, tokens)
    lane = jnp.arange(8, dtype=jnp.int32)
    wanted = jnp.where(lane < experts, me * experts + lane, -1)
    named = jnp.any(
        meta[:, :, 1:, None] == wanted[None, None, None, :, None, None], axis=2
    )
    named = named.transpose(3, 1, 2, 0, 4).reshape(shards, 8, tokens).astype(F32)

    gain_one, gain_two = first_gain.reshape(1, width), second_gain.reshape(1, width)
    router = router_weight.T
    mix, own_mix, qz, k_row, v_row, att, residual, xg, gates, own_in, *probs = pl.pallas_call(
        functools.partial(front_kernel, members, shards),
        out_shape=[
            struct((length, width), BF16),
            struct((tokens, width), BF16),
            struct((rows_here, TILES, 4 * BLOCK, LANES), BF16),
            struct((length, inner), BF16),
            struct((length, inner), BF16),
            struct((tokens, width), BF16),
            struct((tokens, width), F32),
            struct((tokens + PAD, width), BF16),
            struct((expert_count, tokens), F32),
            struct((tokens, width), BF16),
        ]
        + [
            struct((TILES, 4 * BLOCK, (piece + 1) * members * BLOCK), BF16)
            for piece in range(rows_here)
        ],
        in_specs=[scalars()] + [whole()] * (shards + 11),
        out_specs=[whole()] * (10 + rows_here),
        scratch_shapes=[pltpu.VMEM((length, width), BF16)],
        compiler_params=params(56),
        cost_estimate=took(19.5),
        name="front",
    )(
        me_row,
        *row_in,
        cosine,
        sine,
        own_pos,
        own_ids,
        gain_one,
        query_weight,
        key_weight,
        value_weight,
        output_weight,
        gain_two,
        router,
    )

    per_row = members // PAIR
    one_on = onward(xg, 1)
    beside = [across(xg, other) for other in range(1, members)]
    one_on = after([one_on], *beside)[0]
    sets = [[xg] + beside, [one_on] + [across(one_on, other) for other in range(1, members)]]
    two_on = onward(one_on, 1)
    wide, narrow = experts * slots, hidden
    kept = []
    order = list(range(rows_here))
    dx_parts, dx_sums = [[] for _ in order], []
    for k in order:
        group = sets[k]
        tied = []
        for q in range(members // PAIR):
            pair = (row - k) % rows_here * per_row + ((member // PAIR) ^ q)
            info = [member % PAIR, me, pair, (row - k) % rows_here, (member // PAIR) ^ q]
            info = jnp.stack(info).astype(jnp.int32)
            flat = lambda *shape: pl.BlockSpec(shape, lambda e, info: (0,) * len(shape))
            of_pair = lambda w: pl.BlockSpec((PAIR, slots, w), lambda e, info: (info[2], e, 0))
            of_expert = lambda a, b: pl.BlockSpec((1, a, b), lambda e, info: (e, 0, 0))
            outcome = pl.pallas_call(
                functools.partial(expert_kernel, len(kept) + len(tied)),
                grid_spec=pltpu.PrefetchScalarGridSpec(
                    num_scalar_prefetch=1,
                    grid=(experts,),
                    in_specs=[
                        flat(tokens + PAD, width),
                        flat(tokens + PAD, width),
                        pl.BlockSpec((PAIR, 8, tokens), lambda e, info: (info[2], 0, 0)),
                        pl.BlockSpec(
                            (rows_here, PAIR, 1, block, width),
                            lambda e, info: (0, info[4], info[3], 0, 0),
                        ),
                        of_expert(width, hidden),
                        of_expert(width, hidden),
                        of_expert(hidden, width),
                    ]
                    + [pl.BlockSpec(memory_space=pl.ANY)] * (len(kept) + len(tied)),
                    out_specs=[
                        flat(tokens + PAD, width),
                        flat(tokens + PAD, width),
                        pl.BlockSpec(
                            (PAIR, 1, tokens, width), lambda e, info: (info[4], info[3], 0, 0)
                        ),
                        of_pair(width),
                        of_pair(width),
                        of_pair(hidden),
                        of_pair(hidden),
                        of_pair(hidden),
                    ],
                    scratch_shapes=[
                        pltpu.VMEM((PAIR, wide, width), BF16),
                        pltpu.VMEM((PAIR, wide, width), BF16),
                        pltpu.VMEM((PAIR, wide, tokens), BF16),
                        pltpu.VMEM((PAIR, 8, tokens), F32),
                        pltpu.VMEM((8, tokens), F32),
                        pltpu.VMEM((PAIR, PAD, width), F32),
                    ],
                ),
                out_shape=[
                    struct((tokens + PAD, width), BF16),
                    struct((tokens + PAD, width), BF16),
                    pltpu.HBM((members, rows_here, tokens, width), BF16),
                    pltpu.HBM((shards, wide, width), BF16),
                    pltpu.HBM((shards, wide, width), BF16),
                    pltpu.HBM((shards, wide, hidden), BF16),
                    pltpu.HBM((shards, wide, hidden), BF16),
                    pltpu.HBM((shards, wide, hidden), BF16),
                ],
                input_output_aliases={8 + i: 2 + i for i in range(len(kept))},
                compiler_params=params(40),
                cost_estimate=took(16),
                name="experts",
            )(
                info,
                group[2 * q],
                group[2 * q + 1],
                named,
                *stored,
                *kept,
                *tied,
            )
            dx_parts[k] += outcome[:2]
            kept = outcome[2:]
        part = dx_parts[k]
        if k == 0:
            values = after([two_on], part[0])[0]
            for i in range(2, rows_here):
                values = onward(values, 1) if i > 2 else values
                sets.append([values] + [across(values, other) for other in range(1, members)])
        if k < 2:
            part = part[:1] + list(after(part[1:], *sets[rows_here - 1][1:]))
        dx_sums.append(joined(part))
    sent = [dx_sums[0]] + [onward(dx_sums[k], rows_here - k) for k in range(1, rows_here)]
    dx_sum = add(*sent)

    info = jnp.stack([member % PAIR, me, me, core]).astype(jnp.int32)
    halves = (3, width // 2, hidden)
    one_expert = lambda w: pl.BlockSpec((shards, slots, w), lambda i: (0, i, 0))
    half = pl.BlockSpec((1,) + halves, lambda i: (i, 0, 0, 0))
    keep, send = pl.pallas_call(
        expert_grads_kernel,
        grid=(experts,),
        out_shape=[struct((experts,) + halves, BF16)] * 2,
        in_specs=[scalars(), one_expert(width), one_expert(width)]
        + [one_expert(hidden)] * 3
        + [pl.BlockSpec(memory_space=pl.ANY)] * 2,
        out_specs=[half] * 2,
        compiler_params=params(60),
        cost_estimate=took(60),
        name="expert_grads",
    )(info, *kept[1:], dx_sums[2], dx_sums[3])
    part_of = lambda values, m: lax.dynamic_index_in_dim(values, m, 0, keepdims=False)
    y_all = after([kept[0]], dx_sums[3])[0]
    middle_row = rows_here // 2
    y_near = [
        [across(part_of(y_all, member ^ o)[:middle_row], o) for o in range(1, members)],
        [across(part_of(y_all, member ^ o)[middle_row:], o) for o in range(1, members)],
    ]
    soon = y_near[0]
    own_upstream = lax.dynamic_index_in_dim(upstream, row, 2, keepdims=False)
    own_upstream = lax.dynamic_index_in_dim(own_upstream, member, 1, keepdims=False)
    own_upstream = own_upstream.reshape(tokens, width)
    vectors, grad_mixed, grad_residual, gaz = pl.pallas_call(
        middle_kernel,
        out_shape=[
            struct((EXTRA, width), BF16),
            struct((tokens, width), BF16),
            struct((tokens, width), F32),
            struct((rows_here, TILES, 4 * BLOCK, LANES), BF16),
        ],
        in_specs=[whole()] * 8 + [pl.BlockSpec(memory_space=pl.ANY)] * (1 + len(soon)),
        out_specs=[whole()] * 4,
        compiler_params=params(48),
        cost_estimate=took(6),
        name="middle",
    )(dx_sum, own_upstream, xg, residual, gates, gain_two, router, output_weight, keep, *soon)

    dq, dkv, weights = pl.pallas_call(
        functools.partial(attention_back_kernel, members, expert_count),
        out_shape=[
            struct((tokens, width), BF16),
            struct((members, tokens, width), BF16),
            struct((3 * width + EXTRA, width), BF16),
        ],
        in_specs=[scalars()]
        + [whole()] * (15 + rows_here)
        + [pl.BlockSpec(memory_space=pl.ANY)],
        out_specs=[whole()] * 3,
        scratch_shapes=[
            pltpu.VMEM((length, inner), F32),
            pltpu.VMEM((length, inner), F32),
            pltpu.VMEM((length, width), BF16),
        ],
        compiler_params=params(58),
        cost_estimate=took(0.1),
        name="attention_back",
    )(
        me_pair,
        qz,
        gaz,
        k_row,
        v_row,
        *probs,
        cosine,
        sine,
        mix,
        own_mix,
        att,
        grad_mixed,
        vectors,
        query_weight,
        key_weight,
        value_weight,
        gain_one,
        gain_one,
    )
    received = row_swap(after([send], gaz)[0], 1)
    kept_half = after([keep], dq)[0]
    mine = [plus(kept_half, received, i) for i in range(experts)]
    crossed = [row_swap(m, 2) for m in mine]
    dkv = [part_of(dkv, member)] + [across(part_of(dkv, member ^ o), o) for o in range(1, members)]
    grad_in = pl.pallas_call(
        functools.partial(last_kernel, members),
        out_shape=struct((tokens, width), BF16),
        in_specs=[whole()] * (7 + members) + [pl.BlockSpec(memory_space=pl.ANY)] * len(y_near[1]),
        out_specs=whole(),
        compiler_params=params(48),
        cost_estimate=took(0.1),
        name="last",
    )(dq, *dkv, query_weight, key_weight, value_weight, own_in, grad_residual, gain_one, *y_near[1])

    y_near = [jnp.concatenate(halves, axis=0) for halves in zip(*y_near)]
    y_total = add(after([part_of(y_all, member)], dq)[0], *y_near)
    y_parts = [part_of(y_total, (row - k) % rows_here) for k in range(rows_here)]
    y_sum = scatter(y_parts)
    hidden_out = (residual + y_sum.astype(F32)).astype(BF16)
    back = lambda values: lax.all_to_all(
        values.reshape(rows_here, block, width), "seq", 0, 0, tiled=True, axis_index_groups=same_member
    )
    hidden_out, grad_in = back(hidden_out), back(grad_in)
    finished = []
    for e in range(experts):
        crossed[e] = after([crossed[e]], grad_in)[0] if e == 3 else crossed[e]
        mine[e] = plus(mine[e], crossed[e])
        grad_spec = lambda a, b: pl.BlockSpec((1, a, b), lambda i, e=e: (e, 0, 0))
        half = pl.BlockSpec(halves, lambda i: (0, 0, 0))
        finished = pl.pallas_call(
            functools.partial(finish_kernel, len(finished)),
            grid=(1,),
            out_shape=[
                pltpu.HBM((experts, width, hidden), F32),
                pltpu.HBM((experts, width, hidden), F32),
                pltpu.HBM((experts, hidden, width), F32),
            ],
            in_specs=[scalars(), half, half]
            + [pl.BlockSpec(memory_space=pl.ANY)] * len(finished),
            out_specs=[grad_spec(width, hidden), grad_spec(width, hidden), grad_spec(hidden, width)],
            input_output_aliases={3 + i: i for i in range(len(finished))},
            compiler_params=params(60),
            cost_estimate=took(0.1),
            name="finish",
        )(info, mine[e], row_swap(mine[e], 1), *finished)
    shared = lax.psum(weights, ("rows", "seq"))
    step = 128
    part = lambda i: pl.BlockSpec((step, width), lambda r, i=i: (i * (width // step) + r, 0))
    rows_of = lambda w: pl.BlockSpec((step, w), lambda r: (r, 0))
    query_sum, key_sum, value_sum, output_sum, vector_sum = pl.pallas_call(
        spread_kernel,
        grid=(width // step,),
        out_shape=[
            pltpu.HBM((width, width), F32),
            pltpu.HBM((width, inner), F32),
            pltpu.HBM((width, inner), F32),
            pltpu.HBM((width, width), F32),
            struct((EXTRA, width), F32),
        ],
        in_specs=[part(0), part(1), part(2), pl.BlockSpec((EXTRA, width), lambda r: (3 * width // EXTRA, 0))]
        + [pl.BlockSpec(memory_space=pl.ANY)] * 3,
        out_specs=[
            rows_of(width),
            rows_of(inner),
            rows_of(inner),
            rows_of(width),
            pl.BlockSpec((EXTRA, width), lambda r: (0, 0)),
        ],
        compiler_params=params(24),
        cost_estimate=took(0.1),
        name="spread",
    )(*[pltpu.with_memory_space_constraint(shared, pltpu.HBM)] * 4, hidden_out, grad_in, finished[0])
    return (
        hidden_out,
        grad_in.astype(F32),
        vector_sum[expert_count + 1],
        query_sum,
        key_sum,
        value_sum,
        output_sum,
        vector_sum[expert_count],
        vector_sum[:expert_count].T,
        *finished,
    )


def solution(mesh):
    placed = (
        P("rows", "seq", None),
        P("rows", "seq"),
        P("rows", "seq"),
        P("rows", "seq", None),
        P(),
        P(),
        P(),
        P(),
        P(),
        P(),
        P(),
        P("seq", None, None),
        P("seq", None, None),
        P("seq", None, None),
        P("rows", "seq", None),
    )
    return jax.shard_map(
        local,
        mesh=mesh,
        in_specs=placed,
        out_specs=(
            P("rows", "seq", None),
            P("rows", "seq", None),
            P(),
            P(),
            P(),
            P(),
            P(),
            P(),
            P(),
            P("seq", None, None),
            P("seq", None, None),
            P("seq", None, None),
        ),
        check_vma=False,
    )
```

```python
import functools
import math

import jax
import jax.numpy as jnp
from jax import lax
from jax.experimental import pallas as pl
from jax.experimental.pallas import tpu as pltpu
from jax.sharding import PartitionSpec as P

HEADS = 16
KV_HEADS = 8
HEAD_DIM = 64
TOPK = 8
MOST = 32
BLOCK = 64
LANES = 128
TILES = KV_HEADS * HEAD_DIM // LANES
EXTRA = 128
PAIR = 2
PAD = 16

EPS = 1e-06
THETA = 10000.0
NEG = -1e30
F32 = jnp.float32
BF16 = jnp.bfloat16
EXACT = lax.Precision.HIGHEST
NN = (((1,), (0,)), ((), ()))
NT = (((1,), (1,)), ((), ()))
TN = (((0,), (0,)), ((), ()))


def mul(left, right, dims=NN, precision=None):
    return lax.dot_general(left, right, dims, precision=precision, preferred_element_type=F32)


def params(megabytes):
    return pltpu.CompilerParams(vmem_limit_bytes=megabytes << 20)


def whole():
    return pl.BlockSpec(memory_space=pltpu.VMEM)


def scalars():
    return pl.BlockSpec(memory_space=pltpu.SMEM)


def struct(shape, dtype):
    return jax.ShapeDtypeStruct(shape, dtype)


def took(microseconds):
    return pl.CostEstimate(flops=int(microseconds * 0.5e9), bytes_accessed=0, transcendentals=0)


def low_half(shape):
    return lax.broadcasted_iota(jnp.int32, shape, 1) < HEAD_DIM


def swap_halves(tile):
    lane = lax.broadcasted_iota(jnp.int32, tile.shape, 1)
    quarter = HEAD_DIM // 2
    forward = pltpu.roll(tile, LANES - quarter, 1)
    backward = pltpu.roll(tile, quarter, 1)
    return jnp.where(lane % HEAD_DIM < quarter, forward, backward)


def rotate(tile, cosine, signed_sine):
    return tile * cosine + swap_halves(tile) * signed_sine


def unrotate(tile, cosine, signed_sine):
    return tile * cosine - swap_halves(tile) * signed_sine


def spread_heads(first, second):
    low = low_half(first.shape)
    return jnp.concatenate(
        [
            jnp.where(low, first, 0.0),
            jnp.where(low, pltpu.roll(first, HEAD_DIM, 1), 0.0),
            jnp.where(low, 0.0, pltpu.roll(second, HEAD_DIM, 1)),
            jnp.where(low, 0.0, second),
        ],
        axis=0,
    )


def gather_heads(stacked):
    low = low_half((BLOCK, LANES))
    one, two, three, four = (stacked[i * BLOCK : (i + 1) * BLOCK] for i in range(4))
    first = jnp.where(low, one, pltpu.roll(two, HEAD_DIM, 1))
    second = jnp.where(low, pltpu.roll(three, HEAD_DIM, 1), four)
    return first, second


def allowed_keys(piece, members, member, pos_ref):
    keys = (piece + 1) * members * BLOCK
    start = (piece * members + member) * BLOCK
    place = start + lax.broadcasted_iota(jnp.int32, (BLOCK, keys), 0)
    key = lax.broadcasted_iota(jnp.int32, (BLOCK, keys), 1)
    opening = place - pos_ref[piece * BLOCK : (piece + 1) * BLOCK, :]
    return (key <= place) & (key >= opening)


def probabilities(stacked, key_tile, allowed):
    keys = key_tile.shape[0]
    scores = mul(stacked, key_tile, NT)
    scores = scores.reshape(4, BLOCK, keys)
    scores = jnp.where(allowed[None], scores, NEG)
    weights = jnp.exp(scores - jnp.max(scores, axis=-1, keepdims=True))
    probs = weights * (1.0 / jnp.sum(weights, axis=-1, keepdims=True))
    return probs.reshape(4 * BLOCK, keys)


def two_parts(values):
    high = values.astype(BF16).astype(F32)
    return jnp.concatenate([high, values - high], axis=0).astype(BF16)


def front_kernel(
    members,
    blocks,
    me_ref,
    *refs,
):
    front_body(members, me_ref, refs[:blocks], *refs[blocks:])


def front_body(
    members,
    me_ref,
    block_refs,
    cos_ref,
    sin_ref,
    pos_ref,
    ids_ref,
    gain_one_ref,
    wq_ref,
    wk_ref,
    wv_ref,
    wo_ref,
    gain_two_ref,
    router_ref,
    mix_ref,
    own_ref,
    qz_ref,
    k_ref,
    v_ref,
    att_ref,
    res_ref,
    xg_ref,
    gates_ref,
    input_ref,
    *rest,
):
    probs_refs, h_ref = rest[:-1], rest[-1]
    member = me_ref[0]
    length, width = h_ref.shape
    tokens = own_ref.shape[0]
    pieces = tokens // BLOCK
    step = 256
    for i, block_ref in enumerate(block_refs):
        h_ref[pl.ds(pl.multiple_of(me_ref[2 + i] * BLOCK, BLOCK), BLOCK), :] = block_ref[...]

    def keys_step(i, carry):
        rows = pl.ds(pl.multiple_of(i * step, step), step)
        x = h_ref[rows, :].astype(F32)
        scale = lax.rsqrt(jnp.mean(x * x, axis=-1, keepdims=True) + EPS)
        mix = (x * scale * gain_one_ref[...]).astype(BF16)
        mix_ref[rows, :] = mix
        v_ref[rows, :] = mul(mix, wv_ref[...]).astype(BF16)
        pre = mul(mix, wk_ref[...])
        cosine, sine = cos_ref[rows, :], sin_ref[rows, :]
        for tile in range(TILES):
            lanes = slice(tile * LANES, (tile + 1) * LANES)
            k_ref[rows, lanes] = rotate(pre[:, lanes], cosine, sine).astype(BF16)
        return carry

    lax.fori_loop(0, length // step, keys_step, 0)
    own = [pl.ds(pl.multiple_of((p * members + member) * BLOCK, BLOCK), BLOCK) for p in range(pieces)]
    for piece in range(pieces):
        rows = slice(piece * BLOCK, (piece + 1) * BLOCK)
        own_ref[rows, :] = mix_ref[own[piece], :]
        input_ref[rows, :] = h_ref[own[piece], :]

    def query_step(tile, carry):
        pre = mul(own_ref[...], wq_ref[:, pl.ds(pl.multiple_of(tile * 256, 256), 256)])
        for piece in range(pieces):
            rows = slice(piece * BLOCK, (piece + 1) * BLOCK)
            cosine, sine = cos_ref[own[piece], :], sin_ref[own[piece], :]
            first = rotate(pre[rows, :LANES], cosine, sine)
            second = rotate(pre[rows, LANES:], cosine, sine)
            qz_ref[piece, tile] = (spread_heads(first, second) * HEAD_DIM**-0.5).astype(BF16)
        return carry

    lax.fori_loop(0, TILES, query_step, 0)
    for piece in range(pieces):
        allowed = allowed_keys(piece, members, member, pos_ref)
        keys = allowed.shape[1]
        rows = slice(piece * BLOCK, (piece + 1) * BLOCK)

        def attend(tile, carry):
            lanes = pl.ds(pl.multiple_of(tile * LANES, LANES), LANES)
            probs = probabilities(qz_ref[piece, tile], k_ref[:keys, lanes], allowed)
            probs = probs.astype(BF16)
            probs_refs[piece][tile] = probs
            first, second = gather_heads(mul(probs, v_ref[:keys, lanes]))
            at = pl.multiple_of(tile * 256, 256)
            att_ref[rows, pl.ds(at, LANES)] = first.astype(BF16)
            att_ref[rows, pl.ds(at + LANES, LANES)] = second.astype(BF16)
            return carry

        lax.fori_loop(0, TILES, attend, 0)
    mixed = mul(att_ref[...], wo_ref[...])
    residual = input_ref[...].astype(F32) + mixed
    res_ref[...] = residual
    scale = lax.rsqrt(jnp.mean(residual * residual, axis=-1, keepdims=True) + EPS)
    chosen = (residual * scale * gain_two_ref[...]).astype(BF16)
    xg_ref[:tokens, :] = chosen
    logits = mul(router_ref[...], chosen, NT)
    expert = lax.broadcasted_iota(jnp.int32, logits.shape, 0)
    named = expert == ids_ref[0:1, :]
    for k in range(1, TOPK):
        named = named | (expert == ids_ref[k : k + 1, :])
    logits = jnp.where(named, logits, NEG)
    weights = jnp.where(named, jnp.exp(logits - jnp.max(logits, axis=0, keepdims=True)), 0.0)
    gates = weights / jnp.sum(weights, axis=0, keepdims=True)
    gates_ref[...] = gates
    for part in range(logits.shape[0] // 8):
        lanes = slice(part * tokens, (part + 1) * tokens)
        xg_ref[tokens:, lanes] = two_parts(gates[part * 8 : (part + 1) * 8])


def one_hot(slot_row, rows):
    slot = lax.broadcasted_iota(jnp.int32, (rows, slot_row.shape[1]), 0).astype(F32)
    return slot == slot_row


def expert_kernel(
    kept,
    info_ref,
    xa_ref,
    xb_ref,
    named_ref,
    u_ref,
    wg_ref,
    wu_ref,
    wd_ref,
    *rest,
):
    (dxa_ref, dxb_ref) = rest[kept : kept + 2]
    (y_ref, xs_ref, us_ref, hs_ref, dg_ref, du_ref) = rest[kept + 2 : kept + 8]
    (dxs_ref, ys_ref, pick_ref, slot_ref, gates_ref, back_ref) = rest[kept + 8 :]
    e = pl.program_id(0)
    experts = pl.num_programs(0)
    tokens = named_ref.shape[2]
    width = xa_ref.shape[1]
    rows = tokens * MOST // BLOCK
    places = [(info_ref[0] + c) % PAIR for c in range(PAIR)]
    sources = (xa_ref, xb_ref)

    @pl.when(e == 0)
    def _():
        back_ref[...] = jnp.zeros_like(back_ref)
        earlier = lax.broadcasted_iota(jnp.int32, (tokens, tokens), 0)
        later = lax.broadcasted_iota(jnp.int32, (tokens, tokens), 1)
        before = (earlier < later).astype(F32).astype(BF16)
        for c in range(PAIR):
            named = named_ref[places[c]]
            slot_ref[c] = jnp.where(named > 0, mul(named.astype(BF16), before), -1.0)

    at = pl.ds(pl.multiple_of(e * rows, rows), rows)
    number = info_ref[1] * experts + e
    row = lax.rem(number, 8)
    lanes = pl.ds(pl.multiple_of(lax.div(number, 8) * tokens, tokens), tokens)
    entering, leaving, gate = [], [], []
    for c in range(PAIR):
        hot = one_hot(slot_ref[c, pl.ds(e, 1), :], rows)
        pick = hot.astype(F32).astype(BF16)
        pick_ref[c, at, :] = pick
        picked = mul(pick, sources[c][:tokens, :]).astype(BF16)
        xs_ref[places[c]] = picked
        entering.append(picked)
        picked = mul(pick, u_ref[:, places[c], 0].reshape(tokens, width)).astype(BF16)
        us_ref[places[c]] = picked
        leaving.append(picked)
        sent = sources[c][tokens:, lanes].astype(F32)
        gates_ref[...] = sent[:8] + sent[8:]
        gate.append(jnp.sum(jnp.where(hot, gates_ref[pl.ds(row, 1), :], 0.0), axis=1, keepdims=True))
    entering = jnp.concatenate(entering, axis=0)
    gate = jnp.concatenate(gate, axis=0)
    gate_pre = mul(entering, wg_ref[0])
    up_pre = mul(entering, wu_ref[0])
    product = mul(jnp.concatenate(leaving, axis=0), wd_ref[0], NT)
    share = 0.5 * jnp.tanh(0.5 * gate_pre) + 0.5
    silu = gate_pre * share
    hidden = silu * up_pre
    grad_gate = jnp.sum(hidden * product, axis=1, keepdims=True)
    grad_act = gate * product
    grad_gate_pre = (grad_act * up_pre * share * (1.0 + gate_pre * (1.0 - share))).astype(BF16)
    grad_up_pre = (grad_act * silu).astype(BF16)
    gated = (gate * hidden).astype(BF16)
    grad_rows = (mul(grad_gate_pre, wg_ref[0], NT) + mul(grad_up_pre, wu_ref[0], NT)).astype(BF16)
    out_rows = mul(gated, wd_ref[0]).astype(BF16)
    for c in range(PAIR):
        part = slice(c * rows, (c + 1) * rows)
        hs_ref[places[c]] = gated[part]
        dg_ref[places[c]] = grad_gate_pre[part]
        du_ref[places[c]] = grad_up_pre[part]
        dxs_ref[c, at, :] = grad_rows[part]
        ys_ref[c, at, :] = out_rows[part]
        hot = one_hot(slot_ref[c, pl.ds(e, 1), :], rows)
        returned = jnp.sum(jnp.where(hot, grad_gate[part], 0.0), axis=0, keepdims=True)
        high = returned.astype(BF16).astype(F32)
        back_ref[c, pl.ds(row, 1), lanes] = high
        back_ref[c, pl.ds(row + 8, 1), lanes] = returned - high

    @pl.when(e == experts - 1)
    def _():
        for c, dx_ref in enumerate((dxa_ref, dxb_ref)):
            dx_ref[:tokens, :] = mul(pick_ref[c], dxs_ref[c], TN).astype(BF16)
            dx_ref[tokens:, :] = back_ref[c].astype(BF16)
            y_ref[places[c], 0] = mul(pick_ref[c], ys_ref[c], TN).astype(BF16)


def expert_grads_kernel(info_ref, xs_ref, us_ref, hs_ref, dg_ref, du_ref, *rest):
    keep_ref, send_ref = rest[-2:]
    core = info_ref[3]
    group, rows, width = xs_ref.shape
    inner = hs_ref.shape[2]
    flat = lambda ref: ref[...].reshape(group * rows, ref.shape[2])

    for half, out_ref in ((core, keep_ref), (1 - core, send_ref)):
        step = min(256, width // 2)
        for at in range(0, width // 2, step):
            lanes = pl.ds(pl.multiple_of(half * (width // 2) + at, LANES), step)
            entering = xs_ref[:, :, lanes].reshape(group * rows, step)
            out_ref[0, 0, at : at + step, :] = mul(entering, flat(dg_ref), TN).astype(BF16)
            out_ref[0, 1, at : at + step, :] = mul(entering, flat(du_ref), TN).astype(BF16)
        step = inner // 2
        lanes = pl.ds(pl.multiple_of(half * step, LANES), step)
        gated = hs_ref[:, :, lanes].reshape(group * rows, step)
        product = mul(gated, flat(us_ref), TN).astype(BF16)
        out_ref[0, 2, :step, :] = product[:, :inner]
        out_ref[0, 2, step:, :] = product[:, inner:]


def finish_kernel(kept, info_ref, mine_ref, other_ref, *rest):
    gate_ref, up_ref, down_ref = rest[kept:]
    core = info_ref[3]
    half = mine_ref.shape[1]
    inner = mine_ref.shape[2]
    for source, place in ((mine_ref, core), (other_ref, 1 - core)):
        rows = pl.ds(pl.multiple_of(place * half, half), half)
        gate_ref[0, rows, :] = source[0].astype(F32)
        up_ref[0, rows, :] = source[1].astype(F32)
        rows = pl.ds(pl.multiple_of(place * (half // 2), half // 2), half // 2)
        down_ref[0, rows, :inner] = source[2, : half // 2].astype(F32)
        down_ref[0, rows, inner:] = source[2, half // 2 :].astype(F32)


def spread_kernel(query_ref, keyval_ref, output_ref, vectors_ref, *rest):
    sums = rest[-5:]
    inner = sums[1].shape[1]
    sums[0][...] = query_ref[...].astype(F32)
    sums[1][...] = keyval_ref[:, :inner].astype(F32)
    sums[2][...] = keyval_ref[:, inner:].astype(F32)
    sums[3][...] = output_ref[...].astype(F32)

    @pl.when(pl.program_id(0) == 0)
    def _():
        sums[4][...] = vectors_ref[...].astype(F32)


def add(*terms):
    return sum(term.astype(F32) for term in terms).astype(terms[0].dtype)


def plus_kernel(left_ref, right_ref, out_ref):
    total = left_ref[...].astype(F32) + right_ref[...].astype(F32)
    out_ref[...] = total.reshape(out_ref.shape).astype(out_ref.dtype)


def plus(left, right, at=None):
    parts, rows, columns = left.shape[-3:]
    entry = pl.BlockSpec((1, rows, columns), lambda i: (i, 0, 0))
    source = entry if at is None else pl.BlockSpec((1, 1, rows, columns), lambda i: (at, i, 0, 0))
    return pl.pallas_call(
        plus_kernel,
        grid=(parts,),
        out_shape=struct((parts, rows, columns), left.dtype),
        in_specs=[source, source],
        out_specs=entry,
        compiler_params=params(56),
        cost_estimate=took(0.1),
        name="plus",
    )(left, right)


def after(values, *others):
    anywhere = pl.BlockSpec(memory_space=pl.ANY)
    return pl.pallas_call(
        lambda *refs: None,
        out_shape=[struct(v.shape, v.dtype) for v in values],
        in_specs=[anywhere] * (len(values) + len(others)),
        out_specs=[anywhere] * len(values),
        input_output_aliases={i: i for i in range(len(values))},
        name="after",
    )(*values, *others)


def put_block(whole_array, block, *at):
    for _ in range(whole_array.ndim - block.ndim):
        block = block[None]
    return lax.dynamic_update_slice(
        whole_array, block, tuple(at) + (0,) * (whole_array.ndim - len(at))
    )


def middle_kernel(
    dx_ref,
    u_ref,
    xg_ref,
    res_ref,
    gates_ref,
    gain_two_ref,
    router_ref,
    wo_ref,
    *rest,
):
    vectors_ref, mixed_ref, gres_ref, gaz_ref = rest[-4:]
    tokens, width = u_ref.shape
    experts = gates_ref.shape[0]
    pieces = tokens // BLOCK
    parts = []
    for part in range(experts // 8):
        sent = dx_ref[tokens:, part * tokens : (part + 1) * tokens].astype(F32)
        parts.append(sent[:8] + sent[8:])
    grad_gates = jnp.concatenate(parts, axis=0)
    gates = gates_ref[...]
    grad_logits = gates * (grad_gates - jnp.sum(gates * grad_gates, axis=0, keepdims=True))
    grad_normed = dx_ref[:tokens, :].astype(F32) + mul(
        grad_logits, router_ref[...].astype(F32), TN, EXACT
    )
    router = mul(grad_logits, xg_ref[:tokens, :].astype(F32), NN, EXACT)
    residual = res_ref[...]
    scale = lax.rsqrt(jnp.mean(residual * residual, axis=-1, keepdims=True) + EPS)
    normed = residual * scale
    second = jnp.sum(grad_normed * normed, axis=0, keepdims=True)
    spare = jnp.zeros((vectors_ref.shape[0] - experts - 1, width), F32)
    vectors_ref[...] = jnp.concatenate([router, second, spare], axis=0).astype(BF16)
    scaled = grad_normed * gain_two_ref[...]
    grad_residual = u_ref[...].astype(F32) + scale * (
        scaled - normed * jnp.mean(scaled * normed, axis=-1, keepdims=True)
    )
    gres_ref[...] = grad_residual
    grad_mixed = grad_residual.astype(BF16)
    mixed_ref[...] = grad_mixed
    for tile in range(TILES):
        grad_att = mul(grad_mixed, wo_ref[tile * 256 : (tile + 1) * 256, :], NT)
        for piece in range(pieces):
            rows = slice(piece * BLOCK, (piece + 1) * BLOCK)
            gaz_ref[piece, tile] = spread_heads(
                grad_att[rows, :LANES], grad_att[rows, LANES:]
            ).astype(BF16)


def attention_back_kernel(
    members,
    experts,
    me_ref,
    qz_ref,
    gaz_ref,
    k_ref,
    v_ref,
    *refs,
):
    pieces = gaz_ref.shape[0]
    attention_back_body(
        members, experts, me_ref, qz_ref, gaz_ref, k_ref, v_ref, refs[:pieces], *refs[pieces:]
    )


def attention_back_body(
    members,
    experts,
    me_ref,
    qz_ref,
    gaz_ref,
    k_ref,
    v_ref,
    probs_refs,
    cos_ref,
    sin_ref,
    mix_ref,
    own_ref,
    att_ref,
    mixed_ref,
    vectors_ref,
    wq_ref,
    wk_ref,
    wv_ref,
    gain_one_ref,
    *rest,
):
    dq_ref, dkv_ref, weights_ref, dk_acc, dv_acc, row_ref = rest[-6:]
    member = me_ref[0]
    tokens = own_ref.shape[0]
    pieces = tokens // BLOCK
    length = k_ref.shape[0]
    inner = k_ref.shape[1]
    dk_acc[...] = jnp.zeros_like(dk_acc)
    dv_acc[...] = jnp.zeros_like(dv_acc)
    for piece in range(pieces):
        keys = (piece + 1) * members * BLOCK
        rows = slice(piece * BLOCK, (piece + 1) * BLOCK)
        at = pl.ds(pl.multiple_of((piece * members + member) * BLOCK, BLOCK), BLOCK)

        def step(tile, carry):
            lanes = pl.ds(pl.multiple_of(tile * LANES, LANES), LANES)
            stacked, grads = qz_ref[piece, tile], gaz_ref[piece, tile]
            key_tile = k_ref[:keys, lanes]
            low_probs = probs_refs[piece][tile]
            probs = low_probs.astype(F32)
            weighted = probs * mul(grads, v_ref[:keys, lanes], NT)
            delta = jnp.sum(weighted, axis=-1, keepdims=True)
            grad_scores = (weighted - probs * delta).astype(BF16)
            dk_acc[:keys, lanes] += mul(grad_scores, stacked, TN)
            dv_acc[:keys, lanes] += mul(low_probs, grads, TN)
            first, second = gather_heads(mul(grad_scores, key_tile) * HEAD_DIM**-0.5)
            cosine, sine = cos_ref[at, :], sin_ref[at, :]
            out = pl.multiple_of(tile * 256, 256)
            dq_ref[rows, pl.ds(out, LANES)] = unrotate(first, cosine, sine).astype(BF16)
            dq_ref[rows, pl.ds(out + LANES, LANES)] = unrotate(second, cosine, sine).astype(BF16)
            return carry

        lax.fori_loop(0, TILES, step, 0)
    for block in range(length // BLOCK):
        rows = slice(block * BLOCK, (block + 1) * BLOCK)
        cosine, sine = cos_ref[rows, :], sin_ref[rows, :]
        for tile in range(TILES):
            lanes = slice(tile * LANES, (tile + 1) * LANES)
            row_ref[rows, lanes] = unrotate(dk_acc[rows, lanes], cosine, sine).astype(BF16)
        row_ref[rows, inner:] = dv_acc[rows, :].astype(BF16)
        piece, owner = block // members, block % members
        dkv_ref[owner, piece * BLOCK : (piece + 1) * BLOCK, :] = row_ref[rows, :]
    width = dq_ref.shape[1]
    for i, (left_ref, right_ref) in enumerate(
        ((own_ref, dq_ref), (mix_ref, row_ref), (att_ref, mixed_ref))
    ):
        product = mul(left_ref[...], right_ref[...], TN)
        weights_ref[i * width : (i + 1) * width, :] = product.astype(BF16)
    first = jnp.sum(mul(dq_ref[...], wq_ref[...], NT) * own_ref[...].astype(F32), axis=0, keepdims=True)
    for at in range(0, length, tokens):
        rows = slice(at, at + tokens)
        grad_mixer = mul(row_ref[rows, :inner], wk_ref[...], NT)
        grad_mixer += mul(row_ref[rows, inner:], wv_ref[...], NT)
        first += jnp.sum(grad_mixer * mix_ref[rows, :].astype(F32), axis=0, keepdims=True)
    first = first / gain_one_ref[...]
    vectors = vectors_ref[...].astype(F32)
    place = lax.broadcasted_iota(jnp.int32, vectors.shape, 0)
    weights_ref[3 * width :, :] = jnp.where(place == experts + 1, first, vectors).astype(BF16)


def last_kernel(
    members,
    dq_ref,
    *refs,
):
    last_body(dq_ref, refs[:members], *refs[members:])


def last_body(
    dq_ref,
    dkv_refs,
    wq_ref,
    wk_ref,
    wv_ref,
    input_ref,
    gres_ref,
    gain_one_ref,
    *rest,
):
    gh_ref = rest[-1]
    inner = wk_ref.shape[1]
    grad_kv = sum(dkv_ref[...].astype(F32) for dkv_ref in dkv_refs).astype(BF16)
    grad_mixer = (
        mul(dq_ref[...], wq_ref[...], NT)
        + mul(grad_kv[:, :inner], wk_ref[...], NT)
        + mul(grad_kv[:, inner:], wv_ref[...], NT)
    )
    x = input_ref[...].astype(F32)
    scale = lax.rsqrt(jnp.mean(x * x, axis=-1, keepdims=True) + EPS)
    normed = x * scale
    scaled = grad_mixer * gain_one_ref[...]
    gh_ref[...] = (
        gres_ref[...]
        + scale * (scaled - normed * jnp.mean(scaled * normed, axis=-1, keepdims=True))
    ).astype(gh_ref.dtype)


def rope_tables(places):
    middle = HEAD_DIM // 2
    frequency = jnp.exp(jnp.arange(middle, dtype=F32) * (-2.0 * math.log(THETA) / HEAD_DIM))
    angles = places.astype(F32)[:, None] * frequency
    cosine, sine = jnp.cos(angles), jnp.sin(angles)
    return (
        jnp.concatenate([cosine] * 4, axis=1),
        jnp.concatenate([-sine, sine, -sine, sine], axis=1),
    )


def local(
    hidden_in,
    segment_ids,
    positions,
    expert_ids,
    first_gain,
    query_weight,
    key_weight,
    value_weight,
    output_weight,
    second_gain,
    router_weight,
    gate_weight,
    up_weight,
    down_weight,
    out_grad,
):
    rows_here, block, width = hidden_in.shape
    tokens = rows_here * block
    shards = lax.axis_size("seq")
    members = shards // rows_here
    length = shards * block
    inner = key_weight.shape[1]
    expert_count = router_weight.shape[1]
    experts, _, hidden = gate_weight.shape
    me = lax.axis_index("seq")
    row, member = me // members, me % members
    me_pair = jnp.stack([member, me]).astype(jnp.int32)
    same_member = [[r * members + m for r in range(rows_here)] for m in range(members)]
    same_row = [[r * members + m for m in range(members)] for r in range(rows_here)]
    slots = tokens * MOST // BLOCK

    meta = jnp.concatenate(
        [positions.reshape(1, tokens), expert_ids.reshape(tokens, TOPK).T], axis=0
    )
    row_in = lax.all_to_all(jnp.repeat(hidden_in, members, axis=0), "seq", 0, 0, tiled=True)
    row_in = row_in.reshape(length, width)
    def onward(values, count):
        to = lambda j: (j // members + count) % rows_here * members + j % members
        return lax.ppermute(values, "seq", [(j, to(j)) for j in range(shards)])

    def across(values, other):
        return lax.ppermute(values, "seq", [(j, j ^ other) for j in range(shards)])

    def row_swap(values, other):
        count = lax.axis_size("rows")
        return lax.ppermute(values, "rows", [(j, j ^ other) for j in range(count)])

    def gather(values):
        found = []
        for k in range(rows_here):
            values = onward(values, 1) if k else values
            found.append([values] + [across(values, other) for other in range(1, members)])
        return found

    def joined(part):
        return add(part[0], *(across(part[o], o) for o in range(1, members)))

    def scatter(sums):
        return add(*(onward(total, rows_here - k) if k else total for k, total in enumerate(sums)))

    core = lax.axis_index("rows") % 2

    of_row = lambda k: lax.dynamic_index_in_dim(hidden_in, (row + k) % rows_here, 0, keepdims=False)
    row_in = [of_row(k) for k in range(rows_here)]
    meta = after([jnp.broadcast_to(meta[None], (shards,) + meta.shape)], *row_in)[0]
    meta = lax.all_to_all(meta, "seq", 0, 0, tiled=True)
    row_in = row_in[:1] + [onward(row_in[k], k) for k in range(1, rows_here)]
    row_in = [[v] + [across(v, other) for other in range(1, members)] for v in row_in]
    row_in = [v for blocks in row_in for v in blocks]
    places = [
        (row - k) % rows_here * members + (member ^ other)
        for k in range(rows_here)
        for other in range(members)
    ]
    me_row = jnp.stack([member, me] + places).astype(jnp.int32)
    upstream = lax.all_gather(out_grad, "seq", axis=0, tiled=False)
    upstream = upstream.reshape(rows_here, members, rows_here, block, width)
    stored = [
        pltpu.with_memory_space_constraint(v, pltpu.HBM)
        for v in (upstream, gate_weight, up_weight, down_weight)
    ]

    meta = meta.reshape(rows_here, members, TOPK + 1, rows_here, block)
    row_meta = lax.dynamic_index_in_dim(meta, row, 3, keepdims=False)
    own_meta = lax.dynamic_index_in_dim(row_meta, member, 1, keepdims=False)
    cosine, sine = rope_tables(row_meta[:, :, 0].reshape(length))
    own_pos = own_meta[:, 0].reshape(tokens, 1)
    own_ids = own_meta[:, 1:].transpose(1, 0, 2).reshape(TOPK, tokens)
    lane = jnp.arange(8, dtype=jnp.int32)
    wanted = jnp.where(lane < experts, me * experts + lane, -1)
    named = jnp.any(
        meta[:, :, 1:, None] == wanted[None, None, None, :, None, None], axis=2
    )
    named = named.transpose(3, 1, 2, 0, 4).reshape(shards, 8, tokens).astype(F32)

    gain_one, gain_two = first_gain.reshape(1, width), second_gain.reshape(1, width)
    router = router_weight.T
    mix, own_mix, qz, k_row, v_row, att, residual, xg, gates, own_in, *probs = pl.pallas_call(
        functools.partial(front_kernel, members, shards),
        out_shape=[
            struct((length, width), BF16),
            struct((tokens, width), BF16),
            struct((rows_here, TILES, 4 * BLOCK, LANES), BF16),
            struct((length, inner), BF16),
            struct((length, inner), BF16),
            struct((tokens, width), BF16),
            struct((tokens, width), F32),
            struct((tokens + PAD, width), BF16),
            struct((expert_count, tokens), F32),
            struct((tokens, width), BF16),
        ]
        + [
            struct((TILES, 4 * BLOCK, (piece + 1) * members * BLOCK), BF16)
            for piece in range(rows_here)
        ],
        in_specs=[scalars()] + [whole()] * (shards + 11),
        out_specs=[whole()] * (10 + rows_here),
        scratch_shapes=[pltpu.VMEM((length, width), BF16)],
        compiler_params=params(56),
        cost_estimate=took(19.5),
        name="front",
    )(
        me_row,
        *row_in,
        cosine,
        sine,
        own_pos,
        own_ids,
        gain_one,
        query_weight,
        key_weight,
        value_weight,
        output_weight,
        gain_two,
        router,
    )

    per_row = members // PAIR
    one_on = onward(xg, 1)
    beside = [across(xg, other) for other in range(1, members)]
    one_on = after([one_on], *beside)[0]
    sets = [[xg] + beside, [one_on] + [across(one_on, other) for other in range(1, members)]]
    two_on = onward(one_on, 1)
    wide, narrow = experts * slots, hidden
    kept = []
    order = list(range(rows_here))
    dx_parts, dx_sums = [[] for _ in order], []
    for k in order:
        group = sets[k]
        tied = []
        for q in range(members // PAIR):
            pair = (row - k) % rows_here * per_row + ((member // PAIR) ^ q)
            info = [member % PAIR, me, pair, (row - k) % rows_here, (member // PAIR) ^ q]
            info = jnp.stack(info).astype(jnp.int32)
            flat = lambda *shape: pl.BlockSpec(shape, lambda e, info: (0,) * len(shape))
            of_pair = lambda w: pl.BlockSpec((PAIR, slots, w), lambda e, info: (info[2], e, 0))
            of_expert = lambda a, b: pl.BlockSpec((1, a, b), lambda e, info: (e, 0, 0))
            outcome = pl.pallas_call(
                functools.partial(expert_kernel, len(kept) + len(tied)),
                grid_spec=pltpu.PrefetchScalarGridSpec(
                    num_scalar_prefetch=1,
                    grid=(experts,),
                    in_specs=[
                        flat(tokens + PAD, width),
                        flat(tokens + PAD, width),
                        pl.BlockSpec((PAIR, 8, tokens), lambda e, info: (info[2], 0, 0)),
                        pl.BlockSpec(
                            (rows_here, PAIR, 1, block, width),
                            lambda e, info: (0, info[4], info[3], 0, 0),
                        ),
                        of_expert(width, hidden),
                        of_expert(width, hidden),
                        of_expert(hidden, width),
                    ]
                    + [pl.BlockSpec(memory_space=pl.ANY)] * (len(kept) + len(tied)),
                    out_specs=[
                        flat(tokens + PAD, width),
                        flat(tokens + PAD, width),
                        pl.BlockSpec(
                            (PAIR, 1, tokens, width), lambda e, info: (info[4], info[3], 0, 0)
                        ),
                        of_pair(width),
                        of_pair(width),
                        of_pair(hidden),
                        of_pair(hidden),
                        of_pair(hidden),
                    ],
                    scratch_shapes=[
                        pltpu.VMEM((PAIR, wide, width), BF16),
                        pltpu.VMEM((PAIR, wide, width), BF16),
                        pltpu.VMEM((PAIR, wide, tokens), BF16),
                        pltpu.VMEM((PAIR, 8, tokens), F32),
                        pltpu.VMEM((8, tokens), F32),
                        pltpu.VMEM((PAIR, PAD, width), F32),
                    ],
                ),
                out_shape=[
                    struct((tokens + PAD, width), BF16),
                    struct((tokens + PAD, width), BF16),
                    pltpu.HBM((members, rows_here, tokens, width), BF16),
                    pltpu.HBM((shards, wide, width), BF16),
                    pltpu.HBM((shards, wide, width), BF16),
                    pltpu.HBM((shards, wide, hidden), BF16),
                    pltpu.HBM((shards, wide, hidden), BF16),
                    pltpu.HBM((shards, wide, hidden), BF16),
                ],
                input_output_aliases={8 + i: 2 + i for i in range(len(kept))},
                compiler_params=params(40),
                cost_estimate=took(16),
                name="experts",
            )(
                info,
                group[2 * q],
                group[2 * q + 1],
                named,
                *stored,
                *kept,
                *tied,
            )
            dx_parts[k] += outcome[:2]
            kept = outcome[2:]
        part = dx_parts[k]
        if k == 0:
            values = after([two_on], part[0])[0]
            for i in range(2, rows_here):
                values = onward(values, 1) if i > 2 else values
                sets.append([values] + [across(values, other) for other in range(1, members)])
        if k < 2:
            part = part[:1] + list(after(part[1:], *sets[rows_here - 1][1:]))
        dx_sums.append(joined(part))
    sent = [dx_sums[0]] + [onward(dx_sums[k], rows_here - k) for k in range(1, rows_here)]
    dx_sum = add(*sent)

    info = jnp.stack([member % PAIR, me, me, core]).astype(jnp.int32)
    halves = (3, width // 2, hidden)
    one_expert = lambda w: pl.BlockSpec((shards, slots, w), lambda i: (0, i, 0))
    half = pl.BlockSpec((1,) + halves, lambda i: (i, 0, 0, 0))
    keep, send = pl.pallas_call(
        expert_grads_kernel,
        grid=(experts,),
        out_shape=[struct((experts,) + halves, BF16)] * 2,
        in_specs=[scalars(), one_expert(width), one_expert(width)]
        + [one_expert(hidden)] * 3
        + [pl.BlockSpec(memory_space=pl.ANY)] * 2,
        out_specs=[half] * 2,
        compiler_params=params(60),
        cost_estimate=took(60),
        name="expert_grads",
    )(info, *kept[1:], dx_sums[2], dx_sums[3])
    part_of = lambda values, m: lax.dynamic_index_in_dim(values, m, 0, keepdims=False)
    y_all = after([kept[0]], dx_sums[3])[0]
    middle_row = rows_here // 2
    y_near = [
        [across(part_of(y_all, member ^ o)[:middle_row], o) for o in range(1, members)],
        [across(part_of(y_all, member ^ o)[middle_row:], o) for o in range(1, members)],
    ]
    soon = y_near[0]
    own_upstream = lax.dynamic_index_in_dim(upstream, row, 2, keepdims=False)
    own_upstream = lax.dynamic_index_in_dim(own_upstream, member, 1, keepdims=False)
    own_upstream = own_upstream.reshape(tokens, width)
    vectors, grad_mixed, grad_residual, gaz = pl.pallas_call(
        middle_kernel,
        out_shape=[
            struct((EXTRA, width), BF16),
            struct((tokens, width), BF16),
            struct((tokens, width), F32),
            struct((rows_here, TILES, 4 * BLOCK, LANES), BF16),
        ],
        in_specs=[whole()] * 8 + [pl.BlockSpec(memory_space=pl.ANY)] * (1 + len(soon)),
        out_specs=[whole()] * 4,
        compiler_params=params(48),
        cost_estimate=took(6),
        name="middle",
    )(dx_sum, own_upstream, xg, residual, gates, gain_two, router, output_weight, keep, *soon)

    dq, dkv, weights = pl.pallas_call(
        functools.partial(attention_back_kernel, members, expert_count),
        out_shape=[
            struct((tokens, width), BF16),
            struct((members, tokens, width), BF16),
            struct((3 * width + EXTRA, width), BF16),
        ],
        in_specs=[scalars()]
        + [whole()] * (15 + rows_here)
        + [pl.BlockSpec(memory_space=pl.ANY)],
        out_specs=[whole()] * 3,
        scratch_shapes=[
            pltpu.VMEM((length, inner), F32),
            pltpu.VMEM((length, inner), F32),
            pltpu.VMEM((length, width), BF16),
        ],
        compiler_params=params(58),
        cost_estimate=took(0.1),
        name="attention_back",
    )(
        me_pair,
        qz,
        gaz,
        k_row,
        v_row,
        *probs,
        cosine,
        sine,
        mix,
        own_mix,
        att,
        grad_mixed,
        vectors,
        query_weight,
        key_weight,
        value_weight,
        gain_one,
        gain_one,
    )
    received = row_swap(after([send], gaz)[0], 1)
    kept_half = after([keep], dq)[0]
    mine = [plus(kept_half, received, i) for i in range(experts)]
    crossed = [row_swap(m, 2) for m in mine]
    dkv = [part_of(dkv, member)] + [across(part_of(dkv, member ^ o), o) for o in range(1, members)]
    grad_in = pl.pallas_call(
        functools.partial(last_kernel, members),
        out_shape=struct((tokens, width), BF16),
        in_specs=[whole()] * (7 + members) + [pl.BlockSpec(memory_space=pl.ANY)] * len(y_near[1]),
        out_specs=whole(),
        compiler_params=params(48),
        cost_estimate=took(0.1),
        name="last",
    )(dq, *dkv, query_weight, key_weight, value_weight, own_in, grad_residual, gain_one, *y_near[1])

    y_near = [jnp.concatenate(halves, axis=0) for halves in zip(*y_near)]
    y_total = add(after([part_of(y_all, member)], dq)[0], *y_near)
    y_parts = [part_of(y_total, (row - k) % rows_here) for k in range(rows_here)]
    y_sum = scatter(y_parts)
    hidden_out = (residual + y_sum.astype(F32)).astype(BF16)
    back = lambda values: lax.all_to_all(
        values.reshape(rows_here, block, width), "seq", 0, 0, tiled=True, axis_index_groups=same_member
    )
    hidden_out, grad_in = back(hidden_out), back(grad_in)
    finished = []
    for e in range(experts):
        crossed[e] = after([crossed[e]], grad_in, y_sum)[0] if e == 3 else crossed[e]
        mine[e] = plus(mine[e], crossed[e])
        grad_spec = lambda a, b: pl.BlockSpec((1, a, b), lambda i, e=e: (e, 0, 0))
        half = pl.BlockSpec(halves, lambda i: (0, 0, 0))
        finished = pl.pallas_call(
            functools.partial(finish_kernel, len(finished)),
            grid=(1,),
            out_shape=[
                pltpu.HBM((experts, width, hidden), F32),
                pltpu.HBM((experts, width, hidden), F32),
                pltpu.HBM((experts, hidden, width), F32),
            ],
            in_specs=[scalars(), half, half]
            + [pl.BlockSpec(memory_space=pl.ANY)] * len(finished),
            out_specs=[grad_spec(width, hidden), grad_spec(width, hidden), grad_spec(hidden, width)],
            input_output_aliases={3 + i: i for i in range(len(finished))},
            compiler_params=params(60),
            cost_estimate=took(0.1),
            name="finish",
        )(info, mine[e], row_swap(mine[e], 1), *finished)
    shared = lax.psum(weights, ("rows", "seq"))
    step = 128
    part = lambda i: pl.BlockSpec((step, width), lambda r, i=i: (i * (width // step) + r, 0))
    rows_of = lambda w: pl.BlockSpec((step, w), lambda r: (r, 0))
    query_sum, key_sum, value_sum, output_sum, vector_sum = pl.pallas_call(
        spread_kernel,
        grid=(width // step,),
        out_shape=[
            pltpu.HBM((width, width), F32),
            pltpu.HBM((width, inner), F32),
            pltpu.HBM((width, inner), F32),
            pltpu.HBM((width, width), F32),
            struct((EXTRA, width), F32),
        ],
        in_specs=[part(0), part(1), part(2), pl.BlockSpec((EXTRA, width), lambda r: (3 * width // EXTRA, 0))]
        + [pl.BlockSpec(memory_space=pl.ANY)] * 2,
        out_specs=[
            rows_of(width),
            rows_of(inner),
            rows_of(inner),
            rows_of(width),
            pl.BlockSpec((EXTRA, width), lambda r: (0, 0)),
        ],
        compiler_params=params(24),
        cost_estimate=took(0.1),
        name="spread",
    )(*[pltpu.with_memory_space_constraint(shared, pltpu.HBM)] * 4, grad_in, finished[0])
    hidden_out = after([hidden_out], finished[0])[0]
    return (
        hidden_out,
        grad_in.astype(F32),
        vector_sum[expert_count + 1],
        query_sum,
        key_sum,
        value_sum,
        output_sum,
        vector_sum[expert_count],
        vector_sum[:expert_count].T,
        *finished,
    )


def solution(mesh):
    placed = (
        P("rows", "seq", None),
        P("rows", "seq"),
        P("rows", "seq"),
        P("rows", "seq", None),
        P(),
        P(),
        P(),
        P(),
        P(),
        P(),
        P(),
        P("seq", None, None),
        P("seq", None, None),
        P("seq", None, None),
        P("rows", "seq", None),
    )
    return jax.shard_map(
        local,
        mesh=mesh,
        in_specs=placed,
        out_specs=(
            P("rows", "seq", None),
            P("rows", "seq", None),
            P(),
            P(),
            P(),
            P(),
            P(),
            P(),
            P(),
            P("seq", None, None),
            P("seq", None, None),
            P("seq", None, None),
        ),
        check_vma=False,
    )
```
